32 devices in a mesh: section: 2 (over core), dp: 16 (over z, y, x).
Axes of the slice: x: 2, y: 2, z: 4, core: 2. Of those that a mesh axis runs over, the one named last changes fastest.
Arguments:
- boundary: bfloat16 [2, 2, 16, 128, 1024], P('section', None, 'dp'), may hold values from -8 to 8
- segments: int32 [2, 16, 128], P(None, 'dp'), may hold values from 0 to 3, never falling along the last dimension, each value on 1 to 64 neighbouring positions
- ln_gain: float32 [2, 1024], P('section', 'dp'), may hold values from 0.5 to 1.5
- ln_bias: float32 [2, 1024], P('section', 'dp'), may hold values from -1.75 to 1.75
- w_qkv: float32 [2, 1024, 3072], P('section', 'dp'), may hold values from -0.1875 to 0.1875
- w_out: float32 [2, 1024, 1024], P('section', 'dp'), may hold values from -0.75 to 0.75
- w_in: float32 [2, 1024, 4096], P('section', 'dp'), may hold values from -0.1875 to 0.1875
- b_in: float32 [2, 4096], P('section', 'dp'), may hold values from -3 to 3
- w_fc: float32 [2, 4096, 1024], P('section', 'dp'), may hold values from -0.09375 to 0.09375
- b_fc: float32 [2, 1024], P('section', 'dp'), may hold values from -1.75 to 1.75
Outputs:
- boundary_out: float32 [2, 2, 16, 128, 1024], P('section', None, 'dp')
- g_ln_gain: float32 [2, 1024], P('section', 'dp')
- g_ln_bias: float32 [2, 1024], P('section', 'dp')
- g_w_qkv: float32 [2, 1024, 3072], P('section', 'dp')
- g_w_out: float32 [2, 1024, 1024], P('section', 'dp')
- g_w_in: float32 [2, 1024, 4096], P('section', 'dp')
- g_b_in: float32 [2, 4096], P('section', 'dp')
- g_w_fc: float32 [2, 4096, 1024], P('section', 'dp')
- g_b_fc: float32 [2, 1024], P('section', 'dp')
The draws below stay inside these ranges and needn't reach their ends.
Inputs may be any that keep to these rules, and one draw needn't show every extreme that they name: `segments`: in each row the ids never fall; each protein spans 1 to 64 tokens of its row.
All inputs are finite; a program needn't handle non-finite values.
Results may differ from the reference program's by a relative error of at most 0.012.
The reference program's roundings to bfloat16 on the way count: a program that leaves them out, or rounds other values in their place, can miss the bound.
Values may be sent and summed in bfloat16 or wider, within the bound.
No kernel may reach another device: no remote copies, remote signals or barrier semaphores. Data moves between devices by JAX's collectives and lax.ppermute only.
A program may use at most 256 MiB of HBM per device.

```python
import math
import jax
import jax.numpy as jnp
import numpy as np
from jax import lax

D = 1024
HEADS = 16
HEAD_DIM = 64
ROT = 32
FF = 4096
SEQ_LEN = 128
MICRO = 2
BATCH = 16
N_SECTION = 2


def strengthened(values, rng, source, target, shards_of, factor):
    owner, partner = [(jnp.arange(values.shape[axis_at]) // (values.shape[axis_at] // shards_of)).reshape([-1 if axis == axis_at else 1 for axis in range(values.ndim)]) for axis_at in (source, target)]
    chosen = jax.random.permutation(rng, shards_of)[partner]
    strong = (owner == chosen) | (owner == (partner + shards_of // 2) % shards_of)
    return jnp.where(strong, factor * values, values)


def block_scale(own_key, dims, pieces, least, top_value):
    factor_of = 1.0
    for axis_at, blocks in pieces:
        heights = jax.random.uniform(jax.random.fold_in(jax.random.fold_in(own_key, 6), axis_at), (blocks,), jnp.float32, least / len(pieces), top_value / len(pieces))
        factor_of = factor_of * jnp.repeat(jnp.exp(heights), dims[axis_at] // blocks).reshape((-1,) + (1,) * (len(dims) - 1 - axis_at))
    return factor_of


def length_profile(amount, total, reach, lean):
    loads = [(1 << 20) // math.isqrt(rank ** lean) + 1 for rank in range(2, amount + 1)]
    spare, given = total - reach - (amount - 1), [1] * (amount - 1)
    while spare > 0:
        candidates = [i for i in range(amount - 1) if given[i] < reach]
        pool, left = sum([loads[i] for i in candidates]), spare
        for i in candidates:
            addition = min(reach - given[i], max(1, left * loads[i] // pool), spare)
            given[i] = given[i] + addition
            spare = spare - addition
    return np.array([reach] + given)


def ragged_sizes(own_key, count, total, bound, lean):
    if count == 2:
        one = jax.random.randint(own_key, (), max(1, total - bound), min(bound, total - 1) + 1)
        return jnp.stack([one, total - one])
    lengths = jnp.asarray(length_profile(count, total, bound, lean), jnp.int32)
    couples = (count - 1) // 2
    source_of, receiver = lengths[1:1 + 2 * couples:2], lengths[2:2 + 2 * couples:2]
    margin = jnp.minimum(source_of - 1, bound - receiver)
    passed = jax.random.randint(jax.random.fold_in(own_key, 1), (couples,), 0, 1 << 20) % (margin + 1)
    lengths = lengths.at[1:1 + 2 * couples:2].set(source_of - passed).at[2:2 + 2 * couples:2].set(receiver + passed)
    return lengths[jax.random.permutation(jax.random.fold_in(own_key, 2), count)]


def scatter_about(own_key, shape, scale, bound, cuts=(), held_as=jnp.bfloat16):
    entries = scale * jax.random.normal(own_key, shape, jnp.float32)
    if cuts:
        entries = entries * block_scale(own_key, shape, cuts, -0.22, 0.18)
    return jnp.clip(entries, -bound, bound).astype(held_as)


def heavy_noise(rng, dims, scale, reach, shards, heavy, dtype=jnp.bfloat16):
    entries = scale * jax.random.normal(rng, dims, jnp.float32)
    if shards:
        entries = entries * block_scale(rng, dims, shards, -0.22, 0.18)
    return jnp.clip(strengthened(entries, jax.random.fold_in(rng, 3), *heavy), -reach, reach).astype(dtype)


def setup_inputs(seed: int = 0) -> dict:
    splits = jax.random.split(jax.random.key(seed), 11)
    return {
        "boundary": heavy_noise(splits[0], (2, MICRO, BATCH, SEQ_LEN, D), 1.0, 8.0, ((0, 2), (2, 16)), (2, 4, 16, 2.0)),
        "segments": jax.vmap(lambda own: jnp.searchsorted(jnp.cumsum(ragged_sizes(own, 4, SEQ_LEN, SEQ_LEN // 2, 2)), jnp.arange(SEQ_LEN), side="right"))(jax.random.split(splits[1], MICRO * BATCH)).reshape((MICRO, BATCH, SEQ_LEN)).astype(jnp.int32),
        "ln_gain": jnp.clip(1.0 + 0.1 * jax.random.normal(splits[2], (N_SECTION, D), jnp.float32), 0.5, 1.5),
        "ln_bias": scatter_about(splits[3], (N_SECTION, D), 0.3, 1.75, ((0, 2), (1, 16)), jnp.float32),
        "w_qkv": scatter_about(splits[4], (N_SECTION, D, 3 * D), D ** -0.5, 0.1875, ((0, 2), (1, 16)), jnp.float32),
        "w_out": scatter_about(splits[5], (N_SECTION, D, D), (D // 16) ** -0.5, 0.75, ((0, 2), (1, 16)), jnp.float32),
        "w_in": scatter_about(splits[6], (N_SECTION, D, FF), D ** -0.5, 0.1875, ((0, 2), (1, 16)), jnp.float32),
        "b_in": scatter_about(splits[7], (N_SECTION, FF), 0.5, 3.0, ((0, 2), (1, 16)), jnp.float32),
        "w_fc": scatter_about(splits[8], (N_SECTION, FF, D), FF ** -0.5, 0.09375, ((0, 2), (1, 16)), jnp.float32),
        "b_fc": scatter_about(splits[9], (N_SECTION, D), 0.3, 1.75, ((0, 2), (1, 16)), jnp.float32),
    }


EPSILON = 1e-05
NEGATIVE = -1000000000.0
HIGHEST = lax.Precision.HIGHEST

@jax.custom_vjp
def low(v):
    return lax.optimization_barrier(v.astype(jnp.bfloat16)).astype(jnp.float32)

@jax.custom_vjp
def low_back(v):
    return v

def low_keep(v):
    return (low(v), None)

def low_pass(kept, grad):
    return (grad,)

def back_keep(v):
    return (v, None)

def back_low(kept, grad):
    return (low(grad),)
low.defvjp(low_keep, low_pass)
low_back.defvjp(back_keep, back_low)

def positions_of(segments):
    last = segments.ndim - 1
    index = lax.broadcasted_iota(jnp.int32, segments.shape, last)
    previous = jnp.concatenate([segments[..., :1] - 1, segments[..., :-1]], axis=-1)
    starts = jnp.where(segments != previous, index, 0)
    return index - lax.cummax(starts, axis=last)

def angles_of(positions, rotary):
    freq = 10000.0 ** (-jnp.arange(0, rotary, 2).astype(jnp.float32) / rotary)
    angle = positions.astype(jnp.float32)[..., None] * freq
    return (jnp.cos(angle)[..., None, :], jnp.sin(angle)[..., None, :])

def allowed_of(segments):
    length = segments.shape[-1]
    row = lax.broadcasted_iota(jnp.int32, (length, length), 0)
    col = lax.broadcasted_iota(jnp.int32, (length, length), 1)
    same = segments[..., :, None] == segments[..., None, :]
    return (same & (col <= row))[..., None, :, :]

def rotate(values, cosine, sine):
    span = cosine.shape[-1] * 2
    first = values[..., 0:span:2]
    second = values[..., 1:span:2]
    turned = jnp.stack([first * cosine - second * sine, first * sine + second * cosine], axis=-1)
    turned = turned.reshape(values.shape[:-1] + (span,))
    return jnp.concatenate([turned, values[..., span:]], axis=-1)

def gelu(value):
    return 0.5 * value * (1.0 + jnp.tanh(0.7978845608 * (value + 0.044715 * value * value * value)))

def layer(source, params, cosine, sine, allowed):
    gain, shift, w_qkv, w_out, w_in, b_in, w_fc, b_fc = params
    width = source.shape[-1]
    shape4 = source.shape[:2] + (HEADS, HEAD_DIM)
    scale = HEAD_DIM ** (-0.5)
    mean = lax.optimization_barrier(jnp.mean(source, -1, keepdims=True))
    centered = source - mean
    normed = centered * lax.rsqrt(lax.optimization_barrier(jnp.mean(centered * centered, -1, keepdims=True)) + EPSILON) * gain + shift
    normed = low(normed)
    qkv = low_back(jnp.einsum('bld,de->ble', normed, w_qkv, precision=HIGHEST))
    query = low(rotate(qkv[..., :width].reshape(shape4), cosine, sine))
    key = low(rotate(qkv[..., width:2 * width].reshape(shape4), cosine, sine))
    value = low(qkv[..., 2 * width:].reshape(shape4))
    scores = jnp.einsum('bqhe,bkhe->bhqk', query, key, precision=HIGHEST) * scale
    scores = low_back(jnp.where(allowed, scores, NEGATIVE))
    top = lax.optimization_barrier(jnp.max(scores, -1, keepdims=True))
    expo = jnp.exp(scores - top)
    probs = low(expo / lax.optimization_barrier(jnp.sum(expo, -1, keepdims=True)))
    attended = jnp.einsum('bhqk,bkhe->bqhe', probs, value, precision=HIGHEST).reshape(source.shape)
    attended = low_back(low(attended))
    attention = jnp.einsum('bld,de->ble', attended, w_out, precision=HIGHEST)
    pre = low_back(jnp.einsum('bld,df->blf', normed, w_in, precision=HIGHEST) + b_in)
    active = low(gelu(pre))
    mixed = jnp.einsum('blf,fd->bld', active, w_fc, precision=HIGHEST) + b_fc
    return source + attention + mixed

def reference(boundary, segments, ln_gain, ln_bias, w_qkv, w_out, w_in, b_in, w_fc, b_fc):
    rows = MICRO * BATCH
    source = boundary[0].astype(jnp.float32).reshape(rows, SEQ_LEN, D)
    cotangent = boundary[1].astype(jnp.float32).reshape(rows, SEQ_LEN, D)
    segs = segments.reshape(rows, SEQ_LEN)
    cosine, sine = angles_of(positions_of(segs), ROT)
    allowed = allowed_of(segs)
    group = math.gcd(rows, max(1, 4096 // SEQ_LEN))
    count = rows // group

    def split(array):
        return array.reshape((count, group) + array.shape[1:])
    masters = (ln_gain, ln_bias, w_qkv, w_out, w_in, b_in, w_fc, b_fc)

    def chain(start, weights):
        first = tuple((low(w[0]) for w in weights))
        second = tuple((low(w[1]) for w in weights))

        def run(items):
            block, cos_block, sin_block, allow_block = items
            middle = layer(block, first, cos_block, sin_block, allow_block)
            middle = low_back(low(middle))
            return layer(middle, second, cos_block, sin_block, allow_block)
        result = lax.map(jax.checkpoint(run), (split(start), split(cosine), split(sine), split(allowed)))
        return result.reshape(rows, SEQ_LEN, D)
    result, pullback = jax.vjp(chain, source, masters)
    g_source, grads = pullback(cotangent)
    boundary_out = jnp.stack([g_source, result]).reshape(2, MICRO, BATCH, SEQ_LEN, D)
    return (boundary_out, grads[0], grads[1], grads[2], grads[3], grads[4], grads[5], grads[6], grads[7])
```

```python
import functools

import jax
import jax.numpy as jnp
from jax import lax
from jax.experimental import pallas as pl
from jax.experimental.pallas import tpu as pltpu
from jax.sharding import PartitionSpec as P

D = 1024
PAIR = 128
FB = 512
CI = 3 * PAIR + FB
RO = PAIR + FB
EPS = 1e-05
NEG = -1000000000.0
SCALE = 0.125
ROWS = 128
TOK = 4 * ROWS
BF = jnp.bfloat16
F32 = jnp.float32
VMEM_LIMIT = 56 * 1024 * 1024


def mm(a, b):
    return lax.dot_general(a, b, (((1,), (0,)), ((), ())), preferred_element_type=F32)


def mm_nt(a, b):
    return lax.dot_general(a, b, (((1,), (1,)), ((), ())), preferred_element_type=F32)


def mm_tn(a, b):
    return lax.dot_general(a, b, (((0,), (0,)), ((), ())), preferred_element_type=F32)


def gelu(h):
    return 0.5 * h * (1.0 + jnp.tanh(0.7978845608 * (h + 0.044715 * h * h * h)))


def gelu_slope(h):
    th = jnp.tanh(0.7978845608 * (h + 0.044715 * h * h * h))
    inner = 0.7978845608 * (1.0 + 3 * 0.044715 * h * h)
    return 0.5 * (1.0 + th) + 0.5 * h * (1.0 - th * th) * inner


def partner(x):
    lane = lax.broadcasted_iota(jnp.int32, x.shape, 1)
    return jnp.where(lane % 2 == 0, pltpu.roll(x, PAIR - 1, 1), pltpu.roll(x, 1, 1))


def turned(x, cosine, sine):
    return x * cosine + partner(x) * sine


def by_head(x):
    lane = lax.broadcasted_iota(jnp.int32, (1, PAIR), 1)
    low = jnp.where(lane < 64, 1.0, 0.0).astype(x.dtype)
    high = jnp.where(lane < 64, 0.0, 1.0).astype(x.dtype)
    return jnp.concatenate([x * low, x * high], axis=0)


def beside(x):
    return jnp.concatenate([x[:ROWS], x[ROWS:]], axis=1)


def rows_of(j):
    return pl.ds(j * ROWS, ROWS)


def layer_norm_into(x_refs, gain_ref, bias_ref, normed):
    for j, x_ref in enumerate(x_refs):
        x = x_ref[0:ROWS, :].astype(F32)
        centered = x - jnp.mean(x, -1, keepdims=True)
        inv = lax.rsqrt(jnp.mean(centered * centered, -1, keepdims=True) + EPS)
        normed[rows_of(j), :] = (centered * inv * gain_ref[...] + bias_ref[...]).astype(BF)


def forward_in(g, normed, wi, bin_ref, cos_ref, sin_ref, mask_ref, qkv, probs, oa, pre):
    y = mm(normed[...], wi[g, :, 0 : 3 * PAIR])
    cosine, sine = cos_ref[...], sin_ref[...]
    qkv[g, :, 0:PAIR] = turned(y[:, 0:PAIR], cosine, sine).astype(BF)
    qkv[g, :, PAIR : 2 * PAIR] = turned(y[:, PAIR : 2 * PAIR], cosine, sine).astype(BF)
    qkv[g, :, 2 * PAIR : 3 * PAIR] = y[:, 2 * PAIR : 3 * PAIR].astype(BF)
    for j in range(4):
        q = qkv[g, rows_of(j), 0:PAIR]
        k = qkv[g, rows_of(j), PAIR : 2 * PAIR]
        v = qkv[g, rows_of(j), 2 * PAIR : 3 * PAIR]
        s = mm_nt(by_head(q), k) * SCALE
        allowed = mask_ref[j]
        s = jnp.where(jnp.concatenate([allowed, allowed], axis=0) > 0.5, s, NEG)
        e = jnp.exp(s - jnp.max(s, -1, keepdims=True))
        p = e / jnp.sum(e, -1, keepdims=True)
        probs[g, j] = p
        oa[g, rows_of(j), 0:PAIR] = mm(beside(p.astype(BF)), by_head(v)).astype(BF)
    h = mm(normed[...], wi[g, :, 3 * PAIR : CI]) + bin_ref[g : g + 1, :]
    pre[g] = h
    oa[g, :, PAIR:RO] = gelu(h).astype(BF)


def forward_out(oa, wo, outs):
    for n in range(4):
        cols = slice(n * 256, (n + 1) * 256)
        part = mm(oa[0], wo[0, :, cols]) + mm(oa[1], wo[1, :, cols])
        for j in range(4):
            outs[j][:, cols] = part[j * ROWS : (j + 1) * ROWS].astype(outs[j].dtype)


def backward_out(g, gout, wo, qkv, probs, pre, cos_ref, sin_ref, gcat, gbin_ref):
    go = mm_nt(gout[...], wo[g, 0:PAIR, :]).astype(BF)
    for j in range(4):
        q = qkv[g, rows_of(j), 0:PAIR]
        k = qkv[g, rows_of(j), PAIR : 2 * PAIR]
        v = qkv[g, rows_of(j), 2 * PAIR : 3 * PAIR]
        cosine, sine = cos_ref[rows_of(j), :], sin_ref[rows_of(j), :]
        go2 = by_head(go[j * ROWS : (j + 1) * ROWS])
        p = probs[g, j]
        gp = mm_nt(go2, v)
        gs = (p * (gp - jnp.sum(gp * p, -1, keepdims=True))).astype(BF)
        gv = mm_tn(p.astype(BF), go2)
        gq = mm(beside(gs), by_head(k)) * SCALE
        gk = mm_tn(gs, by_head(q)) * SCALE
        gcat[g, rows_of(j), 0:PAIR] = turned(gq, cosine, -sine).astype(BF)
        gcat[g, rows_of(j), PAIR : 2 * PAIR] = turned(gk, cosine, -sine).astype(BF)
        gcat[g, rows_of(j), 2 * PAIR : 3 * PAIR] = gv.astype(BF)
    ga = mm_nt(gout[...], wo[g, PAIR:RO, :])
    gpre = (ga * gelu_slope(pre[g])).astype(BF)
    gcat[g, :, 3 * PAIR : CI] = gpre
    gbin_ref[g : g + 1, :] = jnp.sum(gpre.astype(F32), 0, keepdims=True)


def backward_in(gcat, wi, outs):
    for n in range(4):
        cols = slice(n * 256, (n + 1) * 256)
        part = mm_nt(gcat[0], wi[0, cols, :]) + mm_nt(gcat[1], wi[1, cols, :])
        for j in range(4):
            outs[j][:, cols] = part[j * ROWS : (j + 1) * ROWS].astype(outs[j].dtype)


def input_copies(fast, refs, wi, sems, place):
    if not fast:
        return [pltpu.make_async_copy(refs[0], wi, sems.at[0])]
    me, core = place
    copies = []
    for own in range(2):
        g = core if own == 0 else 1 - core
        for f, flip in enumerate((0, 8, 1, 9)):
            for j in range(4):
                source = jnp.bitwise_xor(me, flip ^ (2 * j))
                start = pl.multiple_of(source * 64, 64)
                copies.append(
                    pltpu.make_async_copy(
                        refs[own * 4 + f].at[j], wi.at[g, pl.ds(start, 64), :], sems.at[len(copies)]
                    )
                )
    return copies


def output_copies(fast, refs, wo, sems, place):
    if not fast:
        return [pltpu.make_async_copy(refs[0], wo, sems.at[0])]
    me, core = place
    copies = []
    for own in range(2):
        half = core if own == 0 else 1 - core
        for f, flip in enumerate((0, 8, 1, 9)):
            source = jnp.bitwise_xor(me, flip)
            g, r = source // 8, source % 2
            ref = refs[own * 4 + f]
            first = pl.multiple_of(64 * r + 32 * half, 32)
            second = pl.multiple_of(PAIR + 256 * r + 128 * half, 128)
            copies.append(
                pltpu.make_async_copy(ref.at[0:32], wo.at[g, pl.ds(first, 32), :], sems.at[len(copies)])
            )
            copies.append(
                pltpu.make_async_copy(ref.at[32:160], wo.at[g, pl.ds(second, 128), :], sems.at[len(copies)])
            )
    return copies


def place_of(fast):
    return (lax.axis_index("dp"), lax.axis_index("section")) if fast else None


def first_forward_kernel(fast, n_chunks, *refs):
    x_refs, refs = refs[:4], refs[4:]
    (gain, bias, bin_ref, cos_ref, sin_ref, mask_ref), refs = refs[:6], refs[6:]
    wi_refs, wo_refs, refs = refs[:n_chunks], refs[n_chunks : 2 * n_chunks], refs[2 * n_chunks :]
    outs, refs = refs[:4], refs[4:]
    normed, qkv, probs, oa, pre, wi, wo, sem_i, sem_o = refs
    place = place_of(fast)
    loads_i = input_copies(fast, wi_refs, wi, sem_i, place)
    loads_o = output_copies(fast, wo_refs, wo, sem_o, place)
    for copy in loads_i + loads_o:
        copy.start()
    layer_norm_into(x_refs, gain, bias, normed)
    for copy in loads_i:
        copy.wait()
    for g in range(2):
        forward_in(g, normed, wi, bin_ref, cos_ref, sin_ref, mask_ref, qkv, probs, oa, pre)
    for copy in loads_o:
        copy.wait()
    forward_out(oa, wo, outs)


def second_layer_kernel(fast, n_chunks, *refs):
    x_refs, gout_refs, refs = refs[:4], refs[4:8], refs[8:]
    (gain, bias, bin_ref, cos_ref, sin_ref, mask_ref), refs = refs[:6], refs[6:]
    wi_refs, wo_refs, refs = refs[:n_chunks], refs[n_chunks : 2 * n_chunks], refs[2 * n_chunks :]
    outs, gouts, refs = refs[:4], refs[4:8], refs[8:]
    normed, gcat, oa, gbin_ref, qkv, probs, pre, gout, wi, wo, sem_i, sem_o = refs
    place = place_of(fast)
    loads_i = input_copies(fast, wi_refs, wi, sem_i, place)
    loads_o = output_copies(fast, wo_refs, wo, sem_o, place)
    for copy in loads_i + loads_o:
        copy.start()
    layer_norm_into(x_refs, gain, bias, normed)
    for j in range(4):
        gout[rows_of(j), :] = gout_refs[j][ROWS : 2 * ROWS, :]
    for copy in loads_i:
        copy.wait()
    for g in range(2):
        forward_in(g, normed, wi, bin_ref, cos_ref, sin_ref, mask_ref, qkv, probs, oa, pre)
    for copy in loads_o:
        copy.wait()
    for g in range(2):
        backward_out(g, gout, wo, qkv, probs, pre, cos_ref, sin_ref, gcat, gbin_ref)
    backward_in(gcat, wi, gouts)
    forward_out(oa, wo, outs)


def first_backward_kernel(fast, n_chunks, *refs):
    gout_refs, refs = refs[:4], refs[4:]
    (cos_ref, sin_ref, qkv, probs, pre), refs = refs[:5], refs[5:]
    wi_refs, wo_refs, refs = refs[:n_chunks], refs[n_chunks : 2 * n_chunks], refs[2 * n_chunks :]
    gouts, refs = refs[:4], refs[4:]
    gcat, gbin_ref, gout, wi, wo, sem_i, sem_o = refs
    place = place_of(fast)
    loads_i = input_copies(fast, wi_refs, wi, sem_i, place)
    loads_o = output_copies(fast, wo_refs, wo, sem_o, place)
    for copy in loads_o + loads_i:
        copy.start()
    for j in range(4):
        gout[rows_of(j), :] = gout_refs[j][...]
    for copy in loads_o:
        copy.wait()
    for g in range(2):
        backward_out(g, gout, wo, qkv, probs, pre, cos_ref, sin_ref, gcat, gbin_ref)
    for copy in loads_i:
        copy.wait()
    backward_in(gcat, wi, gouts)


def weight_grad_out_kernel(fast, first, *refs):
    gout_refs, oa, refs = refs[:4], refs[4], refs[5:]
    *outs, gout = refs
    for j in range(4):
        gout[rows_of(j), :] = gout_refs[j][first : first + ROWS, :]
    if fast:
        keep, send = outs
        me, core = place_of(fast)
    for g in range(2):
        for r in range(2):
            small = mm_tn(oa[g, :, 64 * r : 64 * r + 64], gout[...]).astype(BF)
            large = mm_tn(oa[g, :, PAIR + 256 * r : PAIR + 256 * (r + 1)], gout[...]).astype(BF)
            if not fast:
                outs[0][g, 64 * r : 64 * r + 64, :] = small
                outs[0][g, PAIR + 256 * r : PAIR + 256 * (r + 1), :] = large
                continue
            flip = 2 * jnp.bitwise_xor(me % 2, r) + jnp.bitwise_xor(me // 8, g)

            @pl.when(core == 0)
            def _():
                keep[flip, 0:32, :], keep[flip, 32:160, :] = small[:32], large[:128]
                send[flip, 0:32, :], send[flip, 32:160, :] = small[32:], large[128:]

            @pl.when(core == 1)
            def _():
                keep[flip, 0:32, :], keep[flip, 32:160, :] = small[32:], large[128:]
                send[flip, 0:32, :], send[flip, 32:160, :] = small[:32], large[:128]


def weight_grad_in_kernel(fast, normed, gcat, *outs):
    if not fast:
        for g in range(2):
            for m in range(4):
                outs[0][g, m * 256 : (m + 1) * 256, :] = mm_tn(normed[:, m * 256 : (m + 1) * 256], gcat[g]).astype(BF)
        return
    me, core = place_of(fast)
    for own in (1, 0):
        g = core if own == 0 else 1 - core
        for m in range(4):
            part = mm_tn(normed[:, m * 256 : (m + 1) * 256], gcat[g]).astype(BF)
            for b in range(4):
                apart = jnp.bitwise_xor(me, 4 * m + b)
                flip, j = 2 * (apart % 2) + apart // 8, (apart // 2) % 4
                outs[own][flip, j] = part[64 * b : 64 * b + 64]


def norm_backward_kernel(own, r1, r2, r3, x_ref, gout_ref, gain, gx_ref, low_ref, sums_ref):
    x = x_ref[0:ROWS, :].astype(F32)
    gn = own[...] + r1[...].astype(F32) + r2[...].astype(F32) + r3[...].astype(F32)
    base = gout_ref.shape[0] - ROWS
    gout = gout_ref[base : base + ROWS, :].astype(F32)
    centered = x - jnp.mean(x, -1, keepdims=True)
    inv = lax.rsqrt(jnp.mean(centered * centered, -1, keepdims=True) + EPS)
    unit = centered * inv
    gu = gn * gain[...]
    gx = gout + inv * (gu - jnp.mean(gu, -1, keepdims=True) - unit * jnp.mean(gu * unit, -1, keepdims=True))
    gx_ref[...] = gx
    low_ref[...] = gx.astype(BF)
    sums_ref[0:1, :] = jnp.sum(gn * unit, 0, keepdims=True)
    sums_ref[1:2, :] = jnp.sum(gn, 0, keepdims=True)
    sums_ref[2:3, :] = jnp.sum(gout, 0, keepdims=True)


def pack_kernel(w_qkv, w_out, w_in, w_fc, wi_keep, wi_send, wo_keep, wo_send):
    t, core = (lax.axis_index("dp") // 2) % 4, lax.axis_index("section")
    for ref, g in ((wi_keep, core), (wi_send, 1 - core)):
        for j in range(4):
            rank = jnp.bitwise_xor(t, j)
            for part in range(3):
                start = pl.multiple_of(part * D + g * 512 + rank * PAIR, PAIR)
                ref[j, :, part * PAIR : (part + 1) * PAIR] = w_qkv[:, pl.ds(start, PAIR)].astype(BF)
            start = pl.multiple_of(g * 2048 + rank * FB, FB)
            ref[j, :, 3 * PAIR : CI] = w_in[:, pl.ds(start, FB)].astype(BF)
    for ref, half in ((wo_keep, core), (wo_send, 1 - core)):
        ref[0:32, :] = w_out[pl.ds(pl.multiple_of(32 * half, 32), 32), :].astype(BF)
        ref[32:160, :] = w_fc[pl.ds(pl.multiple_of(128 * half, 128), 128), :].astype(BF)


def unpack_kernel(own0, own1, own2, own3, other, wo_own, wo_other, g_qkv, g_out, g_in, g_fc):
    t, core = (lax.axis_index("dp") // 2) % 4, lax.axis_index("section")
    for side, g in ((0, core), (1, 1 - core)):
        for j in range(4):
            block = (own0, own1, own2, own3)[j][...] if side == 0 else other[j]
            block = block.astype(F32)
            rank = jnp.bitwise_xor(t, j)
            for part in range(3):
                start = pl.multiple_of(part * D + g * 512 + rank * PAIR, PAIR)
                g_qkv[:, pl.ds(start, PAIR)] = block[:, part * PAIR : (part + 1) * PAIR]
            start = pl.multiple_of(g * 2048 + rank * FB, FB)
            g_in[:, pl.ds(start, FB)] = block[:, 3 * PAIR : CI]
    for ref, half in ((wo_own, core), (wo_other, 1 - core)):
        g_out[pl.ds(pl.multiple_of(32 * half, 32), 32), :] = ref[0:32, :].astype(F32)
        g_fc[pl.ds(pl.multiple_of(128 * half, 128), 128), :] = ref[32:160, :].astype(F32)


VM = pl.BlockSpec(memory_space=pltpu.VMEM)
HB = pl.BlockSpec(memory_space=pl.ANY)


def kernel_call(kernel, args, outs, any_args=0, scratch=(), flops=1e6, name=None):
    sizes = [a.size * a.dtype.itemsize for a in args] + [a.size * a.dtype.itemsize for a in outs]
    return pl.pallas_call(
        kernel,
        out_shape=outs,
        in_specs=[VM] * (len(args) - any_args) + [HB] * any_args,
        out_specs=[VM] * len(outs),
        scratch_shapes=list(scratch),
        compiler_params=pltpu.CompilerParams(vmem_limit_bytes=VMEM_LIMIT),
        cost_estimate=pl.CostEstimate(flops=int(flops), bytes_accessed=int(sum(sizes)), transcendentals=0),
        name=name,
    )(*args)


def arr(shape, dtype):
    return jax.ShapeDtypeStruct(shape, dtype)


def weight_scratch(fast):
    return [
        pltpu.VMEM((2, D, CI), BF),
        pltpu.VMEM((2, RO, D), BF),
        pltpu.SemaphoreType.DMA((32 if fast else 1,)),
        pltpu.SemaphoreType.DMA((16 if fast else 1,)),
    ]


def partial_outs():
    return [arr((ROWS, D), F32)] + [arr((ROWS, D), BF)] * 3


def swap_core(value):
    return lax.ppermute(value, "section", [(0, 1), (1, 0)])


def flipped(value, flip, count):
    return lax.ppermute(value, "dp", [(i, i ^ flip) for i in range(count)])


def small_pack(gain, bias, b_fc, b_in):
    return jnp.concatenate([gain, bias, b_fc, b_in], axis=-1)


def body(boundary, segments, ln_gain, ln_bias, w_qkv, w_out, w_in, b_in, w_fc, b_fc):
    core, me = lax.axis_index("section"), lax.axis_index("dp")
    count = lax.axis_size("dp")
    fast = count == 16
    spread = count // 8
    rank = (me // spread) % 4
    steps = [j * spread for j in range(4)]
    first_core = core == 0
    share = D // count
    share_in = 4 * D // count
    width_small = 3 * share + share_in

    def across(values):
        return [flipped(v, steps[j + 1], count) for j, v in enumerate(values)]

    def choose(keep, recv):
        return jnp.where(first_core, keep, recv), jnp.where(first_core, recv, keep)

    swapped = swap_core(lax.dynamic_index_in_dim(boundary[0], 1 - core, 0, False)[0])
    kept = lax.dynamic_index_in_dim(boundary[0], core, 0, False)[0]
    x0, g1 = choose(kept, swapped)
    small = small_pack(ln_gain, ln_bias, b_fc, b_in).astype(BF)
    small0, small1 = choose(small, swap_core(small))
    seg = lax.dynamic_index_in_dim(segments, core, 0, False)[0].astype(BF)

    if fast:
        extra = jnp.concatenate(
            [
                jnp.pad(seg[None], ((0, 0), (0, D - ROWS))),
                jnp.pad(jnp.concatenate([small0, small1]), ((0, 13 + 0), (0, D - width_small))),
            ]
        )[:16]
    else:
        extra = jnp.zeros((16, D), BF).at[0, :ROWS].set(seg)
    pack = jnp.concatenate([x0, g1, extra])

    if fast:
        wi_keep, wi_send, wo_keep, wo_send = kernel_call(
            pack_kernel,
            [w_qkv[0], w_out[0], w_in[0], w_fc[0]],
            [arr((4, 64, CI), BF), arr((4, 64, CI), BF), arr((160, D), BF), arr((160, D), BF)],
            name="pack",
        )
        wi_recv, wo_recv = swap_core(wi_send), swap_core(wo_send)
        wi_first = [choose(wi_keep[j], wi_recv[j]) for j in range(4)]
        wo_first = choose(wo_keep, wo_recv)

        def gather(layer):
            mine = [w[layer] for w in wi_first]
            arrived = across(mine[1:])
            wi_own = jnp.stack([mine[0]] + arrived)
            wi_far = flipped(wi_own, 8, count)
            wi_got = [wi_own, wi_far, flipped(wi_own, 1, count), flipped(wi_far, 1, count)]
            wo_own = wo_first[layer]
            wo_far = flipped(wo_own, 8, count)
            wo_got = [wo_own, wo_far, flipped(wo_own, 1, count), flipped(wo_far, 1, count)]
            return wi_got + [swap_core(w) for w in wi_got], wo_got + [swap_core(w) for w in wo_got]

    else:
        t_groups = [
            [g * 4 * spread + t * spread + r for t in range(4)] for g in range(2) for r in range(spread)
        ]
        f_groups = [
            [g * 4 * spread + t * spread + r for g in range(2) for r in range(spread)] for t in range(4)
        ]
        wi = jnp.concatenate(
            [
                w_qkv[0].astype(BF).reshape(share, 3, 2, 4, PAIR).transpose(3, 0, 2, 1, 4).reshape(4, share, 2, 3 * PAIR),
                w_in[0].astype(BF).reshape(share, 2, 4, FB).transpose(2, 0, 1, 3),
            ],
            axis=-1,
        )
        wi = lax.all_to_all(wi, "dp", 0, 0, axis_index_groups=t_groups, tiled=True)
        wi = lax.all_gather(wi, "dp", axis_index_groups=f_groups)
        wi = wi.reshape(2, spread, 4, share, 2, CI).transpose(4, 0, 2, 1, 3, 5).reshape(2, D, CI)
        wo = lax.all_gather(w_out[0].astype(BF), "dp", axis_index_groups=f_groups).reshape(2, PAIR, D)
        wf = lax.all_gather(w_fc[0].astype(BF), "dp", axis_index_groups=f_groups).reshape(2, FB, D)
        wo = jnp.concatenate([wo, wf], axis=1)
        wi_both, wo_both = choose(wi, swap_core(wi)), choose(wo, swap_core(wo))

        def gather(layer):
            return [wi_both[layer]], [wo_both[layer]]

    n_chunks = 8 if fast else 1
    wi0, wo0 = gather(0)
    packs = [pack] + across([pack] * 3)
    wi1, wo1 = gather(1)

    if fast:
        held = jnp.stack([p[257:259, :width_small] for p in packs])
        held = jnp.concatenate([held, flipped(held, 8, count)])
        held = jnp.concatenate([held, flipped(held, 1, count)]).reshape(16, 2 * width_small)
        index = jnp.arange(16)
        flip_of = jnp.bitwise_xor(index, me)
        at = (flip_of % 2) * 8 + (flip_of // 8) * 4 + (flip_of // 2) % 4
        onehot = (at[:, None] == index[None, :]).astype(BF)
        everyone = mm(onehot, held).reshape(16, 2, width_small)
    else:
        everyone = lax.all_gather(jnp.concatenate([small0, small1]), "dp").astype(F32)

    def small_of(layer):
        one = everyone[:, layer]
        vectors = [one[:, i * share : (i + 1) * share].reshape(1, D) for i in range(3)]
        b = one[:, 3 * share :].reshape(2, 4, spread * share_in)
        b = lax.dynamic_index_in_dim(b, rank, 1, False)
        return vectors[0], vectors[1], vectors[2], b

    gain0, bias0, bfc0, bin0 = small_of(0)
    gain1, bias1, bfc1, bin1 = small_of(1)

    segs = jnp.stack([p[256, :ROWS] for p in packs])
    row = lax.broadcasted_iota(jnp.int32, (ROWS, ROWS), 0)
    col = lax.broadcasted_iota(jnp.int32, (ROWS, ROWS), 1)
    mask = ((segs[:, :, None] == segs[:, None, :]) & (col <= row)).astype(F32)
    positions = jnp.sum(mask, -1).reshape(TOK, 1) - 1.0
    lane = jnp.arange(PAIR) % 64
    freq = jnp.where(lane < 32, 10000.0 ** (-(lane // 2 * 2).astype(F32) / 32), 0.0)
    angle = positions * freq
    cosine = jnp.cos(angle)
    sine = jnp.sin(angle) * jnp.where(lane % 2 == 0, -1.0, 1.0)

    layer_flops = 2 * TOK * 2 * (D * CI + RO * D)
    saved = [
        arr((TOK, D), BF),
        arr((2, TOK, 3 * PAIR), BF),
        arr((2, 4, 2 * ROWS, ROWS), F32),
        arr((2, TOK, RO), BF),
        arr((2, TOK, FB), F32),
    ]
    got = kernel_call(
        functools.partial(first_forward_kernel, fast, n_chunks),
        [*packs, gain0, bias0, bin0, cosine, sine, mask, *wi0, *wo0],
        partial_outs() + saved,
        any_args=2 * n_chunks,
        scratch=weight_scratch(fast),
        flops=layer_flops,
        name="first_forward",
    )
    own, sends, (normed0, qkv0, probs0, oa0, pre0) = got[0], got[1:4], got[4:]

    def total(own, sends):
        return sum([r.astype(F32) for r in across(sends)], own)

    x1 = (x0.astype(F32) + total(own, sends) + bfc0).astype(BF)
    x1s = [x1] + across([x1] * 3)

    got = kernel_call(
        functools.partial(second_layer_kernel, fast, n_chunks),
        [*x1s, *packs, gain1, bias1, bin1, cosine, sine, mask, *wi1, *wo1],
        partial_outs()
        + partial_outs()
        + [arr((TOK, D), BF), arr((2, TOK, CI), BF), arr((2, TOK, RO), BF), arr((2, FB), F32)],
        any_args=2 * n_chunks,
        scratch=[
            pltpu.VMEM((2, TOK, 3 * PAIR), BF),
            pltpu.VMEM((2, 4, 2 * ROWS, ROWS), F32),
            pltpu.VMEM((2, TOK, FB), F32),
            pltpu.VMEM((TOK, D), BF),
        ]
        + weight_scratch(fast),
        flops=2 * layer_flops,
        name="second_layer",
    )
    out_own, out_sends, gn_own, gn_sends = got[0], got[1:4], got[4], got[5:8]
    normed1, gcat1, oa1, gbin1 = got[8:]

    def norm_backward(own, arrived, x, gout, gain, name):
        return kernel_call(
            norm_backward_kernel,
            [own, *arrived, x, gout, gain],
            [arr((ROWS, D), F32), arr((ROWS, D), BF), arr((3, D), F32)],
            name=name,
        )

    _, g0, sums1 = norm_backward(gn_own, across(gn_sends), x1, g1, gain1, "norm_backward1")
    g0s = [g0] + across([g0] * 3)
    out1 = x1.astype(F32) + total(out_own, out_sends) + bfc1

    def weight_grads(gouts, first, oa, normed, gcat, name):
        if fast:
            outs_o = [arr((4, 160, D), BF)] * 2
            outs_i = [arr((4, 4, 64, CI), BF)] * 2
        else:
            outs_o, outs_i = [arr((2, RO, D), BF)], [arr((2, D, CI), BF)]
        go = kernel_call(
            functools.partial(weight_grad_out_kernel, fast, first),
            [*gouts, oa],
            outs_o,
            scratch=[pltpu.VMEM((TOK, D), BF)],
            flops=2 * TOK * 2 * RO * D,
            name=name + "_out",
        )
        gi = kernel_call(
            functools.partial(weight_grad_in_kernel, fast),
            [normed, gcat],
            outs_i,
            flops=2 * TOK * 2 * CI * D,
            name=name + "_in",
        )
        return go, gi

    def reduce_over_f(keep, send):
        arrived = swap_core(send)
        both = keep.astype(F32) + arrived.astype(F32)
        near = flipped(both[2:4].astype(BF), 1, count)
        both = both[0:2] + near.astype(F32)
        far = flipped(both[1].astype(BF), 8, count)
        return both[0] + far.astype(F32)

    def reduce_fast(grads):
        go, gi = grads
        wo = reduce_over_f(*go)
        wi = reduce_over_f(*gi)
        parts = [wi[0].astype(BF)] + across([wi[j].astype(BF) for j in range(1, 4)])
        return wo.astype(BF), parts

    grads1 = weight_grads(packs, ROWS, oa1, normed1, gcat1, "grads1")

    got = kernel_call(
        functools.partial(first_backward_kernel, fast, n_chunks),
        [*g0s, cosine, sine, qkv0, probs0, pre0, *wi0, *wo0],
        partial_outs() + [arr((2, TOK, CI), BF), arr((2, FB), F32)],
        any_args=2 * n_chunks,
        scratch=[pltpu.VMEM((TOK, D), BF)] + weight_scratch(fast),
        flops=layer_flops,
        name="first_backward",
    )
    gn_own, gn_sends, gcat0, gbin0 = got[0], got[1:4], got[4], got[5]
    grads0 = weight_grads(g0s, 0, oa0, normed0, gcat0, "grads0")
    gx0, _, sums0 = norm_backward(gn_own, across(gn_sends), x0, g0, gain0, "norm_backward0")

    arrived = swap_core(jnp.where(first_core, out1, gx0))
    boundary_out = jnp.where(
        first_core, jnp.stack([gx0, arrived]), jnp.stack([arrived, out1])
    )[None, :, None]

    def small_grads(sums, gbin):
        vectors = sums.reshape(3, count, share).transpose(1, 0, 2).reshape(count, 3 * share)
        onehot = (jnp.arange(4) == rank).astype(F32)
        b = gbin.reshape(2, 1, spread, share_in) * onehot[None, :, None, None]
        return jnp.concatenate([vectors, b.reshape(count, share_in)], axis=1)

    both = choose(small_grads(sums0, gbin0), small_grads(sums1, gbin1))
    vector = both[0] + swap_core(both[1])
    if fast:
        for flip in (2, 4, 1, 8):
            vector = vector + flipped(vector, flip, count)
        vector = lax.dynamic_index_in_dim(vector, me, 0, True)
    else:
        vector = lax.psum_scatter(vector, "dp", scatter_dimension=0, tiled=True)
    g_gain, g_bias, g_bfc = (vector[:, i * share : (i + 1) * share] for i in range(3))
    g_bin = vector[:, 3 * share :]

    if fast:
        wo_1, wi_1 = reduce_fast(grads1)
        wo_0, wi_0 = reduce_fast(grads0)
        wo_mine, wo_theirs = choose(wo_0, wo_1)
        pairs = [choose(a, b) for a, b in zip(wi_0, wi_1)]
        wi_other = swap_core(jnp.stack([p[1] for p in pairs]))
        g_qkv, g_out, g_in, g_fc = kernel_call(
            unpack_kernel,
            [*[p[0] for p in pairs], wi_other, wo_mine, swap_core(wo_theirs)],
            [arr((64, 3 * D), F32), arr((64, D), F32), arr((64, 4 * D), F32), arr((256, D), F32)],
            name="unpack",
        )
    else:
        (go1,), (gi1,) = grads1
        (go0,), (gi0,) = grads0
        mine, theirs = choose(gi0, gi1)
        gi = mine.astype(F32) + swap_core(theirs).astype(F32)
        mine, theirs = choose(go0, go1)
        go = mine.astype(F32) + swap_core(theirs).astype(F32)
        gi = gi.reshape(2, 2, 4, spread, share, CI).transpose(1, 3, 2, 4, 0, 5).reshape(2 * spread, 4, share, 2, CI)
        gi = lax.psum_scatter(gi, "dp", scatter_dimension=0, axis_index_groups=f_groups)
        gi = lax.all_to_all(gi, "dp", 0, 0, axis_index_groups=t_groups, tiled=True)
        g_qkv = gi[..., : 3 * PAIR].reshape(4, share, 2, 3, PAIR).transpose(1, 3, 2, 0, 4).reshape(share, 3 * D)
        g_in = gi[..., 3 * PAIR :].transpose(1, 2, 0, 3).reshape(share, 4 * D)
        g_out = lax.psum_scatter(
            go[:, :PAIR].reshape(2 * spread, share, D), "dp", scatter_dimension=0, axis_index_groups=f_groups
        )
        g_fc = lax.psum_scatter(
            go[:, PAIR:].reshape(2 * spread, share_in, D), "dp", scatter_dimension=0, axis_index_groups=f_groups
        )

    return (boundary_out, g_gain, g_bias, g_qkv[None], g_out[None], g_in[None], g_bin, g_fc[None], g_bfc)


def solution(mesh):
    rows = P("section", None, "dp", None, None)
    vector, matrix = P("section", "dp"), P("section", "dp", None)
    return jax.shard_map(
        body,
        mesh=mesh,
        in_specs=(rows, P(None, "dp", None), vector, vector, matrix, matrix, matrix, vector, matrix, vector),
        out_specs=(rows, vector, vector, matrix, matrix, matrix, vector, matrix, vector),
        check_vma=False,
    )
```

```python
import functools

import jax
import jax.numpy as jnp
from jax import lax
from jax.experimental import pallas as pl
from jax.experimental.pallas import tpu as pltpu
from jax.sharding import PartitionSpec as P

D = 1024
PAIR = 128
FB = 512
CI = 3 * PAIR + FB
RO = PAIR + FB
EPS = 1e-05
NEG = -1000000000.0
SCALE = 0.125
ROWS = 128
TOK = 4 * ROWS
BF = jnp.bfloat16
F32 = jnp.float32
VMEM_LIMIT = 56 * 1024 * 1024


def mm(a, b):
    return lax.dot_general(a, b, (((1,), (0,)), ((), ())), preferred_element_type=F32)


def mm_nt(a, b):
    return lax.dot_general(a, b, (((1,), (1,)), ((), ())), preferred_element_type=F32)


def mm_tn(a, b):
    return lax.dot_general(a, b, (((0,), (0,)), ((), ())), preferred_element_type=F32)


def gelu(h):
    return 0.5 * h * (1.0 + jnp.tanh(0.7978845608 * (h + 0.044715 * h * h * h)))


def gelu_slope(h):
    th = jnp.tanh(0.7978845608 * (h + 0.044715 * h * h * h))
    inner = 0.7978845608 * (1.0 + 3 * 0.044715 * h * h)
    return 0.5 * (1.0 + th) + 0.5 * h * (1.0 - th * th) * inner


def partner(x):
    lane = lax.broadcasted_iota(jnp.int32, x.shape, 1)
    return jnp.where(lane % 2 == 0, pltpu.roll(x, PAIR - 1, 1), pltpu.roll(x, 1, 1))


def turned(x, cosine, sine):
    return x * cosine + partner(x) * sine


def by_head(x):
    lane = lax.broadcasted_iota(jnp.int32, (1, PAIR), 1)
    low = jnp.where(lane < 64, 1.0, 0.0).astype(x.dtype)
    high = jnp.where(lane < 64, 0.0, 1.0).astype(x.dtype)
    return jnp.concatenate([x * low, x * high], axis=0)


def beside(x):
    return jnp.concatenate([x[:ROWS], x[ROWS:]], axis=1)


def rows_of(j):
    return pl.ds(j * ROWS, ROWS)


def layer_norm_into(x_refs, gain_ref, bias_ref, normed):
    for j, x_ref in enumerate(x_refs):
        x = x_ref[0:ROWS, :].astype(F32)
        centered = x - jnp.mean(x, -1, keepdims=True)
        inv = lax.rsqrt(jnp.mean(centered * centered, -1, keepdims=True) + EPS)
        normed[rows_of(j), :] = (centered * inv * gain_ref[...] + bias_ref[...]).astype(BF)


def forward_in(g, normed, wi, bin_ref, cos_ref, sin_ref, mask_ref, qkv, probs, oa, pre):
    y = mm(normed[...], wi[g, :, 0 : 3 * PAIR])
    cosine, sine = cos_ref[...], sin_ref[...]
    qkv[g, :, 0:PAIR] = turned(y[:, 0:PAIR], cosine, sine).astype(BF)
    qkv[g, :, PAIR : 2 * PAIR] = turned(y[:, PAIR : 2 * PAIR], cosine, sine).astype(BF)
    qkv[g, :, 2 * PAIR : 3 * PAIR] = y[:, 2 * PAIR : 3 * PAIR].astype(BF)
    for j in range(4):
        q = qkv[g, rows_of(j), 0:PAIR]
        k = qkv[g, rows_of(j), PAIR : 2 * PAIR]
        v = qkv[g, rows_of(j), 2 * PAIR : 3 * PAIR]
        s = mm_nt(by_head(q), k) * SCALE
        allowed = mask_ref[j]
        s = jnp.where(jnp.concatenate([allowed, allowed], axis=0) > 0.5, s, NEG)
        e = jnp.exp(s - jnp.max(s, -1, keepdims=True))
        p = e / jnp.sum(e, -1, keepdims=True)
        probs[g, j] = p
        oa[g][rows_of(j), 0:PAIR] = mm(beside(p.astype(BF)), by_head(v)).astype(BF)
    h = mm(normed[...], wi[g, :, 3 * PAIR : CI]) + bin_ref[g : g + 1, :]
    pre[g] = h
    oa[g][:, PAIR:RO] = gelu(h).astype(BF)


def forward_out(oa, wo, outs):
    for n in range(4):
        cols = slice(n * 256, (n + 1) * 256)
        part = mm(oa[0][...], wo[0, :, cols]) + mm(oa[1][...], wo[1, :, cols])
        for j in range(4):
            outs[j][:, cols] = part[j * ROWS : (j + 1) * ROWS].astype(outs[j].dtype)


def backward_out(g, gout, wo, qkv, probs, pre, cos_ref, sin_ref, gcat, gbin_ref):
    go = mm_nt(gout[...], wo[g, 0:PAIR, :]).astype(BF)
    for j in range(4):
        q = qkv[g, rows_of(j), 0:PAIR]
        k = qkv[g, rows_of(j), PAIR : 2 * PAIR]
        v = qkv[g, rows_of(j), 2 * PAIR : 3 * PAIR]
        cosine, sine = cos_ref[rows_of(j), :], sin_ref[rows_of(j), :]
        go2 = by_head(go[j * ROWS : (j + 1) * ROWS])
        p = probs[g, j]
        gp = mm_nt(go2, v)
        gs = (p * (gp - jnp.sum(gp * p, -1, keepdims=True))).astype(BF)
        gv = mm_tn(p.astype(BF), go2)
        gq = mm(beside(gs), by_head(k)) * SCALE
        gk = mm_tn(gs, by_head(q)) * SCALE
        gcat[g][rows_of(j), 0:PAIR] = turned(gq, cosine, -sine).astype(BF)
        gcat[g][rows_of(j), PAIR : 2 * PAIR] = turned(gk, cosine, -sine).astype(BF)
        gcat[g][rows_of(j), 2 * PAIR : 3 * PAIR] = gv.astype(BF)
    ga = mm_nt(gout[...], wo[g, PAIR:RO, :])
    gpre = (ga * gelu_slope(pre[g])).astype(BF)
    gcat[g][:, 3 * PAIR : CI] = gpre
    gbin_ref[g : g + 1, :] = jnp.sum(gpre.astype(F32), 0, keepdims=True)


def backward_in(gcat, wi, outs):
    for n in range(4):
        cols = slice(n * 256, (n + 1) * 256)
        part = mm_nt(gcat[0][...], wi[0, cols, :]) + mm_nt(gcat[1][...], wi[1, cols, :])
        for j in range(4):
            outs[j][:, cols] = part[j * ROWS : (j + 1) * ROWS].astype(outs[j].dtype)


A_COLS = D + 2 * RO
B_COLS = CI + 512


def views_a(ship_a):
    return ship_a.at[:, 0:D], (ship_a.at[:, D : D + RO], ship_a.at[:, D + RO : D + 2 * RO])


def views_b(ship_b):
    return ship_b.at[:, 0:CI], ship_b.at[:, CI : CI + 512]


def input_copies(fast, refs, wi, sems):
    if not fast:
        return [pltpu.make_async_copy(refs[0], wi, sems.at[0])]
    return [pltpu.make_async_copy(refs[slot], wi.at[slot], sems.at[slot]) for slot in range(2)]


def output_copies(fast, refs, wo, sems):
    if not fast:
        return [pltpu.make_async_copy(refs[0], wo, sems.at[0])]
    core = lax.axis_index("section")
    copies = []
    for own in range(2):
        half = core if own == 0 else 1 - core
        cols = pl.ds(pl.multiple_of(512 * half, 512), 512)
        for g in range(2):
            slot = jnp.bitwise_xor(core, g)
            copies.append(
                pltpu.make_async_copy(refs[own].at[g], wo.at[slot, :, cols], sems.at[len(copies)])
            )
    return copies


def place_of():
    return lax.axis_index("dp"), lax.axis_index("section")


def other_half(fast, gout, half_ref):
    core = lax.axis_index("section") if fast else 0
    half_ref[...] = gout[:, pl.ds(pl.multiple_of(512 * (1 - core), 512), 512)]


def join_in_kernel(*refs):
    near_own, near_far_a, near_far_b, own, far_a, far_b = refs[:6]
    joined, sems = refs[6:]
    me, _ = place_of()
    copies = []
    for flip, pieces in ((0, own), (8, (far_a, far_b)), (1, near_own), (9, (near_far_a, near_far_b))):
        for j in range(4):
            piece = pieces[j // 2].at[j % 2] if isinstance(pieces, tuple) else pieces.at[j]
            start = pl.multiple_of(jnp.bitwise_xor(me, flip ^ (2 * j)) * 64, 64)
            copies.append(pltpu.make_async_copy(piece, joined.at[pl.ds(start, 64), :], sems.at[len(copies)]))
            copies[-1].start()
    for copy in copies:
        copy.wait()


def join_out_kernel(own, far, near_own, near_far, joined, sems):
    me, _ = place_of()
    copies = []
    for flip, piece in ((0, own), (8, far), (1, near_own), (9, near_far)):
        source = jnp.bitwise_xor(me, flip)
        g, r = source // 8, source % 2
        first, second = pl.multiple_of(64 * r, 64), pl.multiple_of(PAIR + 256 * r, 128)
        for rows, target in ((slice(0, 64), pl.ds(first, 64)), (slice(64, 320), pl.ds(second, 256))):
            copies.append(pltpu.make_async_copy(piece.at[rows], joined.at[g, target], sems.at[len(copies)]))
            copies[-1].start()
    for copy in copies:
        copy.wait()


def first_forward_kernel(fast, n, *refs):
    x_refs, refs = refs[:4], refs[4:]
    (gain, bias, bin_ref, cos_ref, sin_ref, mask_ref), refs = refs[:6], refs[6:]
    wi_refs, wo_refs, refs = refs[:n], refs[n : 2 * n], refs[2 * n :]
    outs, refs = refs[:4], refs[4:]
    ship_a, qkv, probs, pre, wi, wo, sem_i, sem_o = refs
    normed, oa = views_a(ship_a)
    loads_i, loads_o = input_copies(fast, wi_refs, wi, sem_i), output_copies(fast, wo_refs, wo, sem_o)
    for copy in loads_i + loads_o:
        copy.start()
    layer_norm_into(x_refs, gain, bias, normed)
    for copy in loads_i:
        copy.wait()
    for g in range(2):
        forward_in(g, normed, wi, bin_ref, cos_ref, sin_ref, mask_ref, qkv, probs, oa, pre)
    for copy in loads_o:
        copy.wait()
    forward_out(oa, wo, outs)


def second_layer_kernel(fast, n, *refs):
    x_refs, gout_refs, refs = refs[:4], refs[4:8], refs[8:]
    (gain, bias, bin_ref, cos_ref, sin_ref, mask_ref), refs = refs[:6], refs[6:]
    wi_refs, wo_refs, refs = refs[:n], refs[n : 2 * n], refs[2 * n :]
    outs, gouts, refs = refs[:4], refs[4:8], refs[8:]
    ship_a, ship_b, gcat0, gbin_ref, qkv, probs, pre, gout, wi, wo, sem_i, sem_o = refs
    normed, oa = views_a(ship_a)
    gcat1, gout_half = views_b(ship_b)
    gcat = (gcat0, gcat1)
    loads_i, loads_o = input_copies(fast, wi_refs, wi, sem_i), output_copies(fast, wo_refs, wo, sem_o)
    for copy in loads_i + loads_o:
        copy.start()
    layer_norm_into(x_refs, gain, bias, normed)
    for j in range(4):
        gout[rows_of(j), :] = gout_refs[j][...]
    other_half(fast, gout, gout_half)
    for copy in loads_i:
        copy.wait()
    for g in range(2):
        forward_in(g, normed, wi, bin_ref, cos_ref, sin_ref, mask_ref, qkv, probs, oa, pre)
    for copy in loads_o:
        copy.wait()
    for g in range(2):
        backward_out(g, gout, wo, qkv, probs, pre, cos_ref, sin_ref, gcat, gbin_ref)
    backward_in(gcat, wi, gouts)
    forward_out(oa, wo, outs)


def first_backward_kernel(fast, n, *refs):
    gout_refs, refs = refs[:4], refs[4:]
    (cos_ref, sin_ref, qkv, probs, pre), refs = refs[:5], refs[5:]
    wi_refs, wo_refs, refs = refs[:n], refs[n : 2 * n], refs[2 * n :]
    gouts, refs = refs[:4], refs[4:]
    ship_b, gcat0, gbin_ref, gout, wi, wo, sem_i, sem_o = refs
    gcat1, gout_half = views_b(ship_b)
    gcat = (gcat0, gcat1)
    loads_i, loads_o = input_copies(fast, wi_refs, wi, sem_i), output_copies(fast, wo_refs, wo, sem_o)
    for copy in loads_o + loads_i:
        copy.start()
    for j in range(4):
        gout[rows_of(j), :] = gout_refs[j][...]
    other_half(fast, gout, gout_half)
    for copy in loads_o:
        copy.wait()
    for g in range(2):
        backward_out(g, gout, wo, qkv, probs, pre, cos_ref, sin_ref, gcat, gbin_ref)
    for copy in loads_i:
        copy.wait()
    backward_in(gcat, wi, gouts)


def weight_grad_out_kernel(*refs):
    gout_refs, (ship_a, other_a, other_b, keep, send, left, right) = refs[:4], refs[4:]
    me, core = place_of()
    cols = pl.ds(pl.multiple_of(512 * core, 512), 512)
    for j in range(4):
        right[rows_of(j), :] = gout_refs[j][:, cols]
    right[TOK : 2 * TOK, :] = other_b[:, CI : CI + 512]
    for side, ship in enumerate((ship_a, other_a)):
        tokens = slice(side * TOK, (side + 1) * TOK)
        for part in range(2):
            far = jnp.bitwise_xor(me // 8, jnp.bitwise_xor(core, part ^ side))
            flat = ship[:, D + part * RO : D + (part + 1) * RO].T
            for r in range(2):
                near = jnp.bitwise_xor(me % 2, r)
                left[near, far, 0:64, tokens] = flat[64 * r : 64 * r + 64]
                left[near, far, 64:320, tokens] = flat[PAIR + 256 * r : PAIR + 256 * (r + 1)]
    for near, out in ((1, send), (0, keep)):
        for far in range(2):
            out[far] = mm(left[near, far], right[...]).astype(BF)


def weight_grad_in_kernel(ship_a, other_a, gcat, other_b, keep_a, keep_b, send_a, send_b, left, right):
    me, _ = place_of()
    g, t, r = me // 8, (me // 2) % 4, me % 2
    right[0:TOK, :] = gcat[...]
    right[TOK : 2 * TOK, :] = other_b[:, 0:CI]
    for side, ship in enumerate((ship_a, other_a)):
        tokens = slice(side * TOK, (side + 1) * TOK)
        for far in range(2):
            for j in range(4):
                pair = jnp.bitwise_xor(g, far) * 4 + jnp.bitwise_xor(t, j)
                block = ship[:, pl.ds(pl.multiple_of(pair * PAIR, PAIR), PAIR)].T
                for s in range(2):
                    near = jnp.bitwise_xor(r, s)
                    start = (far * 2 + j % 2) * 64
                    left[near, j // 2, start : start + 64, tokens] = block[64 * s : 64 * s + 64]
    for near, half, out in ((1, 0, send_a), (1, 1, send_b), (0, 0, keep_a), (0, 1, keep_b)):
        part = mm(left[near, half], right[...]).astype(BF)
        for i in range(4):
            out[i // 2, i % 2] = part[64 * i : 64 * i + 64]


def whole_grad_out_kernel(*refs):
    gout_refs, (ship_a, out, gout) = refs[:4], refs[4:]
    for j in range(4):
        gout[rows_of(j), :] = gout_refs[j][...]
    for g in range(2):
        out[g] = mm_tn(ship_a[:, D + g * RO : D + (g + 1) * RO], gout[...]).astype(BF)


def whole_grad_in_kernel(ship_a, gcat0, ship_b, out):
    for g in range(2):
        right = gcat0[...] if g == 0 else ship_b[:, 0:CI]
        for m in range(4):
            rows = slice(m * 256, (m + 1) * 256)
            out[g, rows, :] = mm_tn(ship_a[:, rows], right).astype(BF)


def norm_backward_kernel(own, r1, r2, r3, x_ref, gout_ref, gain, gx_ref, low_ref, sums_ref):
    x = x_ref[0:ROWS, :].astype(F32)
    gn = own[...] + r1[...].astype(F32) + r2[...].astype(F32) + r3[...].astype(F32)
    gout = gout_ref[...].astype(F32)
    centered = x - jnp.mean(x, -1, keepdims=True)
    inv = lax.rsqrt(jnp.mean(centered * centered, -1, keepdims=True) + EPS)
    unit = centered * inv
    gu = gn * gain[...]
    gx = gout + inv * (gu - jnp.mean(gu, -1, keepdims=True) - unit * jnp.mean(gu * unit, -1, keepdims=True))
    gx_ref[...] = gx
    low_ref[...] = gx.astype(BF)
    sums_ref[0:1, :] = jnp.sum(gn * unit, 0, keepdims=True)
    sums_ref[1:2, :] = jnp.sum(gn, 0, keepdims=True)
    sums_ref[2:3, :] = jnp.sum(gout, 0, keepdims=True)


def pack_kernel(w_qkv, w_out, w_in, w_fc, wi_keep, wi_send, wo_keep, wo_send):
    t, core = (lax.axis_index("dp") // 2) % 4, lax.axis_index("section")
    for ref, g in ((wi_keep, core), (wi_send, 1 - core)):
        for j in range(4):
            rank = jnp.bitwise_xor(t, j)
            for part in range(3):
                start = pl.multiple_of(part * D + g * 512 + rank * PAIR, PAIR)
                ref[j, :, part * PAIR : (part + 1) * PAIR] = w_qkv[:, pl.ds(start, PAIR)].astype(BF)
            start = pl.multiple_of(g * 2048 + rank * FB, FB)
            ref[j, :, 3 * PAIR : CI] = w_in[:, pl.ds(start, FB)].astype(BF)
    for ref, half in ((wo_keep, core), (wo_send, 1 - core)):
        cols = pl.ds(pl.multiple_of(512 * half, 512), 512)
        ref[0:64, :] = w_out[:, cols].astype(BF)
        ref[64:320, :] = w_fc[:, cols].astype(BF)


def unpack_kernel(own0, own1, own2, own3, other, wo_own, wo_other, g_qkv, g_out, g_in, g_fc):
    t, core = (lax.axis_index("dp") // 2) % 4, lax.axis_index("section")
    for side, g in ((0, core), (1, 1 - core)):
        for j in range(4):
            block = (own0, own1, own2, own3)[j][...] if side == 0 else other[j]
            block = block.astype(F32)
            rank = jnp.bitwise_xor(t, j)
            for part in range(3):
                start = pl.multiple_of(part * D + g * 512 + rank * PAIR, PAIR)
                g_qkv[:, pl.ds(start, PAIR)] = block[:, part * PAIR : (part + 1) * PAIR]
            start = pl.multiple_of(g * 2048 + rank * FB, FB)
            g_in[:, pl.ds(start, FB)] = block[:, 3 * PAIR : CI]
    for ref, half in ((wo_own, core), (wo_other, 1 - core)):
        cols = pl.ds(pl.multiple_of(512 * half, 512), 512)
        g_out[:, cols] = ref[0:64, :].astype(F32)
        g_fc[:, cols] = ref[64:320, :].astype(F32)


VM = pl.BlockSpec(memory_space=pltpu.VMEM)
HB = pl.BlockSpec(memory_space=pl.ANY)


def kernel_call(kernel, args, outs, any_args=0, any_outs=False, scratch=(), flops=1e6, name=None):
    sizes = [a.size * a.dtype.itemsize for a in args] + [a.size * a.dtype.itemsize for a in outs]
    return pl.pallas_call(
        kernel,
        out_shape=outs,
        in_specs=[VM] * (len(args) - any_args) + [HB] * any_args,
        out_specs=[HB if any_outs else VM] * len(outs),
        scratch_shapes=list(scratch),
        compiler_params=pltpu.CompilerParams(vmem_limit_bytes=VMEM_LIMIT),
        cost_estimate=pl.CostEstimate(flops=int(flops), bytes_accessed=int(sum(sizes)), transcendentals=0),
        name=name,
    )(*args)


def arr(shape, dtype):
    return jax.ShapeDtypeStruct(shape, dtype)


def weight_scratch(fast):
    return [
        pltpu.VMEM((2, D, CI), BF),
        pltpu.VMEM((2, RO, D), BF),
        pltpu.SemaphoreType.DMA((2 if fast else 1,)),
        pltpu.SemaphoreType.DMA((4 if fast else 1,)),
    ]


def partial_outs():
    return [arr((ROWS, D), F32)] + [arr((ROWS, D), BF)] * 3


def swap_core(value):
    return lax.ppermute(value, "section", [(0, 1), (1, 0)])


def flipped(value, flip):
    count = lax.axis_size("dp")
    return lax.ppermute(value, "dp", [(i, i ^ flip) for i in range(count)])


def after(value, *earlier):
    return lax.optimization_barrier((value, earlier))[0]


def choose(own, other):
    first_core = lax.axis_index("section") == 0
    return jnp.where(first_core, own, other), jnp.where(first_core, other, own)


def across(values):
    spread = lax.axis_size("dp") // 8
    return [flipped(v, (j + 1) * spread) for j, v in enumerate(values)]


def groups_of(spread):
    places = [[[g * 4 * spread + t * spread + r for r in range(spread)] for t in range(4)] for g in range(2)]
    t_groups = [[places[g][t][r] for t in range(4)] for g in range(2) for r in range(spread)]
    f_groups = [[places[g][t][r] for g in range(2) for r in range(spread)] for t in range(4)]
    return t_groups, f_groups


def any_gather(w_qkv, w_out, w_in, w_fc):
    share, spread = w_qkv.shape[0], lax.axis_size("dp") // 8
    t_groups, f_groups = groups_of(spread)
    qkv = w_qkv.reshape(share, 3, 2, 4, PAIR).transpose(3, 0, 2, 1, 4).reshape(4, share, 2, 3 * PAIR)
    wi = jnp.concatenate([qkv, w_in.reshape(share, 2, 4, FB).transpose(2, 0, 1, 3)], axis=-1).astype(BF)
    wi = lax.all_to_all(wi, "dp", 0, 0, axis_index_groups=t_groups, tiled=True)
    wi = lax.all_gather(wi, "dp", axis_index_groups=f_groups)
    wi = wi.reshape(2, spread, 4, share, 2, CI).transpose(4, 0, 2, 1, 3, 5).reshape(2, D, CI)
    wo = lax.all_gather(w_out.astype(BF), "dp", axis_index_groups=f_groups).reshape(2, PAIR, D)
    wf = lax.all_gather(w_fc.astype(BF), "dp", axis_index_groups=f_groups).reshape(2, FB, D)
    wo = jnp.concatenate([wo, wf], axis=1)
    return choose(wi, swap_core(wi)), choose(wo, swap_core(wo))


def any_reduce(gi, go):
    count = lax.axis_size("dp")
    spread, share = count // 8, D // count
    t_groups, f_groups = groups_of(spread)

    def scattered(value):
        return lax.psum_scatter(value, "dp", scatter_dimension=0, axis_index_groups=f_groups)

    gi = gi.reshape(2, 2, 4, spread, share, CI).transpose(1, 3, 2, 4, 0, 5).reshape(2 * spread, 4, share, 2, CI)
    gi = lax.all_to_all(scattered(gi), "dp", 0, 0, axis_index_groups=t_groups, tiled=True)
    g_qkv = gi[..., : 3 * PAIR].reshape(4, share, 2, 3, PAIR).transpose(1, 3, 2, 0, 4).reshape(share, 3 * D)
    g_in = gi[..., 3 * PAIR :].transpose(1, 2, 0, 3).reshape(share, 4 * D)
    g_out = scattered(go[:, :PAIR].reshape(2 * spread, share, D))
    g_fc = scattered(go[:, PAIR:].reshape(2 * spread, 4 * share, D))
    return g_qkv, g_out, g_in, g_fc


def body(boundary, segments, ln_gain, ln_bias, w_qkv, w_out, w_in, b_in, w_fc, b_fc):
    core, me = lax.axis_index("section"), lax.axis_index("dp")
    count = lax.axis_size("dp")
    fast = count == 16
    spread = count // 8
    rank = (me // spread) % 4
    share = D // count
    width_small = 7 * share
    first_core = core == 0

    if fast:
        wi_keep, wi_send, wo_keep, wo_send = kernel_call(
            pack_kernel,
            [w_qkv[0], w_out[0], w_in[0], w_fc[0]],
            [arr((4, 64, CI), BF), arr((4, 64, CI), BF), arr((320, 512), BF), arr((320, 512), BF)],
            name="pack",
        )
        wi_recv, wo_recv = swap_core(wi_send), swap_core(wo_send)
        wi_first = [choose(wi_keep[j], wi_recv[j]) for j in range(4)]
        wo_first = choose(wo_keep, wo_recv)
        boundary, ln_gain = after((boundary, ln_gain), wi_keep)
    else:
        wi_both, wo_both = any_gather(w_qkv[0], w_out[0], w_in[0], w_fc[0])

    swapped = swap_core(lax.dynamic_index_in_dim(boundary[0], 1 - core, 0, False)[0])
    kept = lax.dynamic_index_in_dim(boundary[0], core, 0, False)[0]
    x0, g1 = choose(kept, swapped)
    small = jnp.concatenate([ln_gain, ln_bias, b_fc, b_in], axis=-1).astype(BF)
    small = jnp.concatenate(choose(small, swap_core(small)))
    seg = lax.dynamic_index_in_dim(segments, core, 0, False)[0].astype(BF)
    extra = jnp.zeros((16, D), BF).at[0, :ROWS].set(seg)
    if fast:
        extra = extra.at[1:3, :width_small].set(small)
    pack = jnp.concatenate([x0, extra])

    if fast:

        def join(wi_pieces, wo_pieces, name):
            wo = kernel_call(
                join_out_kernel,
                wo_pieces,
                [arr((2, RO, 512), BF)],
                any_args=4,
                any_outs=True,
                scratch=[pltpu.SemaphoreType.DMA((8,))],
                name=name + "_out",
            )[0]
            wi = kernel_call(
                join_in_kernel,
                wi_pieces,
                [arr((D, CI), BF)],
                any_args=6,
                any_outs=True,
                scratch=[pltpu.SemaphoreType.DMA((16,))],
                name=name + "_in",
            )[0]
            return [wi, swap_core(wi)], [wo, swap_core(wo)]

        mine = [w[0] for w in wi_first]
        arrived = across(mine[1:])
        wo_own = wo_first[0]
        wo_far = flipped(wo_own, 8)
        wo_near = flipped(wo_own, 1)
        wi_own = jnp.stack([mine[0]] + arrived)
        a_far = flipped(wi_own[0:2], 8)
        wi_near = flipped(wi_own, 1)
        b_far = flipped(after(wi_own[2:4], a_far), 8)
        wo_near_far = flipped(after(wo_far, wo_near), 1)
        a_near = flipped(after(a_far, wi_near), 1)
        b_near = flipped(b_far, 1)
        wi0, wo0 = join([wi_near, a_near, b_near, wi_own, a_far, b_far], [wo_own, wo_far, wo_near, wo_near_far], "join0")
        packs = [pack] + across(after([pack] * 3, arrived))
        mine = [w[1] for w in wi_first]
        arrived = across(after(mine[1:], packs[1:]))
        wo_own = wo_first[1]
        wi_own = jnp.stack([mine[0]] + arrived)
        wo_far, a_far = flipped(after(wo_own, b_far), 8), flipped(after(wi_own[0:2], b_far), 8)
        wo_near = flipped(after(wo_own, b_near), 1)
        wi_near = flipped(after(wi_own, b_near), 1)
        b_far = flipped(after(wi_own[2:4], wo_far), 8)
        wo_near_far = flipped(after(wo_far, wo_near), 1)
        a_near = flipped(after(a_far, wi_near), 1)
        b_near = flipped(b_far, 1)
        wi1, wo1 = join([wi_near, a_near, b_near, wi_own, a_far, b_far], [wo_own, wo_far, wo_near, wo_near_far], "join1")
        g1s = [g1] + across(after([g1] * 3, wi0[0]))

        held = jnp.stack([p[129:131, :width_small] for p in packs])
        held = jnp.concatenate([held, flipped(held, 8)])
        held = jnp.concatenate([held, flipped(held, 1)]).reshape(16, 2 * width_small)
        index = jnp.arange(16)
        flip_of = jnp.bitwise_xor(index, me)
        at = (flip_of % 2) * 8 + (flip_of // 8) * 4 + (flip_of // 2) % 4
        onehot = (at[:, None] == index[None, :]).astype(BF)
        everyone = mm(onehot, held).reshape(16, 2, width_small)
    else:
        wi0, wi1 = [wi_both[0]], [wi_both[1]]
        wo0, wo1 = [wo_both[0]], [wo_both[1]]
        packs, g1s = [pack] + across([pack] * 3), [g1] + across([g1] * 3)
        everyone = lax.all_gather(small, "dp").astype(F32)
    n = len(wi0)

    def parts_in_place(value):
        return jnp.where(first_core, value, value[::-1]) if fast else value

    def small_of(layer):
        one = everyone[:, layer]
        vectors = [one[:, i * share : (i + 1) * share].reshape(1, D) for i in range(3)]
        b = one[:, 3 * share :].reshape(2, 4, FB)
        return *vectors, parts_in_place(lax.dynamic_index_in_dim(b, rank, 1, False))

    gain0, bias0, bfc0, bin0 = small_of(0)
    gain1, bias1, bfc1, bin1 = small_of(1)

    segs = jnp.stack([p[ROWS, :ROWS] for p in packs])
    row = lax.broadcasted_iota(jnp.int32, (ROWS, ROWS), 0)
    col = lax.broadcasted_iota(jnp.int32, (ROWS, ROWS), 1)
    mask = ((segs[:, :, None] == segs[:, None, :]) & (col <= row)).astype(F32)
    positions = jnp.sum(mask, -1).reshape(TOK, 1) - 1.0
    lane = jnp.arange(PAIR) % 64
    freq = jnp.where(lane < 32, 10000.0 ** (-(lane // 2 * 2).astype(F32) / 32), 0.0)
    angle = positions * freq
    cosine = jnp.cos(angle)
    sine = jnp.sin(angle) * jnp.where(lane % 2 == 0, -1.0, 1.0)

    layer_flops = 2 * TOK * 2 * (D * CI + RO * D)
    saved = [
        arr((TOK, A_COLS), BF),
        arr((2, TOK, 3 * PAIR), BF),
        arr((2, 4, 2 * ROWS, ROWS), F32),
        arr((2, TOK, FB), F32),
    ]
    got = kernel_call(
        functools.partial(first_forward_kernel, fast, n),
        [*packs, gain0, bias0, bin0, cosine, sine, mask, *wi0, *wo0],
        partial_outs() + saved,
        any_args=2 * n,
        scratch=weight_scratch(fast),
        flops=layer_flops,
        name="first_forward",
    )
    own, sends, (ship_a0, qkv0, probs0, pre0) = got[0], got[1:4], got[4:]

    def total(own, sends):
        return sum([r.astype(F32) for r in across(sends)], own)

    x1 = (x0.astype(F32) + total(own, sends) + bfc0).astype(BF)
    x1s = [x1] + across([x1] * 3)

    back_outs = [arr((TOK, B_COLS), BF), arr((TOK, CI), BF), arr((2, FB), F32)]
    got = kernel_call(
        functools.partial(second_layer_kernel, fast, n),
        [*x1s, *g1s, gain1, bias1, bin1, cosine, sine, mask, *wi1, *wo1],
        partial_outs()
        + partial_outs()
        + [arr((TOK, A_COLS), BF)]
        + back_outs,
        any_args=2 * n,
        scratch=[
            pltpu.VMEM((2, TOK, 3 * PAIR), BF),
            pltpu.VMEM((2, 4, 2 * ROWS, ROWS), F32),
            pltpu.VMEM((2, TOK, FB), F32),
            pltpu.VMEM((TOK, D), BF),
        ]
        + weight_scratch(fast),
        flops=2 * layer_flops,
        name="second_layer",
    )
    out_own, out_sends, gn_own, gn_sends = got[0], got[1:4], got[4], got[5:8]
    ship_a1, ship_b1, gcat1, gbin1 = got[8:]

    def norm_backward(own, arrived, x, gout, gain, name):
        return kernel_call(
            norm_backward_kernel,
            [own, *arrived, x, gout, gain],
            [arr((ROWS, D), F32), arr((ROWS, D), BF), arr((3, D), F32)],
            name=name,
        )

    def weight_grads(gouts, ship_a, ship_b, gcat, name):
        grad_flops = 2 * TOK * 2 * (CI + RO) * D // 2
        if fast:
            other_a, other_b = swap_core(ship_a), swap_core(ship_b)
            go = kernel_call(
                weight_grad_out_kernel,
                [*gouts, ship_a, other_a, other_b],
                [arr((2, 320, 512), BF)] * 2,
                scratch=[pltpu.VMEM((2, 2, 320, 2 * TOK), BF), pltpu.VMEM((2 * TOK, 512), BF)],
                flops=grad_flops,
                name=name + "_out",
            )
            gi = kernel_call(
                weight_grad_in_kernel,
                [ship_a, other_a, gcat, other_b],
                [arr((2, 2, 64, CI), BF)] * 4,
                scratch=[pltpu.VMEM((2, 2, 256, 2 * TOK), BF), pltpu.VMEM((2 * TOK, CI), BF)],
                flops=grad_flops,
                name=name + "_in",
            )
            return go, gi
        go = kernel_call(
            whole_grad_out_kernel,
            [*gouts, ship_a],
            [arr((2, RO, D), BF)],
            scratch=[pltpu.VMEM((TOK, D), BF)],
            flops=grad_flops,
            name=name + "_out",
        )
        gi = kernel_call(
            whole_grad_in_kernel, [ship_a, gcat, ship_b], [arr((2, D, CI), BF)], flops=grad_flops, name=name + "_in"
        )
        return go, gi

    grads1 = weight_grads(g1s, ship_a1, ship_b1, gcat1, "grads1")
    _, g0, sums1 = norm_backward(after(gn_own, grads1), across(gn_sends), x1, g1, gain1, "norm_backward1")
    g0s = [g0] + across([g0] * 3)
    out1 = x1.astype(F32) + total(out_own, after(out_sends, g0s[1:])) + bfc1

    got = kernel_call(
        functools.partial(first_backward_kernel, fast, n),
        [*g0s, cosine, sine, qkv0, probs0, pre0, *wi0, *wo0],
        partial_outs() + back_outs,
        any_args=2 * n,
        scratch=[pltpu.VMEM((TOK, D), BF)] + weight_scratch(fast),
        flops=layer_flops,
        name="first_backward",
    )
    gn_own, gn_sends, (ship_b0, gcat0, gbin0) = got[0], got[1:4], got[4:]
    grads0 = weight_grads(g0s, ship_a0, ship_b0, gcat0, "grads0")
    gx0, _, sums0 = norm_backward(gn_own, across(gn_sends), x0, g0, gain0, "norm_backward0")

    arrived = swap_core(jnp.where(first_core, out1, gx0))
    boundary_out = jnp.where(first_core, jnp.stack([gx0, arrived]), jnp.stack([arrived, out1]))[None, :, None]

    def small_grads(sums, gbin):
        vectors = sums.reshape(3, count, share).transpose(1, 0, 2).reshape(count, 3 * share)
        onehot = (jnp.arange(4) == rank).astype(F32)
        b = parts_in_place(gbin).reshape(2, 1, spread, 4 * share) * onehot[None, :, None, None]
        return jnp.concatenate([vectors, b.reshape(count, 4 * share)], axis=1)

    both = choose(small_grads(sums0, gbin0), small_grads(sums1, gbin1))
    vector = both[0] + swap_core(both[1])
    if fast:
        for flip in (2, 4, 1, 8):
            vector = vector + flipped(vector, flip)
        vector = lax.dynamic_index_in_dim(vector, me, 0, True)
    else:
        vector = lax.psum_scatter(vector, "dp", scatter_dimension=0, tiled=True)
    g_gain, g_bias, g_bfc = (vector[:, i * share : (i + 1) * share] for i in range(3))
    g_bin = vector[:, 3 * share :]

    if fast:

        def reduce_over_f(keep, send):
            near = flipped(send, 1)
            onward = flipped((keep[1].astype(F32) + near[1].astype(F32)).astype(BF), 8)
            return (keep[0].astype(F32) + near[0].astype(F32) + onward.astype(F32)).astype(BF)

        def reduced(grads):
            (wo_keep, wo_send), (keep_a, keep_b, send_a, send_b) = grads
            wo = reduce_over_f(wo_keep, wo_send)
            a, b = reduce_over_f(keep_a, send_a), reduce_over_f(keep_b, send_b)
            return wo, [a[0]] + across([a[1], b[0], b[1]])

        (wo_1, wi_1), (wo_0, wi_0) = reduced(grads1), reduced(grads0)
        wo_mine, wo_theirs = choose(wo_0, wo_1)
        pairs = [choose(a, b) for a, b in zip(wi_0, wi_1)]
        wi_other = swap_core(jnp.stack([p[1] for p in pairs]))
        g_qkv, g_out, g_in, g_fc = kernel_call(
            unpack_kernel,
            [*[p[0] for p in pairs], wi_other, wo_mine, swap_core(wo_theirs)],
            [arr((64, 3 * D), F32), arr((64, D), F32), arr((64, 4 * D), F32), arr((256, D), F32)],
            name="unpack",
        )
    else:
        (go1,), (gi1,) = grads1
        (go0,), (gi0,) = grads0
        mine, theirs = choose(gi0, gi1)
        gi = mine.astype(F32) + swap_core(theirs).astype(F32)
        mine, theirs = choose(go0, go1)
        go = mine.astype(F32) + swap_core(theirs).astype(F32)
        g_qkv, g_out, g_in, g_fc = any_reduce(gi, go)

    return (boundary_out, g_gain, g_bias, g_qkv[None], g_out[None], g_in[None], g_bin, g_fc[None], g_bfc)


def solution(mesh):
    rows = P("section", None, "dp", None, None)
    vector, matrix = P("section", "dp"), P("section", "dp", None)
    return jax.shard_map(
        body,
        mesh=mesh,
        in_specs=(rows, P(None, "dp", None), vector, vector, matrix, matrix, matrix, vector, matrix, vector),
        out_specs=(rows, vector, vector, matrix, matrix, matrix, vector, matrix, vector),
        check_vma=False,
    )
```

```python
import functools

import jax
import jax.numpy as jnp
from jax import lax
from jax.experimental import pallas as pl
from jax.experimental.pallas import tpu as pltpu
from jax.sharding import PartitionSpec as P

D = 1024
PAIR = 128
FB = 512
CI = 3 * PAIR + FB
RO = PAIR + FB
EPS = 1e-05
NEG = -1000000000.0
SCALE = 0.125
ROWS = 128
TOK = 4 * ROWS
BF = jnp.bfloat16
F32 = jnp.float32
VMEM_LIMIT = 56 * 1024 * 1024


def mm(a, b):
    return lax.dot_general(a, b, (((1,), (0,)), ((), ())), preferred_element_type=F32)


def mm_nt(a, b):
    return lax.dot_general(a, b, (((1,), (1,)), ((), ())), preferred_element_type=F32)


def mm_tn(a, b):
    return lax.dot_general(a, b, (((0,), (0,)), ((), ())), preferred_element_type=F32)


def gelu(h):
    return 0.5 * h * (1.0 + jnp.tanh(0.7978845608 * (h + 0.044715 * h * h * h)))


def gelu_slope(h):
    th = jnp.tanh(0.7978845608 * (h + 0.044715 * h * h * h))
    inner = 0.7978845608 * (1.0 + 3 * 0.044715 * h * h)
    return 0.5 * (1.0 + th) + 0.5 * h * (1.0 - th * th) * inner


def partner(x):
    lane = lax.broadcasted_iota(jnp.int32, x.shape, 1)
    return jnp.where(lane % 2 == 0, pltpu.roll(x, PAIR - 1, 1), pltpu.roll(x, 1, 1))


def turned(x, cosine, sine):
    return x * cosine + partner(x) * sine


def by_head(x):
    lane = lax.broadcasted_iota(jnp.int32, (1, PAIR), 1)
    low = jnp.where(lane < 64, 1.0, 0.0).astype(x.dtype)
    high = jnp.where(lane < 64, 0.0, 1.0).astype(x.dtype)
    return jnp.concatenate([x * low, x * high], axis=0)


def beside(x):
    return jnp.concatenate([x[:ROWS], x[ROWS:]], axis=1)


def rows_of(j):
    return pl.ds(j * ROWS, ROWS)


def layer_norm_into(x_refs, gain_ref, bias_ref, normed):
    for j, x_ref in enumerate(x_refs):
        x = x_ref[0:ROWS, :].astype(F32)
        centered = x - jnp.mean(x, -1, keepdims=True)
        inv = lax.rsqrt(jnp.mean(centered * centered, -1, keepdims=True) + EPS)
        normed[rows_of(j), :] = (centered * inv * gain_ref[...] + bias_ref[...]).astype(BF)


def forward_in(g, normed, wi, bin_ref, cos_ref, sin_ref, mask_ref, qkv, probs, oa, pre):
    y = mm(normed[...], wi[g, :, 0 : 3 * PAIR])
    cosine, sine = cos_ref[...], sin_ref[...]
    qkv[g, :, 0:PAIR] = turned(y[:, 0:PAIR], cosine, sine).astype(BF)
    qkv[g, :, PAIR : 2 * PAIR] = turned(y[:, PAIR : 2 * PAIR], cosine, sine).astype(BF)
    qkv[g, :, 2 * PAIR : 3 * PAIR] = y[:, 2 * PAIR : 3 * PAIR].astype(BF)
    for j in range(4):
        q = qkv[g, rows_of(j), 0:PAIR]
        k = qkv[g, rows_of(j), PAIR : 2 * PAIR]
        v = qkv[g, rows_of(j), 2 * PAIR : 3 * PAIR]
        s = mm_nt(by_head(q), k) * SCALE
        allowed = mask_ref[j]
        s = jnp.where(jnp.concatenate([allowed, allowed], axis=0) > 0.5, s, NEG)
        e = jnp.exp(s - jnp.max(s, -1, keepdims=True))
        p = e / jnp.sum(e, -1, keepdims=True)
        probs[g, j] = p
        oa[g][rows_of(j), 0:PAIR] = mm(beside(p.astype(BF)), by_head(v)).astype(BF)
    h = mm(normed[...], wi[g, :, 3 * PAIR : CI]) + bin_ref[g : g + 1, :]
    pre[g] = h
    oa[g][:, PAIR:RO] = gelu(h).astype(BF)


def forward_out(oa, wo, outs):
    for n in range(4):
        cols = slice(n * 256, (n + 1) * 256)
        part = mm(oa[0][...], wo[0, :, cols]) + mm(oa[1][...], wo[1, :, cols])
        for j in range(4):
            outs[j][0:ROWS, cols] = part[j * ROWS : (j + 1) * ROWS].astype(outs[j].dtype)


def backward_out(g, gout, wo, qkv, probs, pre, cos_ref, sin_ref, gcat, gbin_ref):
    go = mm_nt(gout[...], wo[g, 0:PAIR, :]).astype(BF)
    for j in range(4):
        q = qkv[g, rows_of(j), 0:PAIR]
        k = qkv[g, rows_of(j), PAIR : 2 * PAIR]
        v = qkv[g, rows_of(j), 2 * PAIR : 3 * PAIR]
        cosine, sine = cos_ref[rows_of(j), :], sin_ref[rows_of(j), :]
        go2 = by_head(go[j * ROWS : (j + 1) * ROWS])
        p = probs[g, j]
        gp = mm_nt(go2, v)
        gs = (p * (gp - jnp.sum(gp * p, -1, keepdims=True))).astype(BF)
        gv = mm_tn(p.astype(BF), go2)
        gq = mm(beside(gs), by_head(k)) * SCALE
        gk = mm_tn(gs, by_head(q)) * SCALE
        gcat[g][rows_of(j), 0:PAIR] = turned(gq, cosine, -sine).astype(BF)
        gcat[g][rows_of(j), PAIR : 2 * PAIR] = turned(gk, cosine, -sine).astype(BF)
        gcat[g][rows_of(j), 2 * PAIR : 3 * PAIR] = gv.astype(BF)
    ga = mm_nt(gout[...], wo[g, PAIR:RO, :])
    gpre = (ga * gelu_slope(pre[g])).astype(BF)
    gcat[g][:, 3 * PAIR : CI] = gpre
    gbin_ref[g : g + 1, :] = jnp.sum(gpre.astype(F32), 0, keepdims=True)


def backward_in(gcat, wi, outs):
    for n in range(4):
        cols = slice(n * 256, (n + 1) * 256)
        part = mm_nt(gcat[0][...], wi[0, cols, :]) + mm_nt(gcat[1][...], wi[1, cols, :])
        for j in range(4):
            outs[j][0:ROWS, cols] = part[j * ROWS : (j + 1) * ROWS].astype(outs[j].dtype)


A_COLS = D + 2 * RO
B_COLS = CI + 512


def views_a(ship_a):
    return ship_a.at[:, 0:D], (ship_a.at[:, D : D + RO], ship_a.at[:, D + RO : D + 2 * RO])


def views_b(ship_b):
    return ship_b.at[:, 0:CI], ship_b.at[:, CI : CI + 512]


def input_copies(fast, refs, wi, sems):
    if not fast:
        return [pltpu.make_async_copy(refs[0], wi, sems.at[0])]
    copies = []
    for slot in range(2):
        ref = refs[slot]
        pieces = (
            (ref.at[D : 2 * D, 0 : 3 * PAIR], wi.at[slot, :, 0 : 3 * PAIR]),
            (ref.at[0:D, :], wi.at[slot, :, 3 * PAIR : CI]),
        )
        copies += [pltpu.make_async_copy(*p, sems.at[2 * slot + i]) for i, p in enumerate(pieces)]
    return copies


def output_copies(fast, refs, wo, sems):
    if not fast:
        return [pltpu.make_async_copy(refs[1], wo, sems.at[0])]
    core = lax.axis_index("section")
    copies = []
    for own in range(2):
        half = core if own == 0 else 1 - core
        cols = pl.ds(pl.multiple_of(512 * half, 512), 512)
        for g in range(2):
            slot = jnp.bitwise_xor(core, g)
            piece = refs[own].at[2 * D + g * RO : 2 * D + (g + 1) * RO, :]
            copies.append(pltpu.make_async_copy(piece, wo.at[slot, :, cols], sems.at[len(copies)]))
    return copies


def place_of():
    return lax.axis_index("dp"), lax.axis_index("section")


def other_half(fast, gout, half_ref):
    core = lax.axis_index("section") if fast else 0
    half_ref[...] = gout[:, pl.ds(pl.multiple_of(512 * (1 - core), 512), 512)]


def join_kernel(own, far, near_own, near_far, *refs):
    pieces, joined = refs[:-1], refs[-1]
    me, _ = place_of()
    for flip, piece in ((0, own), (8, far), (1, near_own), (9, near_far)):
        source = jnp.bitwise_xor(me, flip)
        g, r = source // 8, source % 2
        base = 2 * D + g * RO
        joined[pl.ds(pl.multiple_of(base + 64 * r, 64), 64), :] = piece[0:64, :]
        joined[pl.ds(pl.multiple_of(base + PAIR + 256 * r, 128), 256), :] = piece[64:320, :]
    blocks = [(ref, i) for ref in pieces for i in range(ref.shape[0])]
    for (ref, i), flip in zip(blocks, [f ^ (2 * j) for f in (0, 8, 1, 9) for j in range(4)]):
        start = pl.multiple_of(jnp.bitwise_xor(me, flip) * 64, 64)
        joined[pl.ds(start, 64), :] = ref[i, :, 3 * PAIR : CI]
        joined[pl.ds(D + start, 64), 0 : 3 * PAIR] = ref[i, :, 0 : 3 * PAIR]


def first_forward_kernel(fast, *refs):
    x_refs, refs = refs[:4], refs[4:]
    (gain, bias, bin_ref, cos_ref, sin_ref, mask_ref), refs = refs[:6], refs[6:]
    w_refs, refs = refs[:2], refs[2:]
    outs, refs = refs[:4], refs[4:]
    ship_a, qkv, probs, pre, wi, wo, sem_i, sem_o = refs
    normed, oa = views_a(ship_a)
    loads_i, loads_o = input_copies(fast, w_refs, wi, sem_i), output_copies(fast, w_refs, wo, sem_o)
    for copy in loads_i + loads_o:
        copy.start()
    layer_norm_into(x_refs, gain, bias, normed)
    for copy in loads_i:
        copy.wait()
    for g in range(2):
        forward_in(g, normed, wi, bin_ref, cos_ref, sin_ref, mask_ref, qkv, probs, oa, pre)
    for copy in loads_o:
        copy.wait()
    forward_out(oa, wo, outs)


def second_layer_kernel(fast, *refs):
    x_refs, gout_refs, refs = refs[:4], refs[4:8], refs[8:]
    (gain, bias, bin_ref, cos_ref, sin_ref, mask_ref), refs = refs[:6], refs[6:]
    w_refs, refs = refs[:2], refs[2:]
    outs, gouts, refs = refs[:4], refs[4:8], refs[8:]
    ship_a, ship_b, gcat0, gbin_ref, qkv, probs, pre, gout, wi, wo, sem_i, sem_o = refs
    normed, oa = views_a(ship_a)
    gcat1, gout_half = views_b(ship_b)
    gcat = (gcat0, gcat1)
    loads_i, loads_o = input_copies(fast, w_refs, wi, sem_i), output_copies(fast, w_refs, wo, sem_o)
    for copy in loads_i + loads_o:
        copy.start()
    layer_norm_into(x_refs, gain, bias, normed)
    for j in range(4):
        gout[rows_of(j), :] = gout_refs[j][0:ROWS, :]
    other_half(fast, gout, gout_half)
    for copy in loads_i:
        copy.wait()
    for g in range(2):
        forward_in(g, normed, wi, bin_ref, cos_ref, sin_ref, mask_ref, qkv, probs, oa, pre)
    for copy in loads_o:
        copy.wait()
    for g in range(2):
        backward_out(g, gout, wo, qkv, probs, pre, cos_ref, sin_ref, gcat, gbin_ref)
    backward_in(gcat, wi, gouts)
    forward_out(oa, wo, outs)


def first_backward_kernel(fast, *refs):
    gout_refs, riders, refs = refs[:4], refs[4:7], refs[7:]
    (cos_ref, sin_ref, qkv, probs, pre), refs = refs[:5], refs[5:]
    w_refs, refs = refs[:2], refs[2:]
    gouts, refs = refs[:4], refs[4:]
    ship_b, gcat0, gbin_ref, gout, wi, wo, sem_i, sem_o = refs
    gcat1, gout_half = views_b(ship_b)
    gcat = (gcat0, gcat1)
    loads_i, loads_o = input_copies(fast, w_refs, wi, sem_i), output_copies(fast, w_refs, wo, sem_o)
    for copy in loads_o + loads_i:
        copy.start()
    for j in range(3):
        gouts[j + 1][ROWS : 2 * ROWS, :] = riders[j][...]
    for j in range(4):
        gout[rows_of(j), :] = gout_refs[j][...]
    other_half(fast, gout, gout_half)
    for copy in loads_o:
        copy.wait()
    for g in range(2):
        backward_out(g, gout, wo, qkv, probs, pre, cos_ref, sin_ref, gcat, gbin_ref)
    for copy in loads_i:
        copy.wait()
    backward_in(gcat, wi, gouts)


def weight_grad_out_kernel(*refs):
    gout_refs, (ship_a, other_a, other_b, *extras, keep, send, left, right) = refs[:4], refs[4:]
    me, core = place_of()
    for extra in extras:
        for near, out in ((1, send), (0, keep)):
            for far in range(2):
                out[far, 320:336, :] = extra[near, far]
    cols = pl.ds(pl.multiple_of(512 * core, 512), 512)
    for j in range(4):
        right[rows_of(j), :] = gout_refs[j][0:ROWS, cols]
    right[TOK : 2 * TOK, :] = other_b[:, CI : CI + 512]
    for side, ship in enumerate((ship_a, other_a)):
        tokens = slice(side * TOK, (side + 1) * TOK)
        for part in range(2):
            far = jnp.bitwise_xor(me // 8, jnp.bitwise_xor(core, part ^ side))
            flat = ship[:, D + part * RO : D + (part + 1) * RO].T
            for r in range(2):
                near = jnp.bitwise_xor(me % 2, r)
                left[near, far, 0:64, tokens] = flat[64 * r : 64 * r + 64]
                left[near, far, 64:320, tokens] = flat[PAIR + 256 * r : PAIR + 256 * (r + 1)]
    for near, out in ((1, send), (0, keep)):
        for far in range(2):
            out[far, 0:320, :] = mm(left[near, far], right[...]).astype(BF)


def weight_grad_in_kernel(ship_a, other_a, gcat, other_b, keep, send, left, right):
    me, _ = place_of()
    g, t, r = me // 8, (me // 2) % 4, me % 2
    right[0:TOK, :] = gcat[...]
    right[TOK : 2 * TOK, :] = other_b[:, 0:CI]
    for side, ship in enumerate((ship_a, other_a)):
        tokens = slice(side * TOK, (side + 1) * TOK)
        for far in range(2):
            for j in range(4):
                pair = jnp.bitwise_xor(g, far) * 4 + jnp.bitwise_xor(t, j)
                block = ship[:, pl.ds(pl.multiple_of(pair * PAIR, PAIR), PAIR)].T
                for s in range(2):
                    near = jnp.bitwise_xor(r, s)
                    left[near, far, 64 * j : 64 * j + 64, tokens] = block[64 * s : 64 * s + 64]
    for near, out in ((1, send), (0, keep)):
        for far in range(2):
            part = mm(left[near, far], right[...]).astype(BF)
            for j in range(4):
                out[far, j] = part[64 * j : 64 * j + 64]


def whole_grad_out_kernel(*refs):
    gout_refs, (ship_a, out, gout) = refs[:4], refs[4:]
    for j in range(4):
        gout[rows_of(j), :] = gout_refs[j][0:ROWS, :]
    for g in range(2):
        out[g] = mm_tn(ship_a[:, D + g * RO : D + (g + 1) * RO], gout[...]).astype(BF)


def whole_grad_in_kernel(ship_a, gcat0, ship_b, out):
    for g in range(2):
        right = gcat0[...] if g == 0 else ship_b[:, 0:CI]
        for m in range(4):
            rows = slice(m * 256, (m + 1) * 256)
            out[g, rows, :] = mm_tn(ship_a[:, rows], right).astype(BF)


def norm_backward_kernel(own, r1, r2, r3, x_ref, gout_ref, gain, gx_ref, low_ref, sums_ref):
    x = x_ref[0:ROWS, :].astype(F32)
    gn = own[...] + sum(r[0:ROWS, :].astype(F32) for r in (r1, r2, r3))
    gout = gout_ref[...].astype(F32)
    centered = x - jnp.mean(x, -1, keepdims=True)
    inv = lax.rsqrt(jnp.mean(centered * centered, -1, keepdims=True) + EPS)
    unit = centered * inv
    gu = gn * gain[...]
    gx = gout + inv * (gu - jnp.mean(gu, -1, keepdims=True) - unit * jnp.mean(gu * unit, -1, keepdims=True))
    gx_ref[...] = gx
    low_ref[...] = gx.astype(BF)
    sums_ref[0:1, :] = jnp.sum(gn * unit, 0, keepdims=True)
    sums_ref[1:2, :] = jnp.sum(gn, 0, keepdims=True)
    sums_ref[2:3, :] = jnp.sum(gout, 0, keepdims=True)


def pack_kernel(w_qkv, w_out, w_in, w_fc, wi_keep, wi_send, wo_keep, wo_send):
    t, core = (lax.axis_index("dp") // 2) % 4, lax.axis_index("section")
    for ref, g in ((wi_keep, core), (wi_send, 1 - core)):
        for j in range(4):
            rank = jnp.bitwise_xor(t, j)
            for part in range(3):
                start = pl.multiple_of(part * D + g * 512 + rank * PAIR, PAIR)
                ref[j, :, part * PAIR : (part + 1) * PAIR] = w_qkv[:, pl.ds(start, PAIR)].astype(BF)
            start = pl.multiple_of(g * 2048 + rank * FB, FB)
            ref[j, :, 3 * PAIR : CI] = w_in[:, pl.ds(start, FB)].astype(BF)
    for ref, half in ((wo_keep, core), (wo_send, 1 - core)):
        cols = pl.ds(pl.multiple_of(512 * half, 512), 512)
        ref[0:64, :] = w_out[:, cols].astype(BF)
        ref[64:320, :] = w_fc[:, cols].astype(BF)


def unpack_kernel(own0, own1, own2, own3, other, wo_own, wo_other, g_qkv, g_out, g_in, g_fc):
    t, core = (lax.axis_index("dp") // 2) % 4, lax.axis_index("section")
    for side, g in ((0, core), (1, 1 - core)):
        for j in range(4):
            block = (own0, own1, own2, own3)[j][...] if side == 0 else other[j]
            block = block.astype(F32)
            rank = jnp.bitwise_xor(t, j)
            for part in range(3):
                start = pl.multiple_of(part * D + g * 512 + rank * PAIR, PAIR)
                g_qkv[:, pl.ds(start, PAIR)] = block[:, part * PAIR : (part + 1) * PAIR]
            start = pl.multiple_of(g * 2048 + rank * FB, FB)
            g_in[:, pl.ds(start, FB)] = block[:, 3 * PAIR : CI]
    for ref, half in ((wo_own, core), (wo_other, 1 - core)):
        cols = pl.ds(pl.multiple_of(512 * half, 512), 512)
        g_out[:, cols] = ref[0:64, :].astype(F32)
        g_fc[:, cols] = ref[64:320, :].astype(F32)


VM = pl.BlockSpec(memory_space=pltpu.VMEM)
HB = pl.BlockSpec(memory_space=pl.ANY)


def kernel_call(kernel, args, outs, any_args=0, scratch=(), cost=2e10, name=None):
    return pl.pallas_call(
        kernel,
        out_shape=outs,
        in_specs=[VM] * (len(args) - any_args) + [HB] * any_args,
        out_specs=[VM] * len(outs),
        scratch_shapes=list(scratch),
        compiler_params=pltpu.CompilerParams(vmem_limit_bytes=VMEM_LIMIT),
        cost_estimate=pl.CostEstimate(flops=int(cost), bytes_accessed=1, transcendentals=0),
        name=name,
    )(*args)


def arr(shape, dtype):
    return jax.ShapeDtypeStruct(shape, dtype)


def weight_scratch(fast):
    return [
        pltpu.VMEM((2, D, CI), BF),
        pltpu.VMEM((2, RO, D), BF),
        pltpu.SemaphoreType.DMA((4 if fast else 1,)),
        pltpu.SemaphoreType.DMA((4 if fast else 1,)),
    ]


def partial_outs():
    return [arr((ROWS, D), F32)] + [arr((ROWS, D), BF)] * 3


def swap_core(value):
    return lax.ppermute(value, "section", [(0, 1), (1, 0)])


def swap_core_now(value):
    both = jnp.stack([value, value])
    core = lax.axis_index("section")
    return lax.dynamic_index_in_dim(lax.all_to_all(both, "section", 0, 0, tiled=True), 1 - core, 0, False)


def flipped(value, flip):
    count = lax.axis_size("dp")
    return lax.ppermute(value, "dp", [(i, i ^ flip) for i in range(count)])


def after(value, *earlier):
    return lax.optimization_barrier((value, earlier))[0]


def choose(own, other):
    first_core = lax.axis_index("section") == 0
    return jnp.where(first_core, own, other), jnp.where(first_core, other, own)


def across(values):
    spread = lax.axis_size("dp") // 8
    return [flipped(v, (j + 1) * spread) for j, v in enumerate(values)]


def groups_of(spread):
    places = [[[g * 4 * spread + t * spread + r for r in range(spread)] for t in range(4)] for g in range(2)]
    t_groups = [[places[g][t][r] for t in range(4)] for g in range(2) for r in range(spread)]
    f_groups = [[places[g][t][r] for g in range(2) for r in range(spread)] for t in range(4)]
    return t_groups, f_groups


def any_gather(w_qkv, w_out, w_in, w_fc):
    share, spread = w_qkv.shape[0], lax.axis_size("dp") // 8
    t_groups, f_groups = groups_of(spread)
    qkv = w_qkv.reshape(share, 3, 2, 4, PAIR).transpose(3, 0, 2, 1, 4).reshape(4, share, 2, 3 * PAIR)
    wi = jnp.concatenate([qkv, w_in.reshape(share, 2, 4, FB).transpose(2, 0, 1, 3)], axis=-1).astype(BF)
    wi = lax.all_to_all(wi, "dp", 0, 0, axis_index_groups=t_groups, tiled=True)
    wi = lax.all_gather(wi, "dp", axis_index_groups=f_groups)
    wi = wi.reshape(2, spread, 4, share, 2, CI).transpose(4, 0, 2, 1, 3, 5).reshape(2, D, CI)
    wo = lax.all_gather(w_out.astype(BF), "dp", axis_index_groups=f_groups).reshape(2, PAIR, D)
    wf = lax.all_gather(w_fc.astype(BF), "dp", axis_index_groups=f_groups).reshape(2, FB, D)
    wo = jnp.concatenate([wo, wf], axis=1)
    return choose(wi, swap_core(wi)), choose(wo, swap_core(wo))


def any_reduce(gi, go):
    count = lax.axis_size("dp")
    spread, share = count // 8, D // count
    t_groups, f_groups = groups_of(spread)

    def scattered(value):
        return lax.psum_scatter(value, "dp", scatter_dimension=0, axis_index_groups=f_groups)

    gi = gi.reshape(2, 2, 4, spread, share, CI).transpose(1, 3, 2, 4, 0, 5).reshape(2 * spread, 4, share, 2, CI)
    gi = lax.all_to_all(scattered(gi), "dp", 0, 0, axis_index_groups=t_groups, tiled=True)
    g_qkv = gi[..., : 3 * PAIR].reshape(4, share, 2, 3, PAIR).transpose(1, 3, 2, 0, 4).reshape(share, 3 * D)
    g_in = gi[..., 3 * PAIR :].transpose(1, 2, 0, 3).reshape(share, 4 * D)
    g_out = scattered(go[:, :PAIR].reshape(2 * spread, share, D))
    g_fc = scattered(go[:, PAIR:].reshape(2 * spread, 4 * share, D))
    return g_qkv, g_out, g_in, g_fc


def body(boundary, segments, ln_gain, ln_bias, w_qkv, w_out, w_in, b_in, w_fc, b_fc):
    core, me = lax.axis_index("section"), lax.axis_index("dp")
    count = lax.axis_size("dp")
    fast = count == 16
    spread = count // 8
    rank = (me // spread) % 4
    share = D // count
    width_small = 7 * share
    first_core = core == 0

    if fast:
        wi_keep, wi_send, wo_keep, wo_send = kernel_call(
            pack_kernel,
            [w_qkv[0], w_out[0], w_in[0], w_fc[0]],
            [arr((4, 64, CI), BF), arr((4, 64, CI), BF), arr((320, 512), BF), arr((320, 512), BF)],
            name="pack",
        )
        wi_recv, wo_recv = swap_core(wi_send), swap_core(wo_send)
        wi_first = [choose(wi_keep[j], wi_recv[j]) for j in range(4)]
        wo_first = choose(wo_keep, wo_recv)
        boundary, ln_gain, ln_bias, b_fc, b_in, segments = after(
            (boundary, ln_gain, ln_bias, b_fc, b_in, segments), wi_keep
        )
    else:
        wi_both, wo_both = any_gather(w_qkv[0], w_out[0], w_in[0], w_fc[0])

    swapped = swap_core(lax.dynamic_index_in_dim(boundary[0], 1 - core, 0, False)[0])
    kept = lax.dynamic_index_in_dim(boundary[0], core, 0, False)[0]
    x0, g1 = choose(kept, swapped)
    small = jnp.concatenate([ln_gain, ln_bias, b_fc, b_in], axis=-1).astype(BF)
    small = jnp.concatenate(choose(small, swap_core(small)))
    seg = lax.dynamic_index_in_dim(segments, core, 0, False)[0].astype(BF)
    extra = jnp.zeros((16, D), BF).at[0, :ROWS].set(seg)
    if fast:
        small = jnp.stack([small, flipped(small, 8)])
        small = jnp.stack([small, flipped(small, 1)])
        extra = extra.at[1:9, :width_small].set(small.reshape(8, width_small))
    pack = jnp.concatenate([x0, extra])

    if fast:

        def join(wi_pieces, wo_pieces, name):
            pieces = [*wo_pieces, *wi_pieces]
            return kernel_call(join_kernel, pieces, [arr((2 * D + 2 * RO, 512), BF)], cost=1, name=name)[0]

        mine = [w[0] for w in wi_first]
        arrived = across(mine[1:])
        wo_own = wo_first[0]
        wo_far, wo_near = flipped(wo_own, 8), flipped(after(wo_own, arrived), 1)
        wi_own = jnp.stack([mine[0]] + arrived)
        wi_far, wi_near = flipped(after(wi_own, wo_far), 8), flipped(wi_own, 1)
        wo_near_far = flipped(after(wo_far, wo_near), 1)
        packs = [pack] + across(after([pack] * 3, arrived))
        mine = [w[1] for w in wi_first]
        arrived = across(
            after([jnp.concatenate([g1, jnp.pad(w, ((0, 0), (0, D - CI)))]) for w in mine[1:]], packs)
        )
        g1s = [g1] + arrived
        wo_own1 = after(wo_first[1], wi_far)
        wi_own1 = after(jnp.stack([mine[0]] + [w[ROWS:, :CI] for w in arrived]), wi_far)
        wo_far1, wi_far1 = flipped(wo_own1, 8), flipped(wi_own1, 8)

        held = jnp.stack([p[129:137, :width_small] for p in packs])
        held = held.reshape(16, 2 * width_small)
        index = jnp.arange(16)
        flip_of = jnp.bitwise_xor(index, me)
        at = (flip_of // 2) % 4 * 4 + (flip_of % 2) * 2 + flip_of // 8
        onehot = (at[:, None] == index[None, :]).astype(BF)
        everyone = mm(onehot, held).reshape(16, 2, width_small)
    else:
        w0, w1 = ([wi_both[l], wo_both[l]] for l in range(2))
        packs, g1s = [pack] + across([pack] * 3), [g1] + across([g1] * 3)
        everyone = lax.all_gather(small, "dp").astype(F32)

    def parts_in_place(value):
        return jnp.where(first_core, value, value[::-1]) if fast else value

    def small_of(layer):
        one = everyone[:, layer]
        vectors = [one[:, i * share : (i + 1) * share].reshape(1, D) for i in range(3)]
        b = one[:, 3 * share :].reshape(2, 4, FB)
        return *vectors, parts_in_place(lax.dynamic_index_in_dim(b, rank, 1, False))

    gain0, bias0, bfc0, bin0 = small_of(0)
    gain1, bias1, bfc1, bin1 = small_of(1)

    segs = jnp.stack([p[ROWS, :ROWS] for p in packs])
    row = lax.broadcasted_iota(jnp.int32, (ROWS, ROWS), 0)
    col = lax.broadcasted_iota(jnp.int32, (ROWS, ROWS), 1)
    mask = ((segs[:, :, None] == segs[:, None, :]) & (col <= row)).astype(F32)
    positions = jnp.sum(mask, -1).reshape(TOK, 1) - 1.0
    lane = jnp.arange(PAIR) % 64
    freq = jnp.where(lane < 32, 10000.0 ** (-(lane // 2 * 2).astype(F32) / 32), 0.0)
    angle = positions * freq
    cosine = jnp.cos(angle)
    sine = jnp.sin(angle) * jnp.where(lane % 2 == 0, -1.0, 1.0)

    if fast:
        tables = (gain0, bias0, bin0, cosine, sine, mask, gain1, bias1, bin1, bfc0, bfc1)
        wi_near_far = flipped(after(wi_far, wi_near, tables, g1s), 1)
        w0 = join([wi_own, wi_far, wi_near, wi_near_far], [wo_own, wo_far, wo_near, wo_near_far], "join0")
        w0 = [w0, swap_core(after(w0, wo_far1))]
        wo_near1, wi_near1 = flipped(after(wo_own1, wi_near_far), 1), flipped(after(wi_own1, wi_near_far), 1)

    saved = [
        arr((TOK, A_COLS), BF),
        arr((2, TOK, 3 * PAIR), BF),
        arr((2, 4, 2 * ROWS, ROWS), F32),
        arr((2, TOK, FB), F32),
    ]
    got = kernel_call(
        functools.partial(first_forward_kernel, fast),
        [*packs, gain0, bias0, bin0, cosine, sine, mask, *w0],
        partial_outs() + saved,
        any_args=2,
        scratch=weight_scratch(fast),
        cost=1,
        name="first_forward",
    )
    own, sends, (ship_a0, qkv0, probs0, pre0) = got[0], got[1:4], got[4:]

    def total(own, arrived):
        return sum([r.astype(F32) for r in arrived], own)

    arrived = across(sends)
    sums = total(own, arrived)
    if fast:
        wo_near_far1 = flipped(after(wo_far1, own, wo_near1), 1)
        wi_near_far1 = flipped(after(wi_far1, own, wi_near1), 1)
        w1 = join([wi_own1, wi_far1, wi_near1, wi_near_far1], [wo_own1, wo_far1, wo_near1, wo_near_far1], "join1")
        w1 = [w1, swap_core_now(w1)]
    x1 = (x0.astype(F32) + sums + bfc0).astype(BF)
    x1s = [x1] + across([x1] * 3)

    back_outs = [arr((TOK, B_COLS), BF), arr((TOK, CI), BF), arr((2, FB), F32)]
    got = kernel_call(
        functools.partial(second_layer_kernel, fast),
        [*x1s, *g1s, gain1, bias1, bin1, cosine, sine, mask, *w1],
        partial_outs()
        + partial_outs()
        + [arr((TOK, A_COLS), BF)]
        + back_outs,
        any_args=2,
        scratch=[
            pltpu.VMEM((2, TOK, 3 * PAIR), BF),
            pltpu.VMEM((2, 4, 2 * ROWS, ROWS), F32),
            pltpu.VMEM((2, TOK, FB), F32),
            pltpu.VMEM((TOK, D), BF),
        ]
        + weight_scratch(fast),
        name="second_layer",
    )
    out_own, out_sends, gn_own, gn_sends = got[0], got[1:4], got[4], got[5:8]
    ship_a1, ship_b1, gcat1, gbin1 = got[8:]

    def norm_backward(own, arrived, x, gout, gain, name):
        return kernel_call(
            norm_backward_kernel,
            [own, *arrived, x, gout, gain],
            [arr((ROWS, D), F32), arr((ROWS, D), BF), arr((3, D), F32)],
            name=name,
        )

    def grads_out(gouts, ship_a, other_a, other_b, extra, name):
        if fast:
            extras = [] if extra is None else [extra]
            rows = 320 + 16 * len(extras)
            return kernel_call(
                weight_grad_out_kernel,
                [*gouts, ship_a, other_a, other_b, *extras],
                [arr((2, rows, 512), BF)] * 2,
                scratch=[pltpu.VMEM((2, 2, 320, 2 * TOK), BF), pltpu.VMEM((2 * TOK, 512), BF)],
                name=name,
            )
        scratch = [pltpu.VMEM((TOK, D), BF)]
        return kernel_call(whole_grad_out_kernel, [*gouts, ship_a], [arr((2, RO, D), BF)], scratch=scratch, name=name)

    def grads_in(ship_a, other_a, ship_b, other_b, gcat, name):
        if fast:
            return kernel_call(
                weight_grad_in_kernel,
                [ship_a, other_a, gcat, other_b],
                [arr((2, 4, 64, CI), BF)] * 2,
                scratch=[pltpu.VMEM((2, 2, 256, 2 * TOK), BF), pltpu.VMEM((2 * TOK, CI), BF)],
                name=name,
            )
        return kernel_call(whole_grad_in_kernel, [ship_a, gcat, ship_b], [arr((2, D, CI), BF)], name=name)

    def onward(keep, near):
        return flipped((keep[1].astype(F32) + near[1].astype(F32)).astype(BF), 8)

    def reduced(keep, near, far):
        return keep[0].astype(F32) + near[0].astype(F32) + far.astype(F32)

    arrived_gn = across(gn_sends)
    other_a1, other_b1 = (swap_core(ship_a1), swap_core(ship_b1)) if fast else (None, None)
    other_a0 = swap_core(ship_a0) if fast else None
    go1 = grads_out(g1s, after(ship_a1, other_a0), other_a1, other_b1, None, "grads1_out")
    _, g0, sums1 = norm_backward(after(gn_own, go1), arrived_gn, x1, g1, gain1, "norm_backward1")
    g0s = [g0] + across([g0] * 3)
    gi1 = grads_in(after(ship_a1, g0), other_a1, ship_b1, other_b1, gcat1, "grads1_in")
    if fast:
        keep1, send1 = zip(go1, gi1)
        near1 = [flipped(v, 1) for v in send1]
        far1 = [onward(k, v) for k, v in zip(keep1, near1)]
        g0s[0] = after(g0, near1[0], gi1)

    got = kernel_call(
        functools.partial(first_backward_kernel, fast),
        [*g0s, *out_sends, cosine, sine, qkv0, probs0, pre0, *w0],
        [arr((ROWS, D), F32)] + [arr((2 * ROWS, D), BF)] * 3 + back_outs,
        any_args=2,
        scratch=[pltpu.VMEM((TOK, D), BF)] + weight_scratch(fast),
        name="first_backward",
    )
    gn_own, gn_sends, (ship_b0, gcat0, gbin0) = got[0], got[1:4], got[4:]
    arrived_gn = across(gn_sends)
    if fast:
        other_b0 = swap_core(after(ship_b0, near1[1], far1[0]))
    else:
        other_b0 = None
    gi0 = grads_in(ship_a0, other_a0, ship_b0, other_b0, gcat0, "grads0_in")
    gx0, _, sums0 = norm_backward(after(gn_own, gi0), arrived_gn, x0, g0, gain0, "norm_backward0")

    def small_grads(sums, gbin):
        onehot = (jnp.arange(4) == rank).astype(F32)
        vectors = sums.reshape(3, 2, 4, spread, share).transpose(1, 2, 3, 0, 4).reshape(2, 4, spread, 3 * share)
        b = parts_in_place(gbin).reshape(2, 1, spread, 4 * share)
        return (vectors, b) if fast else jnp.concatenate([vectors, b * onehot[None, :, None, None]], axis=-1)

    both = jax.tree.map(choose, small_grads(sums0, gbin0), small_grads(sums1, gbin1))
    if fast:
        mine, theirs = (jnp.concatenate([v[i].reshape(-1) for v in both]) for i in range(2))
        mine = mine + swap_core(theirs)
        vectors, b = mine[: 3 * D].reshape(2, 4, 2, 192), mine[3 * D :].reshape(2, 1, 2, 256)
        values = jnp.concatenate([vectors.transpose(2, 0, 1, 3).reshape(2, 2, 768), b[:, 0].transpose(1, 0, 2)], axis=-1)
        values = jnp.where(me // 8 == 0, values, values[:, ::-1])
        values = jnp.where(me % 2 == 0, values, values[::-1])
        extra = jnp.zeros((2, 2, 16, 512), BF).at[:, :, :2].set(values.reshape(2, 2, 2, 512).astype(BF))
        wo_1, wi_1 = (reduced(*v).astype(BF) for v in zip(keep1, near1, far1))
        wi_1 = [wi_1[0]] + across([wi_1[j] for j in range(1, 4)])
        near_in0 = flipped(gi0[1], 1)
        far_in0 = onward(gi0[0], near_in0)
        extra = after(extra, wi_1, near_in0)
    else:
        extra = None
    go0 = grads_out(g0s, ship_a0, other_a0, other_b0, extra, "grads0_out")

    out1 = x1.astype(F32) + total(out_own, [r[ROWS:] for r in arrived_gn]) + bfc1
    arrived = swap_core(jnp.where(first_core, out1, gx0))
    boundary_out = jnp.where(first_core, jnp.stack([gx0, arrived]), jnp.stack([arrived, out1]))[None, :, None]
    if fast:
        near_out0 = flipped(go0[1], 1)
        far_out0 = onward(go0[0], near_out0)
        wo_0 = reduced(go0[0], near_out0, far_out0)
        wi_0 = after(reduced(gi0[0], near_in0, far_in0), go0)
        vector = wo_0[320:322].reshape(1024)
        ranks = vector[:768].reshape(4, 192)
        ranks = [lax.dynamic_index_in_dim(ranks, jnp.bitwise_xor(rank, j), 0, True) for j in range(4)]
        summed = sum([r.astype(F32) for r in across([r.astype(BF) for r in ranks[1:]])], ranks[0])
        vector = jnp.concatenate([summed, vector[None, 768:]], axis=1)
        wo_0, wi_0 = wo_0[:320].astype(BF), wi_0.astype(BF)
        wi_0 = [wi_0[0]] + across([wi_0[j] for j in range(1, 4)])
        wo_mine, wo_theirs = choose(wo_0, wo_1)
        pairs = [choose(a, b) for a, b in zip(wi_0, wi_1)]
        wi_other = swap_core(jnp.stack([p[1] for p in pairs]))
        g_qkv, g_out, g_in, g_fc = kernel_call(
            unpack_kernel,
            [*[p[0] for p in pairs], wi_other, wo_mine, swap_core(wo_theirs)],
            [arr((64, 3 * D), F32), arr((64, D), F32), arr((64, 4 * D), F32), arr((256, D), F32)],
            name="unpack",
        )
    else:
        vector = (both[0] + swap_core(both[1])).reshape(count, 7 * share)
        vector = lax.psum_scatter(vector, "dp", scatter_dimension=0, tiled=True)
        mine, theirs = choose(gi0[0], gi1[0])
        gi = mine.astype(F32) + swap_core(theirs).astype(F32)
        mine, theirs = choose(go0[0], go1[0])
        go = mine.astype(F32) + swap_core(theirs).astype(F32)
        g_qkv, g_out, g_in, g_fc = any_reduce(gi, go)
    g_gain, g_bias, g_bfc = (vector[:, i * share : (i + 1) * share] for i in range(3))
    g_bin = vector[:, 3 * share :]

    return (boundary_out, g_gain, g_bias, g_qkv[None], g_out[None], g_in[None], g_bin, g_fc[None], g_bfc)


def solution(mesh):
    rows = P("section", None, "dp", None, None)
    vector, matrix = P("section", "dp"), P("section", "dp", None)
    return jax.shard_map(
        body,
        mesh=mesh,
        in_specs=(rows, P(None, "dp", None), vector, vector, matrix, matrix, matrix, vector, matrix, vector),
        out_specs=(rows, vector, vector, matrix, matrix, matrix, vector, matrix, vector),
        check_vma=False,
    )
```

```python
import functools

import jax
import jax.numpy as jnp
from jax import lax
from jax.experimental import pallas as pl
from jax.experimental.pallas import tpu as pltpu
from jax.sharding import PartitionSpec as P

D = 1024
PAIR = 128
FB = 512
CI = 3 * PAIR + FB
RO = PAIR + FB
EPS = 1e-05
NEG = -1000000000.0
SCALE = 0.125
ROWS = 128
TOK = 4 * ROWS
BF = jnp.bfloat16
F32 = jnp.float32
VMEM_LIMIT = 24 * 1024 * 1024


def mm(a, b):
    return lax.dot_general(a, b, (((1,), (0,)), ((), ())), preferred_element_type=F32)


def mm_nt(a, b):
    return lax.dot_general(a, b, (((1,), (1,)), ((), ())), preferred_element_type=F32)


def mm_tn(a, b):
    return lax.dot_general(a, b, (((0,), (0,)), ((), ())), preferred_element_type=F32)


def gelu(h):
    return 0.5 * h * (1.0 + jnp.tanh(0.7978845608 * (h + 0.044715 * h * h * h)))


def gelu_slope(h):
    th = jnp.tanh(0.7978845608 * (h + 0.044715 * h * h * h))
    inner = 0.7978845608 * (1.0 + 3 * 0.044715 * h * h)
    return 0.5 * (1.0 + th) + 0.5 * h * (1.0 - th * th) * inner


def partner(x):
    lane = lax.broadcasted_iota(jnp.int32, x.shape, 1)
    return jnp.where(lane % 2 == 0, pltpu.roll(x, PAIR - 1, 1), pltpu.roll(x, 1, 1))


def turned(x, cosine, sine):
    return x * cosine + partner(x) * sine


def by_head(x):
    lane = lax.broadcasted_iota(jnp.int32, (1, PAIR), 1)
    low = jnp.where(lane < 64, 1.0, 0.0).astype(x.dtype)
    high = jnp.where(lane < 64, 0.0, 1.0).astype(x.dtype)
    return jnp.concatenate([x * low, x * high], axis=0)


def beside(x):
    return jnp.concatenate([x[:ROWS], x[ROWS:]], axis=1)


def heads_of(x):
    return [x[ROWS * j : ROWS * (j + 1)] for j in range(4)]


def rows_of(j):
    return pl.ds(j * ROWS, ROWS)


def layer_norm_into(x_refs, gain_ref, bias_ref, normed):
    for j, x_ref in enumerate(x_refs):
        x = x_ref[0:ROWS, :].astype(F32)
        centered = x - jnp.mean(x, -1, keepdims=True)
        inv = lax.rsqrt(jnp.mean(centered * centered, -1, keepdims=True) + EPS)
        normed[rows_of(j), :] = (centered * inv * gain_ref[...] + bias_ref[...]).astype(BF)


def forward_in(g, normed, w, bin_ref, cos_ref, sin_ref, mask_ref, qkv, probs, oa, pre):
    w_qkv, w_in = w[g]
    y = mm(normed[...], w_qkv[...])
    cosine, sine = cos_ref[...], sin_ref[...]
    qkv[g, :, 0:PAIR] = turned(y[:, 0:PAIR], cosine, sine).astype(BF)
    qkv[g, :, PAIR : 2 * PAIR] = turned(y[:, PAIR : 2 * PAIR], cosine, sine).astype(BF)
    qkv[g, :, 2 * PAIR : 3 * PAIR] = y[:, 2 * PAIR : 3 * PAIR].astype(BF)
    q, k, v = (heads_of(qkv[g, :, i * PAIR : (i + 1) * PAIR]) for i in range(3))
    s = jnp.concatenate([mm_nt(by_head(q[j]), k[j]) for j in range(4)], axis=0) * SCALE
    s = jnp.where(mask_ref[...] > 0.5, s, NEG)
    e = jnp.exp(s - jnp.max(s, -1, keepdims=True))
    p = e / jnp.sum(e, -1, keepdims=True)
    probs[g] = p
    p = p.astype(BF)
    o = [mm(beside(p[2 * ROWS * j : 2 * ROWS * (j + 1)]), by_head(v[j])) for j in range(4)]
    oa[g][:, 0:PAIR] = jnp.concatenate(o, axis=0).astype(BF)
    h = mm(normed[...], w_in[...]) + bin_ref[g : g + 1, :]
    pre[g] = h
    oa[g][:, PAIR:RO] = gelu(h).astype(BF)


def forward_out(oa, w_out, outs):
    for (start, w0), (_, w1) in zip(*w_out):
        for n in range(2):
            part = mm(oa[0][...], w0[:, n * 256 : (n + 1) * 256]) + mm(oa[1][...], w1[:, n * 256 : (n + 1) * 256])
            cols = pl.ds(pl.multiple_of(start + n * 256, 256), 256)
            for j in range(4):
                outs[j][0:ROWS, cols] = part[j * ROWS : (j + 1) * ROWS].astype(outs[j].dtype)


def backward_out(g, gout, w_out, qkv, probs, pre, cos_ref, sin_ref, gcat, gbin_ref):
    halves = [(gout[:, pl.ds(start, 512)], w) for start, w in w_out[g]]
    go = sum(mm_nt(rows, w[0:PAIR, :]) for rows, w in halves).astype(BF)
    q, k, v = (heads_of(qkv[g, :, i * PAIR : (i + 1) * PAIR]) for i in range(3))
    cosine, sine = cos_ref[...], sin_ref[...]
    go = [by_head(rows) for rows in heads_of(go)]
    p = probs[g]
    gp = jnp.concatenate([mm_nt(go[j], v[j]) for j in range(4)], axis=0)
    gs = (p * (gp - jnp.sum(gp * p, -1, keepdims=True))).astype(BF)
    gs = [gs[2 * ROWS * j : 2 * ROWS * (j + 1)] for j in range(4)]
    p = p.astype(BF)
    gq = jnp.concatenate([mm(beside(gs[j]), by_head(k[j])) for j in range(4)], axis=0) * SCALE
    gk = jnp.concatenate([mm_tn(gs[j], by_head(q[j])) for j in range(4)], axis=0) * SCALE
    gv = jnp.concatenate([mm_tn(p[2 * ROWS * j : 2 * ROWS * (j + 1)], go[j]) for j in range(4)], axis=0)
    gcat[g][:, 0:PAIR] = turned(gq, cosine, -sine).astype(BF)
    gcat[g][:, PAIR : 2 * PAIR] = turned(gk, cosine, -sine).astype(BF)
    gcat[g][:, 2 * PAIR : 3 * PAIR] = gv.astype(BF)
    ga = sum(mm_nt(rows, w[PAIR:RO, :]) for rows, w in halves)
    gpre = (ga * gelu_slope(pre[g])).astype(BF)
    gcat[g][:, 3 * PAIR : CI] = gpre
    gbin_ref[g : g + 1, :] = jnp.sum(gpre.astype(F32), 0, keepdims=True)


def backward_in(gcat, w, outs):
    for n in range(4):
        cols = slice(n * 256, (n + 1) * 256)
        part = sum(
            mm_nt(gcat[g][:, 0 : 3 * PAIR], w[g][0][cols, :]) + mm_nt(gcat[g][:, 3 * PAIR : CI], w[g][1][cols, :])
            for g in range(2)
        )
        for j in range(4):
            outs[j][0:ROWS, cols] = part[j * ROWS : (j + 1) * ROWS].astype(outs[j].dtype)


A_COLS = D + 2 * RO
B_COLS = CI + 512


def views_a(ship_a):
    return ship_a.at[:, 0:D], (ship_a.at[:, D : D + RO], ship_a.at[:, D + RO : D + 2 * RO])


def views_b(ship_b):
    return ship_b.at[:, 0:CI], ship_b.at[:, CI : CI + 512]


HALF = (2 * D + 2 * RO, 512)


def weights_of(fast, refs):
    if not fast:
        wi, wo = refs
        ins = [(wi.at[g, :, 0 : 3 * PAIR], wi.at[g, :, 3 * PAIR : CI]) for g in range(2)]
        return ins, [[(0, wo.at[g, :, 0:512]), (512, wo.at[g, :, 512:1024])] for g in range(2)]
    core = lax.axis_index("section")
    halves = refs if len(refs) == 2 else [refs[0].at[core], refs[0].at[1 - core]]
    starts = [pl.multiple_of(512 * c, 512) for c in (core, 1 - core)]
    rows = [pl.ds(pl.multiple_of(2 * D + RO * c, 128), RO) for c in (core, 1 - core)]
    ins = [(half.at[D : 2 * D, 0 : 3 * PAIR], half.at[0:D, :]) for half in halves]
    return ins, [[(start, half.at[rows[g], :]) for start, half in zip(starts, halves)] for g in range(2)]


def place_of():
    return lax.axis_index("dp"), lax.axis_index("section")


def other_half(fast, gout, half_ref):
    core = lax.axis_index("section") if fast else 0
    half_ref[...] = gout[:, pl.ds(pl.multiple_of(512 * (1 - core), 512), 512)]


def join_kernel(own, far, near_own, near_far, *refs):
    pieces, joined = refs[:-1], refs[-1]
    me, _ = place_of()
    for flip, piece in ((0, own), (8, far), (1, near_own), (9, near_far)):
        source = jnp.bitwise_xor(me, flip)
        g, r = source // 8, source % 2
        base = 2 * D + g * RO
        joined[pl.ds(pl.multiple_of(base + 64 * r, 64), 64), :] = piece[0:64, :]
        joined[pl.ds(pl.multiple_of(base + PAIR + 256 * r, 128), 256), :] = piece[64:320, :]
    blocks = [(ref, i) for ref in pieces for i in range(ref.shape[0])]
    for (ref, i), flip in zip(blocks, [f ^ (2 * j) for f in (0, 8, 1, 9) for j in range(4)]):
        start = pl.multiple_of(jnp.bitwise_xor(me, flip) * 64, 64)
        joined[pl.ds(start, 64), :] = ref[i, :, 3 * PAIR : CI]
        joined[pl.ds(D + start, 64), 0 : 3 * PAIR] = ref[i, :, 0 : 3 * PAIR]


def join_twice_kernel(*refs):
    join_kernel(*refs[:-1], refs[-1].at[0])
    refs[-1][1] = refs[-1][0]


def first_forward_kernel(fast, n_w, *refs):
    x_refs, (gain, bias, bin_ref, cos_ref, sin_ref, mask_ref), refs = refs[:4], refs[4:10], refs[10:]
    w_in, w_out = weights_of(fast, refs[:n_w])
    outs, (ship_a, qkv, probs, pre) = refs[n_w : n_w + 4], refs[n_w + 4 :]
    normed, oa = views_a(ship_a)
    layer_norm_into(x_refs, gain, bias, normed)
    for g in range(2):
        forward_in(g, normed, w_in, bin_ref, cos_ref, sin_ref, mask_ref, qkv, probs, oa, pre)
    forward_out(oa, w_out, outs)


def second_layer_kernel(fast, n_w, *refs):
    x_refs, gout_refs, refs = refs[:4], refs[4:8], refs[8:]
    (gain, bias, bin_ref, cos_ref, sin_ref, mask_ref), refs = refs[:6], refs[6:]
    w_in, w_out = weights_of(fast, refs[:n_w])
    outs, gouts, refs = refs[n_w : n_w + 4], refs[n_w + 4 : n_w + 8], refs[n_w + 8 :]
    ship_a, ship_b, gcat0, gbin_ref, qkv, probs, pre, gout = refs
    normed, oa = views_a(ship_a)
    gcat1, gout_half = views_b(ship_b)
    gcat = (gcat0, gcat1)
    layer_norm_into(x_refs, gain, bias, normed)
    for j in range(4):
        gout[rows_of(j), :] = gout_refs[j][...]
    other_half(fast, gout, gout_half)
    for g in range(2):
        forward_in(g, normed, w_in, bin_ref, cos_ref, sin_ref, mask_ref, qkv, probs, oa, pre)
    for g in range(2):
        backward_out(g, gout, w_out, qkv, probs, pre, cos_ref, sin_ref, gcat, gbin_ref)
    backward_in(gcat, w_in, gouts)
    forward_out(oa, w_out, outs)


def first_backward_kernel(fast, n_w, *refs):
    gout_refs, refs = refs[:4], refs[4:]
    (cos_ref, sin_ref, qkv, probs, pre), refs = refs[:5], refs[5:]
    w_in, w_out = weights_of(fast, refs[:n_w])
    gouts, (ship_b, gcat0, gbin_ref, gout) = refs[n_w : n_w + 4], refs[n_w + 4 :]
    gcat1, gout_half = views_b(ship_b)
    gcat = (gcat0, gcat1)
    for j in range(4):
        gout[rows_of(j), :] = gout_refs[j][...]
    other_half(fast, gout, gout_half)
    for g in range(2):
        backward_out(g, gout, w_out, qkv, probs, pre, cos_ref, sin_ref, gcat, gbin_ref)
    backward_in(gcat, w_in, gouts)


def turn_kernel(ship_a, other_a, left_in, left_out):
    me, core = place_of()
    g, t, r = me // 8, (me // 2) % 4, me % 2
    for side, ship in enumerate((ship_a, other_a)):
        tokens = slice(side * TOK, (side + 1) * TOK)
        for part in range(2):
            far = jnp.bitwise_xor(g, jnp.bitwise_xor(core, part ^ side))
            flat = ship[:, D + part * RO : D + (part + 1) * RO].T
            for s in range(2):
                near = jnp.bitwise_xor(r, s)
                left_out[near, far, 0:64, tokens] = flat[64 * s : 64 * s + 64]
                left_out[near, far, 64:320, tokens] = flat[PAIR + 256 * s : PAIR + 256 * (s + 1)]
        for far in range(2):
            for j in range(4):
                pair = jnp.bitwise_xor(g, far) * 4 + jnp.bitwise_xor(t, j)
                block = ship[:, pl.ds(pl.multiple_of(pair * PAIR, PAIR), PAIR)].T
                start = far * 256 + 64 * j
                for s in range(2):
                    left_in[jnp.bitwise_xor(r, s), start : start + 64, tokens] = block[64 * s : 64 * s + 64]


def weight_grad_out_kernel(*refs):
    gout_refs, (left, other_b, *extras, keep, send, right) = refs[:4], refs[4:]
    cols = pl.ds(pl.multiple_of(512 * lax.axis_index("section"), 512), 512)
    for j in range(4):
        right[rows_of(j), :] = gout_refs[j][:, cols]
    for near, out in ((1, send), (0, keep)):
        for far in range(2):
            part = mm(left[near, far, :, 0:TOK], right[...])
            part += mm(left[near, far, :, TOK : 2 * TOK], other_b[:, CI : CI + 512])
            out[far, 0:320, :] = part.astype(BF)
            for extra in extras:
                out[far, 320:336, :] = extra[near, far]


def weight_grad_in_kernel(left, gcat, other_b, keep, send):
    for near, out in ((1, send), (0, keep)):
        part = mm(left[near, :, 0:TOK], gcat[...]) + mm(left[near, :, TOK : 2 * TOK], other_b[:, 0:CI])
        part = part.astype(BF)
        for i in range(8):
            out[i // 4, i % 4] = part[64 * i : 64 * i + 64]


def whole_grad_out_kernel(*refs):
    gout_refs, (ship_a, out, gout) = refs[:4], refs[4:]
    for j in range(4):
        gout[rows_of(j), :] = gout_refs[j][...]
    for g in range(2):
        out[g] = mm_tn(ship_a[:, D + g * RO : D + (g + 1) * RO], gout[...]).astype(BF)


def whole_grad_in_kernel(ship_a, gcat0, ship_b, out):
    for g in range(2):
        right = gcat0[...] if g == 0 else ship_b[:, 0:CI]
        for m in range(4):
            rows = slice(m * 256, (m + 1) * 256)
            out[g, rows, :] = mm_tn(ship_a[:, rows], right).astype(BF)


def norm_backward_kernel(own, r1, r2, r3, x_ref, gout_ref, gain, gx_ref, low_ref, sums_ref):
    x = x_ref[0:ROWS, :].astype(F32)
    gn = own[...] + sum(r[...].astype(F32) for r in (r1, r2, r3))
    gout = gout_ref[...].astype(F32)
    centered = x - jnp.mean(x, -1, keepdims=True)
    inv = lax.rsqrt(jnp.mean(centered * centered, -1, keepdims=True) + EPS)
    unit = centered * inv
    gu = gn * gain[...]
    gx = gout + inv * (gu - jnp.mean(gu, -1, keepdims=True) - unit * jnp.mean(gu * unit, -1, keepdims=True))
    gx_ref[...] = gx
    low_ref[...] = gx.astype(BF)
    sums_ref[0:1, :] = jnp.sum(gn * unit, 0, keepdims=True)
    sums_ref[1:2, :] = jnp.sum(gn, 0, keepdims=True)
    sums_ref[2:3, :] = jnp.sum(gout, 0, keepdims=True)


def pack_kernel(w_qkv, w_out, w_in, w_fc, wi_keep, wi_send, wo_keep, wo_send):
    t, core = (lax.axis_index("dp") // 2) % 4, lax.axis_index("section")
    for ref, g in ((wi_keep, core), (wi_send, 1 - core)):
        for j in range(4):
            rank = jnp.bitwise_xor(t, j)
            for part in range(3):
                start = pl.multiple_of(part * D + g * 512 + rank * PAIR, PAIR)
                ref[j, :, part * PAIR : (part + 1) * PAIR] = w_qkv[:, pl.ds(start, PAIR)].astype(BF)
            start = pl.multiple_of(g * 2048 + rank * FB, FB)
            ref[j, :, 3 * PAIR : CI] = w_in[:, pl.ds(start, FB)].astype(BF)
    for ref, half in ((wo_keep, core), (wo_send, 1 - core)):
        cols = pl.ds(pl.multiple_of(512 * half, 512), 512)
        ref[0:64, :] = w_out[:, cols].astype(BF)
        ref[64:320, :] = w_fc[:, cols].astype(BF)


def unpack_kernel(own0, own1, own2, own3, other, wo_own, wo_other, g_qkv, g_out, g_in, g_fc):
    t, core = (lax.axis_index("dp") // 2) % 4, lax.axis_index("section")
    for side, g in ((0, core), (1, 1 - core)):
        for j in range(4):
            block = (own0, own1, own2, own3)[j][...] if side == 0 else other[j]
            block = block.astype(F32)
            rank = jnp.bitwise_xor(t, j)
            for part in range(3):
                start = pl.multiple_of(part * D + g * 512 + rank * PAIR, PAIR)
                g_qkv[:, pl.ds(start, PAIR)] = block[:, part * PAIR : (part + 1) * PAIR]
            start = pl.multiple_of(g * 2048 + rank * FB, FB)
            g_in[:, pl.ds(start, FB)] = block[:, 3 * PAIR : CI]
    for ref, half in ((wo_own, core), (wo_other, 1 - core)):
        cols = pl.ds(pl.multiple_of(512 * half, 512), 512)
        g_out[:, cols] = ref[0:64, :].astype(F32)
        g_fc[:, cols] = ref[64:320, :].astype(F32)


VM = pl.BlockSpec(memory_space=pltpu.VMEM)


def kernel_call(kernel, args, outs, scratch=(), cost=2e10, name=None):
    return pl.pallas_call(
        kernel,
        out_shape=outs,
        in_specs=[VM] * len(args),
        out_specs=[VM] * len(outs),
        scratch_shapes=list(scratch),
        compiler_params=pltpu.CompilerParams(vmem_limit_bytes=VMEM_LIMIT),
        cost_estimate=pl.CostEstimate(flops=int(cost), bytes_accessed=1, transcendentals=0),
        name=name,
    )(*args)


def arr(shape, dtype):
    return jax.ShapeDtypeStruct(shape, dtype)


def partial_outs():
    return [arr((ROWS, D), F32)] + [arr((ROWS, D), BF)] * 3


def swap_core(value):
    return lax.ppermute(value, "section", [(0, 1), (1, 0)])


def flipped(value, flip):
    count = lax.axis_size("dp")
    return lax.ppermute(value, "dp", [(i, i ^ flip) for i in range(count)])


def after(value, *earlier):
    return lax.optimization_barrier((value, earlier))[0]


def choose(own, other):
    first_core = lax.axis_index("section") == 0
    return jnp.where(first_core, own, other), jnp.where(first_core, other, own)


def across(values):
    spread = lax.axis_size("dp") // 8
    return [flipped(v, (j + 1) * spread) for j, v in enumerate(values)]


def groups_of(spread):
    places = [[[g * 4 * spread + t * spread + r for r in range(spread)] for t in range(4)] for g in range(2)]
    t_groups = [[places[g][t][r] for t in range(4)] for g in range(2) for r in range(spread)]
    f_groups = [[places[g][t][r] for g in range(2) for r in range(spread)] for t in range(4)]
    return t_groups, f_groups


def any_gather(w_qkv, w_out, w_in, w_fc):
    share, spread = w_qkv.shape[0], lax.axis_size("dp") // 8
    t_groups, f_groups = groups_of(spread)
    qkv = w_qkv.reshape(share, 3, 2, 4, PAIR).transpose(3, 0, 2, 1, 4).reshape(4, share, 2, 3 * PAIR)
    wi = jnp.concatenate([qkv, w_in.reshape(share, 2, 4, FB).transpose(2, 0, 1, 3)], axis=-1).astype(BF)
    wi = lax.all_to_all(wi, "dp", 0, 0, axis_index_groups=t_groups, tiled=True)
    wi = lax.all_gather(wi, "dp", axis_index_groups=f_groups)
    wi = wi.reshape(2, spread, 4, share, 2, CI).transpose(4, 0, 2, 1, 3, 5).reshape(2, D, CI)
    wo = lax.all_gather(w_out.astype(BF), "dp", axis_index_groups=f_groups).reshape(2, PAIR, D)
    wf = lax.all_gather(w_fc.astype(BF), "dp", axis_index_groups=f_groups).reshape(2, FB, D)
    wo = jnp.concatenate([wo, wf], axis=1)
    return choose(wi, swap_core(wi)), choose(wo, swap_core(wo))


def any_reduce(gi, go):
    count = lax.axis_size("dp")
    spread, share = count // 8, D // count
    t_groups, f_groups = groups_of(spread)

    def scattered(value):
        return lax.psum_scatter(value, "dp", scatter_dimension=0, axis_index_groups=f_groups)

    gi = gi.reshape(2, 2, 4, spread, share, CI).transpose(1, 3, 2, 4, 0, 5).reshape(2 * spread, 4, share, 2, CI)
    gi = lax.all_to_all(scattered(gi), "dp", 0, 0, axis_index_groups=t_groups, tiled=True)
    g_qkv = gi[..., : 3 * PAIR].reshape(4, share, 2, 3, PAIR).transpose(1, 3, 2, 0, 4).reshape(share, 3 * D)
    g_in = gi[..., 3 * PAIR :].transpose(1, 2, 0, 3).reshape(share, 4 * D)
    g_out = scattered(go[:, :PAIR].reshape(2 * spread, share, D))
    g_fc = scattered(go[:, PAIR:].reshape(2 * spread, 4 * share, D))
    return g_qkv, g_out, g_in, g_fc


def body(boundary, segments, ln_gain, ln_bias, w_qkv, w_out, w_in, b_in, w_fc, b_fc):
    core, me = lax.axis_index("section"), lax.axis_index("dp")
    count = lax.axis_size("dp")
    fast = count == 16
    spread = count // 8
    rank = (me // spread) % 4
    share = D // count
    width_small = 7 * share
    first_core = core == 0

    if fast:
        wi_keep, wi_send, wo_keep, wo_send = kernel_call(
            pack_kernel,
            [w_qkv[0], w_out[0], w_in[0], w_fc[0]],
            [arr((4, 64, CI), BF), arr((4, 64, CI), BF), arr((320, 512), BF), arr((320, 512), BF)],
            name="pack",
        )
        wi_recv, wo_recv = swap_core(wi_send), swap_core(wo_send)
        wi_first = [choose(wi_keep[j], wi_recv[j]) for j in range(4)]
        wo_first = choose(wo_keep, wo_recv)
        boundary, ln_gain, ln_bias, b_fc, b_in, segments = after(
            (boundary, ln_gain, ln_bias, b_fc, b_in, segments), wi_keep
        )
    else:
        wi_both, wo_both = any_gather(w_qkv[0], w_out[0], w_in[0], w_fc[0])

    swapped = swap_core(lax.dynamic_index_in_dim(boundary[0], 1 - core, 0, False)[0])
    kept = lax.dynamic_index_in_dim(boundary[0], core, 0, False)[0]
    x0, g1 = choose(kept, swapped)
    small = jnp.concatenate([ln_gain, ln_bias, b_fc, b_in], axis=-1).astype(BF)
    small = jnp.concatenate(choose(small, swap_core(small)))
    seg = lax.dynamic_index_in_dim(segments, core, 0, False)[0].astype(BF)
    extra = jnp.zeros((16, D), BF).at[0, :ROWS].set(seg)
    if fast:

        def join(wi_pieces, wo_pieces, name):
            pieces = [*wo_pieces, *wi_pieces]
            if name == "join0":
                own = kernel_call(join_kernel, pieces, [arr(HALF, BF)], cost=1, name=name)[0]
                return own
            both = kernel_call(join_twice_kernel, pieces, [arr((2, *HALF), BF)], cost=1, name=name)[0]
            return lax.all_to_all(both, "section", 0, 0, tiled=True)

        mine = [after(jnp.stack(w), wo_first) for w in wi_first]
        arrived = across(mine[1:])
        wi_own, wi_own1 = (jnp.stack([w[l] for w in [mine[0], *arrived]]) for l in range(2))
        wo_own, wo_own1 = wo_first
        wo_far, wo_near = flipped(wo_own, 8), flipped(wo_own, 1)
        wi_far, wi_near = flipped(after(wi_own, wo_far), 8), flipped(after(wi_own, wo_near), 1)
        wo_near_far = flipped(after(wo_far, wi_near), 1)
        small = after(small, arrived)
        small = jnp.stack([small, flipped(small, 8)])
        small = jnp.stack([small, flipped(small, 1)])
        extra = extra.at[1:9, :width_small].set(small.reshape(8, width_small))
        pack = jnp.concatenate([x0, extra])
        packs = [pack] + across([pack] * 3)
        g1s = [g1] + across(after([g1] * 3, packs))
        wo_far1, wi_far1 = flipped(after(wo_own1, wi_far), 8), flipped(after(wi_own1, wi_far), 8)

        held = jnp.stack([p[129:137, :width_small] for p in packs])
        held = held.reshape(16, 2 * width_small)
        index = jnp.arange(16)
        flip_of = jnp.bitwise_xor(index, me)
        at = (flip_of // 2) % 4 * 4 + (flip_of % 2) * 2 + flip_of // 8
        onehot = (at[:, None] == index[None, :]).astype(BF)
        everyone = mm(onehot, held).reshape(16, 2, width_small)
    else:
        w0, w1 = ([wi_both[l], wo_both[l]] for l in range(2))
        pack = jnp.concatenate([x0, extra])
        packs, g1s = [pack] + across([pack] * 3), [g1] + across([g1] * 3)
        everyone = lax.all_gather(small, "dp").astype(F32)

    def parts_in_place(value):
        return jnp.where(first_core, value, value[::-1]) if fast else value

    def small_of(layer):
        one = everyone[:, layer]
        vectors = [one[:, i * share : (i + 1) * share].reshape(1, D) for i in range(3)]
        b = one[:, 3 * share :].reshape(2, 4, FB)
        return *vectors, parts_in_place(lax.dynamic_index_in_dim(b, rank, 1, False))

    gain0, bias0, bfc0, bin0 = small_of(0)
    gain1, bias1, bfc1, bin1 = small_of(1)

    segs = jnp.stack([p[ROWS, :ROWS] for p in packs])
    row = lax.broadcasted_iota(jnp.int32, (ROWS, ROWS), 0)
    col = lax.broadcasted_iota(jnp.int32, (ROWS, ROWS), 1)
    mask = ((segs[:, :, None] == segs[:, None, :]) & (col <= row)).astype(F32)
    positions = jnp.sum(mask, -1).reshape(TOK, 1) - 1.0
    mask = jnp.stack([mask, mask], axis=1).reshape(8 * ROWS, ROWS)
    lane = jnp.arange(PAIR) % 64
    freq = jnp.where(lane < 32, 10000.0 ** (-(lane // 2 * 2).astype(F32) / 32), 0.0)
    angle = positions * freq
    cosine = jnp.cos(angle)
    sine = jnp.sin(angle) * jnp.where(lane % 2 == 0, -1.0, 1.0)

    if fast:
        tables = (gain0, bias0, bin0, cosine, sine, mask, gain1, bias1, bin1, bfc0, bfc1)
        wi_near_far = flipped(after(wi_far, wo_near_far), 1)
        wi_got = [wi_own, wi_far, wi_near, wi_near_far]
        w0 = join(after(wi_got, tables), [wo_own, wo_far, wo_near, wo_near_far], "join0")
        w0 = [w0, swap_core(after(w0, wo_far1, g1s))]
        wo_near1, wi_near1 = flipped(after(wo_own1, wi_near_far), 1), flipped(after(wi_own1, wi_near_far), 1)

    saved = [
        arr((TOK, A_COLS), BF),
        arr((2, TOK, 3 * PAIR), BF),
        arr((2, 8 * ROWS, ROWS), F32),
        arr((2, TOK, FB), F32),
    ]
    got = kernel_call(
        functools.partial(first_forward_kernel, fast, len(w0)),
        [*packs, gain0, bias0, bin0, cosine, sine, mask, *w0],
        partial_outs() + saved,
        cost=1,
        name="first_forward",
    )
    own, sends, (ship_a0, qkv0, probs0, pre0) = got[0], got[1:4], got[4:]

    def total(own, arrived):
        return sum([r.astype(F32) for r in arrived], own)

    arrived = across(sends)
    sums = total(own, arrived)
    if fast:
        wo_near_far1 = flipped(after(wo_far1, own, wo_near1), 1)
        wi_near_far1 = flipped(after(wi_far1, own, wi_near1), 1)
        w1 = join([wi_own1, wi_far1, wi_near1, wi_near_far1], [wo_own1, wo_far1, wo_near1, wo_near_far1], "join1")
        w1 = [w1]
    x1 = (x0.astype(F32) + sums + bfc0).astype(BF)
    x1s = [x1] + across([x1] * 3)

    back_outs = [arr((TOK, B_COLS), BF), arr((TOK, CI), BF), arr((2, FB), F32)]
    got = kernel_call(
        functools.partial(second_layer_kernel, fast, len(w1)),
        [*x1s, *g1s, gain1, bias1, bin1, cosine, sine, mask, *w1],
        partial_outs()
        + partial_outs()
        + [arr((TOK, A_COLS), BF)]
        + back_outs,
        scratch=[
            pltpu.VMEM((2, TOK, 3 * PAIR), BF),
            pltpu.VMEM((2, 8 * ROWS, ROWS), F32),
            pltpu.VMEM((2, TOK, FB), F32),
            pltpu.VMEM((TOK, D), BF),
        ],
        name="second_layer",
    )
    out_own, out_sends, gn_own, gn_sends = got[0], got[1:4], got[4], got[5:8]
    ship_a1, ship_b1, gcat1, gbin1 = got[8:]

    def norm_backward(own, arrived, x, gout, gain, name):
        return kernel_call(
            norm_backward_kernel,
            [own, *arrived, x, gout, gain],
            [arr((ROWS, D), F32), arr((ROWS, D), BF), arr((3, D), F32)],
            name=name,
        )

    def turned_ships(ship_a, other_a, name):
        outs = [arr((2, 512, 2 * TOK), BF), arr((2, 2, 320, 2 * TOK), BF)]
        return kernel_call(turn_kernel, [ship_a, other_a], outs, name=name) if fast else (ship_a, ship_a)

    def grads_out(gouts, left, other_b, extra, name):
        if fast:
            extras = [] if extra is None else [extra]
            return kernel_call(
                weight_grad_out_kernel,
                [*gouts, left, other_b, *extras],
                [arr((2, 320 + 16 * len(extras), 512), BF)] * 2,
                scratch=[pltpu.VMEM((TOK, 512), BF)],
                name=name,
            )
        scratch = [pltpu.VMEM((TOK, D), BF)]
        return kernel_call(whole_grad_out_kernel, [*gouts, left], [arr((2, RO, D), BF)], scratch=scratch, name=name)

    def grads_in(left, ship_b, other_b, gcat, name):
        if fast:
            return kernel_call(
                weight_grad_in_kernel, [left, gcat, other_b], [arr((2, 4, 64, CI), BF)] * 2, name=name
            )
        return kernel_call(whole_grad_in_kernel, [left, gcat, ship_b], [arr((2, D, CI), BF)], name=name)

    def onward(keep, near):
        return flipped((keep[1].astype(F32) + near[1].astype(F32)).astype(BF), 8)

    def reduced(keep, near, far):
        return keep[0].astype(F32) + near[0].astype(F32) + far.astype(F32)

    arrived_gn = across(gn_sends)
    other_a1, other_b1 = (swap_core(ship_a1), swap_core(ship_b1)) if fast else (None, None)
    other_a0 = swap_core(ship_a0) if fast else None
    left_in1, left_out1 = turned_ships(after(ship_a1, other_a0), other_a1, "turn1")
    go1 = grads_out(g1s, left_out1, other_b1, None, "grads1_out")
    _, g0, sums1 = norm_backward(after(gn_own, go1), arrived_gn, x1, g1, gain1, "norm_backward1")
    g0s = [g0] + across([g0] * 3)
    gi1 = grads_in(after(left_in1, g0), ship_b1, other_b1, gcat1, "grads1_in")
    left_in0, left_out0 = turned_ships(after(ship_a0, g0), other_a0, "turn0")
    if fast:
        keep1, send1 = zip(go1, gi1)
        near1 = [flipped(v, 1) for v in send1]
        far1 = [onward(k, v) for k, v in zip(keep1, near1)]
        g0s[0] = after(g0, near1[0], gi1, left_in0)

    got = kernel_call(
        functools.partial(first_backward_kernel, fast, len(w0)),
        [*g0s, cosine, sine, qkv0, probs0, pre0, *w0],
        partial_outs() + back_outs,
        scratch=[pltpu.VMEM((TOK, D), BF)],
        name="first_backward",
    )
    gn_own, gn_sends, (ship_b0, gcat0, gbin0) = got[0], got[1:4], got[4:]
    arrived_gn = across(gn_sends)
    if fast:
        other_b0 = swap_core(after(ship_b0, near1[1], far1[0]))
    else:
        other_b0 = None
    gi0 = grads_in(left_in0, ship_b0, other_b0, gcat0, "grads0_in")
    gx0, _, sums0 = norm_backward(after(gn_own, gi0), arrived_gn, x0, g0, gain0, "norm_backward0")

    out1 = x1.astype(F32) + total(out_own, across(after(out_sends, arrived_gn))) + bfc1

    def small_grads(sums, gbin):
        onehot = (jnp.arange(4) == rank).astype(F32)
        vectors = sums.reshape(3, 2, 4, spread, share).transpose(1, 2, 3, 0, 4).reshape(2, 4, spread, 3 * share)
        b = parts_in_place(gbin).reshape(2, 1, spread, 4 * share)
        return (vectors, b) if fast else jnp.concatenate([vectors, b * onehot[None, :, None, None]], axis=-1)

    both = jax.tree.map(choose, small_grads(sums0, gbin0), small_grads(sums1, gbin1))
    if fast:
        mine, theirs = (jnp.concatenate([v[i].reshape(-1) for v in both]) for i in range(2))
        mine = mine + swap_core(theirs)
        vectors, b = mine[: 3 * D].reshape(2, 4, 2, 192), mine[3 * D :].reshape(2, 1, 2, 256)
        values = jnp.concatenate([vectors.transpose(2, 0, 1, 3).reshape(2, 2, 768), b[:, 0].transpose(1, 0, 2)], axis=-1)
        values = jnp.where(me // 8 == 0, values, values[:, ::-1])
        values = jnp.where(me % 2 == 0, values, values[::-1])
        extra = jnp.zeros((2, 2, 16, 512), BF).at[:, :, :2].set(values.reshape(2, 2, 2, 512).astype(BF))
        wo_1, wi_1 = (reduced(*v).astype(BF) for v in zip(keep1, near1, far1))
        near_in0 = flipped(gi0[1], 1)
        far_in0 = onward(gi0[0], near_in0)
        extra = after(extra, wi_1, near_in0, out1)
    else:
        extra = None
    go0 = grads_out(g0s, left_out0, other_b0, extra, "grads0_out")

    arrived = swap_core(jnp.where(first_core, out1, gx0))
    boundary_out = jnp.where(first_core, jnp.stack([gx0, arrived]), jnp.stack([arrived, out1]))[None, :, None]
    if fast:
        near_out0 = flipped(go0[1], 1)
        far_out0 = onward(go0[0], near_out0)
        wo_0 = reduced(go0[0], near_out0, far_out0)
        wi_1 = after(wi_1, go0)
        wi_1 = [wi_1[0]] + across([wi_1[j] for j in range(1, 4)])
        wi_0 = after(reduced(gi0[0], near_in0, far_in0), wi_1)
        vector = wo_0[320:322].reshape(1024)
        ranks = vector[:768].reshape(4, 192)
        ranks = [lax.dynamic_index_in_dim(ranks, jnp.bitwise_xor(rank, j), 0, True) for j in range(4)]
        summed = sum([r.astype(F32) for r in across([r.astype(BF) for r in ranks[1:]])], ranks[0])
        vector = jnp.concatenate([summed, vector[None, 768:]], axis=1)
        wo_0, wi_0 = wo_0[:320].astype(BF), wi_0.astype(BF)
        wi_0 = [wi_0[0]] + across([wi_0[j] for j in range(1, 4)])
        wo_mine, wo_theirs = choose(wo_0, wo_1)
        pairs = [choose(a, b) for a, b in zip(wi_0, wi_1)]
        wi_other = swap_core(jnp.stack([p[1] for p in pairs]))
        g_qkv, g_out, g_in, g_fc = kernel_call(
            unpack_kernel,
            [*[p[0] for p in pairs], wi_other, wo_mine, swap_core(wo_theirs)],
            [arr((64, 3 * D), F32), arr((64, D), F32), arr((64, 4 * D), F32), arr((256, D), F32)],
            name="unpack",
        )
    else:
        vector = (both[0] + swap_core(both[1])).reshape(count, 7 * share)
        vector = lax.psum_scatter(vector, "dp", scatter_dimension=0, tiled=True)
        mine, theirs = choose(gi0[0], gi1[0])
        gi = mine.astype(F32) + swap_core(theirs).astype(F32)
        mine, theirs = choose(go0[0], go1[0])
        go = mine.astype(F32) + swap_core(theirs).astype(F32)
        g_qkv, g_out, g_in, g_fc = any_reduce(gi, go)
    g_gain, g_bias, g_bfc = (vector[:, i * share : (i + 1) * share] for i in range(3))
    g_bin = vector[:, 3 * share :]

    return (boundary_out, g_gain, g_bias, g_qkv[None], g_out[None], g_in[None], g_bin, g_fc[None], g_bfc)


def solution(mesh):
    rows = P("section", None, "dp", None, None)
    vector, matrix = P("section", "dp"), P("section", "dp", None)
    return jax.shard_map(
        body,
        mesh=mesh,
        in_specs=(rows, P(None, "dp", None), vector, vector, matrix, matrix, matrix, vector, matrix, vector),
        out_specs=(rows, vector, vector, matrix, matrix, matrix, vector, matrix, vector),
        check_vma=False,
    )
```

```python
import functools

import jax
import jax.numpy as jnp
from jax import lax
from jax.experimental import pallas as pl
from jax.experimental.pallas import tpu as pltpu
from jax.sharding import PartitionSpec as P

D = 1024
PAIR = 128
FB = 512
CI = 3 * PAIR + FB
RO = PAIR + FB
EPS = 1e-05
NEG = -1000000000.0
SCALE = 0.125
ROWS = 128
TOK = 4 * ROWS
BF = jnp.bfloat16
F32 = jnp.float32
SMALL, LARGE = 24, 56
GRANTS = {"join0": LARGE, "first_forward": LARGE, "first_backward": LARGE, "grads0_out": LARGE, "pack": LARGE, "norm_backward0": LARGE}


def mm(a, b):
    return lax.dot_general(a, b, (((1,), (0,)), ((), ())), preferred_element_type=F32)


def mm_nt(a, b):
    return lax.dot_general(a, b, (((1,), (1,)), ((), ())), preferred_element_type=F32)


def mm_tn(a, b):
    return lax.dot_general(a, b, (((0,), (0,)), ((), ())), preferred_element_type=F32)


def gelu(h):
    return 0.5 * h * (1.0 + jnp.tanh(0.7978845608 * (h + 0.044715 * h * h * h)))


def gelu_slope(h):
    th = jnp.tanh(0.7978845608 * (h + 0.044715 * h * h * h))
    inner = 0.7978845608 * (1.0 + 3 * 0.044715 * h * h)
    return 0.5 * (1.0 + th) + 0.5 * h * (1.0 - th * th) * inner


def partner(x):
    lane = lax.broadcasted_iota(jnp.int32, x.shape, 1)
    return jnp.where(lane % 2 == 0, pltpu.roll(x, PAIR - 1, 1), pltpu.roll(x, 1, 1))


def turned(x, cosine, sine):
    return x * cosine + partner(x) * sine


def by_head(x):
    lane = lax.broadcasted_iota(jnp.int32, (1, PAIR), 1)
    low = jnp.where(lane < 64, 1.0, 0.0).astype(x.dtype)
    high = jnp.where(lane < 64, 0.0, 1.0).astype(x.dtype)
    return jnp.concatenate([x * low, x * high], axis=0)


def beside(x):
    return jnp.concatenate([x[:ROWS], x[ROWS:]], axis=1)


def heads_of(x):
    return [x[ROWS * j : ROWS * (j + 1)] for j in range(4)]


def rows_of(j):
    return pl.ds(j * ROWS, ROWS)


def layer_norm_into(x_refs, gain_ref, bias_ref, normed):
    for j, x_ref in enumerate(x_refs):
        x = x_ref[0:ROWS, :].astype(F32)
        centered = x - jnp.mean(x, -1, keepdims=True)
        inv = lax.rsqrt(jnp.mean(centered * centered, -1, keepdims=True) + EPS)
        normed[rows_of(j), :] = (centered * inv * gain_ref[...] + bias_ref[...]).astype(BF)


def forward_in(g, normed, w, bin_ref, cos_ref, sin_ref, mask_ref, qkv, probs, oa, pre):
    w_qkv, w_in = w[g]
    y = mm(normed[...], w_qkv[...])
    cosine, sine = cos_ref[...], sin_ref[...]
    qkv[g, :, 0:PAIR] = turned(y[:, 0:PAIR], cosine, sine).astype(BF)
    qkv[g, :, PAIR : 2 * PAIR] = turned(y[:, PAIR : 2 * PAIR], cosine, sine).astype(BF)
    qkv[g, :, 2 * PAIR : 3 * PAIR] = y[:, 2 * PAIR : 3 * PAIR].astype(BF)
    q, k, v = (heads_of(qkv[g, :, i * PAIR : (i + 1) * PAIR]) for i in range(3))
    s = jnp.concatenate([mm_nt(by_head(q[j]), k[j]) for j in range(4)], axis=0) * SCALE
    s = jnp.where(mask_ref[...] > 0.5, s, NEG)
    e = jnp.exp(s - jnp.max(s, -1, keepdims=True))
    p = e / jnp.sum(e, -1, keepdims=True)
    probs[g] = p
    p = p.astype(BF)
    o = [mm(beside(p[2 * ROWS * j : 2 * ROWS * (j + 1)]), by_head(v[j])) for j in range(4)]
    oa[g][:, 0:PAIR] = jnp.concatenate(o, axis=0).astype(BF)
    h = mm(normed[...], w_in[...]) + bin_ref[g : g + 1, :]
    pre[g] = h
    oa[g][:, PAIR:RO] = gelu(h).astype(BF)


def forward_out(oa, w_out, outs):
    for (start, w0), (_, w1) in zip(*w_out):
        for n in range(2):
            part = mm(oa[0][...], w0[:, n * 256 : (n + 1) * 256]) + mm(oa[1][...], w1[:, n * 256 : (n + 1) * 256])
            cols = pl.ds(pl.multiple_of(start + n * 256, 256), 256)
            for j in range(4):
                outs[j][0:ROWS, cols] = part[j * ROWS : (j + 1) * ROWS].astype(outs[j].dtype)


def backward_out(g, gout, w_out, qkv, probs, pre, cos_ref, sin_ref, gcat, gbin_ref):
    halves = [(gout[:, pl.ds(start, 512)], w) for start, w in w_out[g]]
    go = sum(mm_nt(rows, w[0:PAIR, :]) for rows, w in halves).astype(BF)
    q, k, v = (heads_of(qkv[g, :, i * PAIR : (i + 1) * PAIR]) for i in range(3))
    cosine, sine = cos_ref[...], sin_ref[...]
    go = [by_head(rows) for rows in heads_of(go)]
    p = probs[g]
    gp = jnp.concatenate([mm_nt(go[j], v[j]) for j in range(4)], axis=0)
    gs = (p * (gp - jnp.sum(gp * p, -1, keepdims=True))).astype(BF)
    gs = [gs[2 * ROWS * j : 2 * ROWS * (j + 1)] for j in range(4)]
    p = p.astype(BF)
    gq = jnp.concatenate([mm(beside(gs[j]), by_head(k[j])) for j in range(4)], axis=0) * SCALE
    gk = jnp.concatenate([mm_tn(gs[j], by_head(q[j])) for j in range(4)], axis=0) * SCALE
    gv = jnp.concatenate([mm_tn(p[2 * ROWS * j : 2 * ROWS * (j + 1)], go[j]) for j in range(4)], axis=0)
    gcat[g][:, 0:PAIR] = turned(gq, cosine, -sine).astype(BF)
    gcat[g][:, PAIR : 2 * PAIR] = turned(gk, cosine, -sine).astype(BF)
    gcat[g][:, 2 * PAIR : 3 * PAIR] = gv.astype(BF)
    ga = sum(mm_nt(rows, w[PAIR:RO, :]) for rows, w in halves)
    gpre = (ga * gelu_slope(pre[g])).astype(BF)
    gcat[g][:, 3 * PAIR : CI] = gpre
    gbin_ref[g : g + 1, :] = jnp.sum(gpre.astype(F32), 0, keepdims=True)


def backward_in(gcat, w, outs):
    for n in range(4):
        cols = slice(n * 256, (n + 1) * 256)
        part = sum(
            mm_nt(gcat[g][:, 0 : 3 * PAIR], w[g][0][cols, :]) + mm_nt(gcat[g][:, 3 * PAIR : CI], w[g][1][cols, :])
            for g in range(2)
        )
        for j in range(4):
            outs[j][0:ROWS, cols] = part[j * ROWS : (j + 1) * ROWS].astype(outs[j].dtype)


A_COLS = D + 2 * RO
B_COLS = CI + 512


def views_a(ship_a):
    return ship_a.at[:, 0:D], (ship_a.at[:, D : D + RO], ship_a.at[:, D + RO : D + 2 * RO])


def views_b(ship_b):
    return ship_b.at[:, 0:CI], ship_b.at[:, CI : CI + 512]


HALF = (2 * D + 2 * RO, 512)


def weights_of(fast, refs):
    if not fast:
        wi, wo = refs
        ins = [(wi.at[g, :, 0 : 3 * PAIR], wi.at[g, :, 3 * PAIR : CI]) for g in range(2)]
        return ins, [[(0, wo.at[g, :, 0:512]), (512, wo.at[g, :, 512:1024])] for g in range(2)]
    core, halves = lax.axis_index("section"), refs
    starts = [pl.multiple_of(512 * c, 512) for c in (core, 1 - core)]
    rows = [pl.ds(pl.multiple_of(2 * D + RO * c, 128), RO) for c in (core, 1 - core)]
    ins = [(half.at[D : 2 * D, 0 : 3 * PAIR], half.at[0:D, :]) for half in halves]
    return ins, [[(start, half.at[rows[g], :]) for start, half in zip(starts, halves)] for g in range(2)]


def weight_loads(fast, refs, held, sems):
    if fast:
        core = lax.axis_index("section")
        halves = refs if len(refs) == 2 else [refs[0].at[core], refs[0].at[1 - core]]
        ins = [pltpu.make_async_copy(h.at[0 : 2 * D], v.at[0 : 2 * D], sems.at[i]) for i, (h, v) in enumerate(zip(halves, held))]
        end = 2 * D + 2 * RO
        outs = [
            pltpu.make_async_copy(h.at[2 * D : end], v.at[2 * D : end], sems.at[2 + i])
            for i, (h, v) in enumerate(zip(halves, held))
        ]
        return ins, outs
    ins = [pltpu.make_async_copy(refs[0].at[g], held[0].at[g], sems.at[g]) for g in range(2)]
    return ins, [pltpu.make_async_copy(refs[1], held[1], sems.at[2])]


def start(copies):
    for copy in copies:
        copy.start()
    return copies


def finish(copies):
    for copy in copies:
        copy.wait()


def moves(sources, targets, sems, first=0):
    return [pltpu.make_async_copy(a, b, sems.at[first + i]) for i, (a, b) in enumerate(zip(sources, targets))]


def place_of():
    return lax.axis_index("dp"), lax.axis_index("section")


def other_half(fast, gout, half_ref):
    core = lax.axis_index("section") if fast else 0
    half_ref[...] = gout[:, pl.ds(pl.multiple_of(512 * (1 - core), 512), 512)]


def join_kernel(own, far, near_own, near_far, *refs):
    pieces, joined, sems = refs[:-2], refs[-2], refs[-1]
    target = joined if len(joined.shape) == 2 else joined.at[0]
    me, _ = place_of()
    copies = []

    def copy(source, rows, cols=slice(None)):
        copies.append(pltpu.make_async_copy(source, target.at[rows, cols], sems.at[len(copies)]))
        copies[-1].start()

    for flip, piece in ((0, own), (8, far), (1, near_own), (9, near_far)):
        source = jnp.bitwise_xor(me, flip)
        g, r = source // 8, source % 2
        base = 2 * D + g * RO
        copy(piece.at[0:64], pl.ds(pl.multiple_of(base + 64 * r, 64), 64))
        copy(piece.at[64:320], pl.ds(pl.multiple_of(base + PAIR + 256 * r, 128), 256))
    blocks = [(ref, i) for ref in pieces for i in range(ref.shape[0])]
    for (ref, i), flip in zip(blocks, [f ^ (2 * j) for f in (0, 8, 1, 9) for j in range(4)]):
        start = pl.multiple_of(jnp.bitwise_xor(me, flip) * 64, 64)
        copy(ref.at[i, :, 3 * PAIR : CI], pl.ds(start, 64))
        copy(ref.at[i, :, 0 : 3 * PAIR], pl.ds(D + start, 64), slice(0, 3 * PAIR))
    for one in copies:
        one.wait()
    if len(joined.shape) == 3:
        joined[1] = joined[0]


def first_forward_kernel(fast, n_w, *refs):
    x_refs, (gain, bias, bin_ref, cos_ref, sin_ref, mask_ref), refs = refs[:4], refs[4:10], refs[10:]
    w_refs, outs, saved, refs = refs[:n_w], refs[n_w : n_w + 4], refs[n_w + 4 : n_w + 8], refs[n_w + 8 :]
    w_held, held, (w_sems, sems) = refs[:2], refs[2:6], refs[6:]
    loads_in, loads_out = weight_loads(fast, w_refs, w_held, w_sems)
    start(loads_in + loads_out)
    w_in, w_out = weights_of(fast, w_held)
    ship_a, qkv, probs, pre = held
    normed, oa = views_a(ship_a)
    layer_norm_into(x_refs, gain, bias, normed)
    puts = []
    for g in range(2):
        finish(loads_in[g : g + 1])
        forward_in(g, normed, w_in, bin_ref, cos_ref, sin_ref, mask_ref, qkv, probs, oa, pre)
        puts += start(moves([h.at[g] for h in held[1:]], [h.at[g] for h in saved[1:]], sems, 1 + 3 * g))
    puts += start(moves(held[:1], saved[:1], sems))
    finish(loads_out)
    forward_out(oa, w_out, outs)
    finish(puts)


def second_layer_kernel(fast, n_w, *refs):
    x_refs, gout_refs, refs = refs[:4], refs[4:8], refs[8:]
    (gain, bias, bin_ref, cos_ref, sin_ref, mask_ref), refs = refs[:6], refs[6:]
    w_refs, refs = refs[:n_w], refs[n_w:]
    if fast:
        core = lax.axis_index("section")
        w_refs = [w_refs[0].at[core], w_refs[0].at[1 - core]]
    w_in, w_out = weights_of(fast, w_refs)
    outs, gouts, gbin_ref, refs = refs[:4], refs[4:8], refs[8], refs[9:]
    ship_a, ship_b, gcat0, qkv, probs, pre, gout = refs
    normed, oa = views_a(ship_a)
    gcat1, gout_half = views_b(ship_b)
    gcat = (gcat0, gcat1)
    layer_norm_into(x_refs, gain, bias, normed)
    for j in range(4):
        gout[rows_of(j), :] = gout_refs[j][...]
    other_half(fast, gout, gout_half)
    for g in range(2):
        forward_in(g, normed, w_in, bin_ref, cos_ref, sin_ref, mask_ref, qkv, probs, oa, pre)
    for g in range(2):
        backward_out(g, gout, w_out, qkv, probs, pre, cos_ref, sin_ref, gcat, gbin_ref)
    backward_in(gcat, w_in, gouts)
    forward_out(oa, w_out, outs)


def first_backward_kernel(fast, n_w, *refs):
    gout_refs, (cos_ref, sin_ref), saved, refs = refs[:4], refs[4:6], refs[6:9], refs[9:]
    w_refs, refs = refs[:n_w], refs[n_w:]
    gouts, gbin_ref, put_refs, refs = refs[:4], refs[4], refs[5:7], refs[7:]
    w_held, held, (ship_b, gcat0, gout, w_sems, sems) = refs[:2], refs[2:5], refs[5:]
    loads_in, loads_out = weight_loads(fast, w_refs, w_held, w_sems)
    loads = [moves([h.at[g] for h in saved], [h.at[g] for h in held], sems, 3 * g) for g in range(2)]
    start(loads_out + loads[0] + loads[1] + loads_in)
    w_in, w_out = weights_of(fast, w_held)
    gcat1, gout_half = views_b(ship_b)
    gcat = (gcat0, gcat1)
    for j in range(4):
        gout[rows_of(j), :] = gout_refs[j][...]
    other_half(fast, gout, gout_half)
    finish(loads_out)
    for g in range(2):
        finish(loads[g])
        backward_out(g, gout, w_out, *held, cos_ref, sin_ref, gcat, gbin_ref)
    puts = start(moves([ship_b, gcat0], put_refs, sems, 6))
    finish(loads_in)
    backward_in(gcat, w_in, gouts)
    finish(puts)


def turn_kernel(ship_a, other_a, put_in, put_out, held_a, held_b, left_in, left_out, sems):
    me, core = place_of()
    g, t, r = me // 8, (me // 2) % 4, me % 2
    loads = start(moves([ship_a, other_a], [held_a, held_b], sems))
    for side, ship in enumerate((held_a, held_b)):
        tokens = slice(side * TOK, (side + 1) * TOK)
        finish(loads[side : side + 1])
        for part in range(2):
            far = jnp.bitwise_xor(g, jnp.bitwise_xor(core, part ^ side))
            flat = ship[:, D + part * RO : D + (part + 1) * RO].T
            for s in range(2):
                near = jnp.bitwise_xor(r, s)
                left_out[near, far, 0:64, tokens] = flat[64 * s : 64 * s + 64]
                left_out[near, far, 64:320, tokens] = flat[PAIR + 256 * s : PAIR + 256 * (s + 1)]
        for far in range(2):
            for j in range(4):
                pair = jnp.bitwise_xor(g, far) * 4 + jnp.bitwise_xor(t, j)
                block = ship[:, pl.ds(pl.multiple_of(pair * PAIR, PAIR), PAIR)].T
                start_row = far * 256 + 64 * j
                for s in range(2):
                    left_in[jnp.bitwise_xor(r, s), start_row : start_row + 64, tokens] = block[64 * s : 64 * s + 64]
    finish(start(moves([left_in, left_out], [put_in, put_out], sems, 2)))


def weight_grad_out_kernel(*refs):
    gout_refs, refs = refs[:4], refs[4:]
    *extras, left_ref, other_b, keep, send, left, right, right_other, sems = refs
    loads = start(
        moves([other_b.at[:, CI : CI + 512], left_ref.at[1], left_ref.at[0]], [right_other, left.at[1], left.at[0]], sems)
    )
    cols = pl.ds(pl.multiple_of(512 * lax.axis_index("section"), 512), 512)
    for j in range(4):
        right[rows_of(j), :] = gout_refs[j][:, cols]
    finish(loads[:1])
    for near, out in ((1, send), (0, keep)):
        finish(loads[2 - near : 3 - near])
        for far in range(2):
            part = mm(left[near, far, :, 0:TOK], right[...]) + mm(left[near, far, :, TOK : 2 * TOK], right_other[...])
            out[far, 0:320, :] = part.astype(BF)
            for extra in extras:
                out[far, 320:336, :] = extra[near, far]


def weight_grad_in_kernel(left_ref, gcat, other_b, keep, send, left, right, right_other, sems):
    sources = [gcat, left_ref.at[1], other_b.at[:, 0:CI], left_ref.at[0]]
    loads = start(moves(sources, [right, left.at[1], right_other, left.at[0]], sems))
    finish(loads[:3])
    for near, out in ((1, send), (0, keep)):
        if near == 0:
            finish(loads[3:])
        part = mm(left[near, :, 0:TOK], right[...]) + mm(left[near, :, TOK : 2 * TOK], right_other[...])
        part = part.astype(BF)
        for i in range(8):
            out[i // 4, i % 4] = part[64 * i : 64 * i + 64]


def whole_grad_out_kernel(*refs):
    gout_refs, (ship_a, out, gout) = refs[:4], refs[4:]
    for j in range(4):
        gout[rows_of(j), :] = gout_refs[j][...]
    for g in range(2):
        out[g] = mm_tn(ship_a[:, D + g * RO : D + (g + 1) * RO], gout[...]).astype(BF)


def whole_grad_in_kernel(ship_a, gcat0, ship_b, out):
    for g in range(2):
        right = gcat0[...] if g == 0 else ship_b[:, 0:CI]
        for m in range(4):
            rows = slice(m * 256, (m + 1) * 256)
            out[g, rows, :] = mm_tn(ship_a[:, rows], right).astype(BF)


def norm_backward_kernel(own, r1, r2, r3, x_ref, gout_ref, gain, gx_ref, low_ref, sums_ref):
    x = x_ref[0:ROWS, :].astype(F32)
    gn = own[...] + sum(r[...].astype(F32) for r in (r1, r2, r3))
    gout = gout_ref[...].astype(F32)
    centered = x - jnp.mean(x, -1, keepdims=True)
    inv = lax.rsqrt(jnp.mean(centered * centered, -1, keepdims=True) + EPS)
    unit = centered * inv
    gu = gn * gain[...]
    gx = gout + inv * (gu - jnp.mean(gu, -1, keepdims=True) - unit * jnp.mean(gu * unit, -1, keepdims=True))
    gx_ref[...] = gx
    low_ref[...] = gx.astype(BF)
    sums_ref[0:1, :] = jnp.sum(gn * unit, 0, keepdims=True)
    sums_ref[1:2, :] = jnp.sum(gn, 0, keepdims=True)
    sums_ref[2:3, :] = jnp.sum(gout, 0, keepdims=True)


def pack_kernel(w_qkv, w_out, w_in, w_fc, wi_keep, wi_send, wo_keep, wo_send):
    t, core = (lax.axis_index("dp") // 2) % 4, lax.axis_index("section")
    for ref, g in ((wi_keep, core), (wi_send, 1 - core)):
        for j in range(4):
            rank = jnp.bitwise_xor(t, j)
            for part in range(3):
                start = pl.multiple_of(part * D + g * 512 + rank * PAIR, PAIR)
                ref[j, :, part * PAIR : (part + 1) * PAIR] = w_qkv[:, pl.ds(start, PAIR)].astype(BF)
            start = pl.multiple_of(g * 2048 + rank * FB, FB)
            ref[j, :, 3 * PAIR : CI] = w_in[:, pl.ds(start, FB)].astype(BF)
    for ref, half in ((wo_keep, core), (wo_send, 1 - core)):
        cols = pl.ds(pl.multiple_of(512 * half, 512), 512)
        ref[0:64, :] = w_out[:, cols].astype(BF)
        ref[64:320, :] = w_fc[:, cols].astype(BF)


def unpack_kernel(own0, own1, own2, own3, other, wo_own, wo_other, g_qkv, g_out, g_in, g_fc):
    t, core = (lax.axis_index("dp") // 2) % 4, lax.axis_index("section")
    for side, g in ((0, core), (1, 1 - core)):
        for j in range(4):
            block = (own0, own1, own2, own3)[j][...] if side == 0 else other[j]
            block = block.astype(F32)
            rank = jnp.bitwise_xor(t, j)
            for part in range(3):
                start = pl.multiple_of(part * D + g * 512 + rank * PAIR, PAIR)
                g_qkv[:, pl.ds(start, PAIR)] = block[:, part * PAIR : (part + 1) * PAIR]
            start = pl.multiple_of(g * 2048 + rank * FB, FB)
            g_in[:, pl.ds(start, FB)] = block[:, 3 * PAIR : CI]
    for ref, half in ((wo_own, core), (wo_other, 1 - core)):
        cols = pl.ds(pl.multiple_of(512 * half, 512), 512)
        g_out[:, cols] = ref[0:64, :].astype(F32)
        g_fc[:, cols] = ref[64:320, :].astype(F32)


VM = pl.BlockSpec(memory_space=pltpu.VMEM)


HB = pl.BlockSpec(memory_space=pl.ANY)


def kernel_call(kernel, args, outs, hbm_args=0, hbm_outs=0, scratch=(), cost=2e10, name=None):
    return pl.pallas_call(
        kernel,
        out_shape=outs,
        in_specs=[VM] * (len(args) - hbm_args) + [HB] * hbm_args,
        out_specs=[VM] * (len(outs) - hbm_outs) + [HB] * hbm_outs,
        scratch_shapes=list(scratch),
        compiler_params=pltpu.CompilerParams(vmem_limit_bytes=GRANTS.get(name, SMALL) * 1024 * 1024),
        cost_estimate=pl.CostEstimate(flops=int(cost), bytes_accessed=1, transcendentals=0),
        name=name,
    )(*args)


def dma(count):
    return pltpu.SemaphoreType.DMA((count,))


def arr(shape, dtype):
    return jax.ShapeDtypeStruct(shape, dtype)


def partial_outs():
    return [arr((ROWS, D), F32)] + [arr((ROWS, D), BF)] * 3


def swap_core(value):
    return lax.ppermute(value, "section", [(0, 1), (1, 0)])


def flipped(value, flip):
    count = lax.axis_size("dp")
    return lax.ppermute(value, "dp", [(i, i ^ flip) for i in range(count)])


def after(value, *earlier):
    return lax.optimization_barrier((value, earlier))[0]


def choose(own, other):
    first_core = lax.axis_index("section") == 0
    return jnp.where(first_core, own, other), jnp.where(first_core, other, own)


def across(values):
    spread = lax.axis_size("dp") // 8
    return [flipped(v, (j + 1) * spread) for j, v in enumerate(values)]


def groups_of(spread):
    places = [[[g * 4 * spread + t * spread + r for r in range(spread)] for t in range(4)] for g in range(2)]
    t_groups = [[places[g][t][r] for t in range(4)] for g in range(2) for r in range(spread)]
    f_groups = [[places[g][t][r] for g in range(2) for r in range(spread)] for t in range(4)]
    return t_groups, f_groups


def any_gather(w_qkv, w_out, w_in, w_fc):
    share, spread = w_qkv.shape[0], lax.axis_size("dp") // 8
    t_groups, f_groups = groups_of(spread)
    qkv = w_qkv.reshape(share, 3, 2, 4, PAIR).transpose(3, 0, 2, 1, 4).reshape(4, share, 2, 3 * PAIR)
    wi = jnp.concatenate([qkv, w_in.reshape(share, 2, 4, FB).transpose(2, 0, 1, 3)], axis=-1).astype(BF)
    wi = lax.all_to_all(wi, "dp", 0, 0, axis_index_groups=t_groups, tiled=True)
    wi = lax.all_gather(wi, "dp", axis_index_groups=f_groups)
    wi = wi.reshape(2, spread, 4, share, 2, CI).transpose(4, 0, 2, 1, 3, 5).reshape(2, D, CI)
    wo = lax.all_gather(w_out.astype(BF), "dp", axis_index_groups=f_groups).reshape(2, PAIR, D)
    wf = lax.all_gather(w_fc.astype(BF), "dp", axis_index_groups=f_groups).reshape(2, FB, D)
    wo = jnp.concatenate([wo, wf], axis=1)
    return choose(wi, swap_core(wi)), choose(wo, swap_core(wo))


def any_reduce(gi, go):
    count = lax.axis_size("dp")
    spread, share = count // 8, D // count
    t_groups, f_groups = groups_of(spread)

    def scattered(value):
        return lax.psum_scatter(value, "dp", scatter_dimension=0, axis_index_groups=f_groups)

    gi = gi.reshape(2, 2, 4, spread, share, CI).transpose(1, 3, 2, 4, 0, 5).reshape(2 * spread, 4, share, 2, CI)
    gi = lax.all_to_all(scattered(gi), "dp", 0, 0, axis_index_groups=t_groups, tiled=True)
    g_qkv = gi[..., : 3 * PAIR].reshape(4, share, 2, 3, PAIR).transpose(1, 3, 2, 0, 4).reshape(share, 3 * D)
    g_in = gi[..., 3 * PAIR :].transpose(1, 2, 0, 3).reshape(share, 4 * D)
    g_out = scattered(go[:, :PAIR].reshape(2 * spread, share, D))
    g_fc = scattered(go[:, PAIR:].reshape(2 * spread, 4 * share, D))
    return g_qkv, g_out, g_in, g_fc


def body(boundary, segments, ln_gain, ln_bias, w_qkv, w_out, w_in, b_in, w_fc, b_fc):
    core, me = lax.axis_index("section"), lax.axis_index("dp")
    count = lax.axis_size("dp")
    fast = count == 16
    spread = count // 8
    rank = (me // spread) % 4
    share = D // count
    width_small = 7 * share
    first_core = core == 0

    if fast:
        small = jnp.concatenate([ln_gain, ln_bias, b_fc, b_in], axis=-1).astype(BF)
        small = jnp.concatenate([small, flipped(small, 8)])
        small = jnp.concatenate([small, flipped(small, 1)])
        small = jnp.stack(choose(small, swap_core(small)), axis=1).reshape(8, width_small)

    if fast:
        wi_keep, wi_send, wo_keep, wo_send = kernel_call(
            pack_kernel,
            [w_qkv[0], w_out[0], w_in[0], w_fc[0]],
            [arr((4, 64, CI), BF), arr((4, 64, CI), BF), arr((320, 512), BF), arr((320, 512), BF)],
            name="pack",
        )
        wi_recv, wo_recv = swap_core(wi_send), swap_core(wo_send)
        wi_first = [choose(wi_keep[j], wi_recv[j]) for j in range(4)]
        wo_first = choose(wo_keep, wo_recv)
        boundary, segments = after((boundary, segments), wi_keep)
    else:
        wi_both, wo_both = any_gather(w_qkv[0], w_out[0], w_in[0], w_fc[0])

    swapped = swap_core(lax.dynamic_index_in_dim(boundary[0], 1 - core, 0, False)[0])
    kept = lax.dynamic_index_in_dim(boundary[0], core, 0, False)[0]
    x0, g1 = choose(kept, swapped)
    if not fast:
        small = jnp.concatenate([ln_gain, ln_bias, b_fc, b_in], axis=-1).astype(BF)
        small = jnp.concatenate(choose(small, swap_core(small)))
    seg = lax.dynamic_index_in_dim(segments, core, 0, False)[0].astype(BF)
    extra = jnp.zeros((16, D), BF).at[0, :ROWS].set(seg)
    if fast:

        def join(wi_pieces, wo_pieces, name):
            pieces, sems = [*wo_pieces, *wi_pieces], [pltpu.SemaphoreType.DMA((40,))]
            if name == "join0":
                own = kernel_call(join_kernel, pieces, [arr(HALF, BF)], 8, 0, sems, 1, name)[0]
                return own
            both = kernel_call(join_kernel, pieces, [arr((2, *HALF), BF)], 8, 0, sems, 1, name)[0]
            return lax.all_to_all(both, "section", 0, 0, tiled=True)

        mine = [after(jnp.stack(w), wo_first) for w in wi_first]
        arrived = across(mine[1:])
        wi_own, wi_own1 = (jnp.stack([w[l] for w in [mine[0], *arrived]]) for l in range(2))
        wo_own, wo_own1 = wo_first
        wo_far, wo_near = flipped(wo_own, 8), flipped(wo_own, 1)
        wi_far, wi_near = flipped(after(wi_own, wo_far), 8), flipped(wi_own, 1)
        wo_near_far = flipped(wo_far, 1)
        extra = extra.at[1:9, :width_small].set(small)
        pack = jnp.concatenate([x0, extra])
        packs = [pack] + across(after([pack] * 3, arrived))
        g1s = [g1] + across(after([g1] * 3, packs))
        wo_far1, wi_far1 = flipped(after(wo_own1, wi_far), 8), flipped(after(wi_own1, wi_far), 8)

        held = jnp.stack([p[129:137, :width_small] for p in packs])
        held = held.reshape(16, 2 * width_small)
        index = jnp.arange(16)
        flip_of = jnp.bitwise_xor(index, me)
        at = (flip_of // 2) % 4 * 4 + (flip_of % 2) * 2 + flip_of // 8
        onehot = (at[:, None] == index[None, :]).astype(BF)
        everyone = mm(onehot, held).reshape(16, 2, width_small)
    else:
        w0, w1 = ([wi_both[l], wo_both[l]] for l in range(2))
        pack = jnp.concatenate([x0, extra])
        packs, g1s = [pack] + across([pack] * 3), [g1] + across([g1] * 3)
        everyone = lax.all_gather(small, "dp").astype(F32)

    def parts_in_place(value):
        return jnp.where(first_core, value, value[::-1]) if fast else value

    def small_of(layer):
        one = everyone[:, layer]
        vectors = [one[:, i * share : (i + 1) * share].reshape(1, D) for i in range(3)]
        b = one[:, 3 * share :].reshape(2, 4, FB)
        return *vectors, parts_in_place(lax.dynamic_index_in_dim(b, rank, 1, False))

    gain0, bias0, bfc0, bin0 = small_of(0)
    gain1, bias1, bfc1, bin1 = small_of(1)

    segs = jnp.stack([p[ROWS, :ROWS] for p in packs])
    row = lax.broadcasted_iota(jnp.int32, (ROWS, ROWS), 0)
    col = lax.broadcasted_iota(jnp.int32, (ROWS, ROWS), 1)
    mask = ((segs[:, :, None] == segs[:, None, :]) & (col <= row)).astype(F32)
    positions = jnp.sum(mask, -1).reshape(TOK, 1) - 1.0
    mask = jnp.stack([mask, mask], axis=1).reshape(8 * ROWS, ROWS)
    lane = jnp.arange(PAIR) % 64
    freq = jnp.where(lane < 32, 10000.0 ** (-(lane // 2 * 2).astype(F32) / 32), 0.0)
    angle = positions * freq
    cosine = jnp.cos(angle)
    sine = jnp.sin(angle) * jnp.where(lane % 2 == 0, -1.0, 1.0)

    if fast:
        tables = (gain0, bias0, bin0, cosine, sine, mask, gain1, bias1, bin1, bfc0, bfc1)
        wi_near_far = flipped(after(wi_far, wo_near_far, wi_near, wo_near), 1)
        wi_got = [wi_own, wi_far, wi_near, wi_near_far]
        w0 = join(after(wi_got, tables), [wo_own, wo_far, wo_near, wo_near_far], "join0")
        w0 = [w0, swap_core(after(w0, wo_far1, g1s))]
        wo_near1, wi_near1 = flipped(after(wo_own1, wi_near_far), 1), flipped(after(wi_own1, wi_near_far), 1)

    held_weights = [pltpu.VMEM(HALF, BF)] * 2 if fast else [pltpu.VMEM((2, D, CI), BF), pltpu.VMEM((2, RO, D), BF)]

    saved = [
        arr((TOK, A_COLS), BF),
        arr((2, TOK, 3 * PAIR), BF),
        arr((2, 8 * ROWS, ROWS), F32),
        arr((2, TOK, FB), F32),
    ]
    got = kernel_call(
        functools.partial(first_forward_kernel, fast, len(w0)),
        [*packs, gain0, bias0, bin0, cosine, sine, mask, *w0],
        partial_outs() + saved,
        hbm_args=2,
        hbm_outs=4,
        scratch=[*held_weights, *(pltpu.VMEM(a.shape, a.dtype) for a in saved), dma(4), dma(7)],
        cost=1,
        name="first_forward",
    )
    own, sends, (ship_a0, qkv0, probs0, pre0) = got[0], got[1:4], got[4:]

    def total(own, arrived):
        return sum([r.astype(F32) for r in arrived], own)

    arrived = across(sends)
    sums = total(own, arrived)
    if fast:
        wo_near_far1 = flipped(after(wo_far1, own, wo_near1), 1)
        wi_near_far1 = flipped(after(wi_far1, own, wi_near1), 1)
        w1 = join([wi_own1, wi_far1, wi_near1, wi_near_far1], [wo_own1, wo_far1, wo_near1, wo_near_far1], "join1")
        w1 = [w1]
    x1 = (x0.astype(F32) + sums + bfc0).astype(BF)
    x1s = [x1] + across([x1] * 3)

    back_outs = [arr((TOK, B_COLS), BF), arr((TOK, CI), BF)]
    got = kernel_call(
        functools.partial(second_layer_kernel, fast, len(w1)),
        [*x1s, *g1s, gain1, bias1, bin1, cosine, sine, mask, *w1],
        [*partial_outs(), *partial_outs(), arr((2, FB), F32), arr((TOK, A_COLS), BF), *back_outs],
        scratch=[*(pltpu.VMEM(a.shape, a.dtype) for a in saved[1:]), pltpu.VMEM((TOK, D), BF)],
        name="second_layer",
    )
    out_own, out_sends, gn_own, gn_sends = got[0], got[1:4], got[4], got[5:8]
    gbin1, ship_a1, ship_b1, gcat1 = got[8:]

    def norm_backward(own, arrived, x, gout, gain, name):
        return kernel_call(
            norm_backward_kernel,
            [own, *arrived, x, gout, gain],
            [arr((ROWS, D), F32), arr((ROWS, D), BF), arr((3, D), F32)],
            name=name,
        )

    def turned_ships(ship_a, other_a, name):
        outs = [arr((2, 512, 2 * TOK), BF), arr((2, 2, 320, 2 * TOK), BF)]
        if not fast:
            return ship_a, ship_a
        scratch = [pltpu.VMEM((TOK, A_COLS), BF)] * 2 + [pltpu.VMEM(a.shape, BF) for a in outs] + [dma(4)]
        return kernel_call(turn_kernel, [ship_a, other_a], outs, 2, 2, scratch, name=name)

    def grads_out(gouts, left, other_b, extra, name):
        if fast:
            extras = [] if extra is None else [extra]
            return kernel_call(
                weight_grad_out_kernel,
                [*gouts, *extras, left, other_b],
                [arr((2, 320 + 16 * len(extras), 512), BF)] * 2,
                hbm_args=2,
                scratch=[pltpu.VMEM(left.shape, BF), pltpu.VMEM((TOK, 512), BF), pltpu.VMEM((TOK, 512), BF), dma(3)],
                name=name,
            )
        scratch = [pltpu.VMEM((TOK, D), BF)]
        return kernel_call(whole_grad_out_kernel, [*gouts, left], [arr((2, RO, D), BF)], scratch=scratch, name=name)

    def grads_in(left, ship_b, other_b, gcat, name):
        if fast:
            scratch = [pltpu.VMEM(left.shape, BF), pltpu.VMEM((TOK, CI), BF), pltpu.VMEM((TOK, CI), BF), dma(4)]
            outs = [arr((2, 4, 64, CI), BF)] * 2
            return kernel_call(weight_grad_in_kernel, [left, gcat, other_b], outs, 3, 0, scratch, name=name)
        return kernel_call(whole_grad_in_kernel, [left, gcat, ship_b], [arr((2, D, CI), BF)], name=name)

    def onward(keep, near):
        return flipped((keep[1].astype(F32) + near[1].astype(F32)).astype(BF), 8)

    def reduced(keep, near, far):
        return keep[0].astype(F32) + near[0].astype(F32) + far.astype(F32)

    arrived_gn = across(gn_sends)
    other_a1, other_b1 = (swap_core(ship_a1), swap_core(ship_b1)) if fast else (None, None)
    other_a0 = swap_core(ship_a0) if fast else None
    left_in1, left_out1 = turned_ships(after(ship_a1, other_a0), other_a1, "turn1")
    go1 = grads_out(g1s, left_out1, other_b1, None, "grads1_out")
    _, g0, sums1 = norm_backward(after(gn_own, go1), arrived_gn, x1, g1, gain1, "norm_backward1")
    g0s = [g0] + across([g0] * 3)
    gi1 = grads_in(after(left_in1, g0), ship_b1, other_b1, gcat1, "grads1_in")
    left_in0, left_out0 = turned_ships(after(ship_a0, g0), other_a0, "turn0")
    if fast:
        keep1, send1 = zip(go1, gi1)
        near1 = [flipped(v, 1) for v in send1]
        far1 = [onward(k, v) for k, v in zip(keep1, near1)]
        g0s[0] = after(g0, near1[0], gi1, left_in0)

    got = kernel_call(
        functools.partial(first_backward_kernel, fast, len(w0)),
        [*g0s, cosine, sine, qkv0, probs0, pre0, *w0],
        [*partial_outs(), arr((2, FB), F32), *back_outs],
        hbm_args=5,
        hbm_outs=2,
        scratch=[
            *held_weights,
            *(pltpu.VMEM(a.shape, a.dtype) for a in saved[1:]),
            *(pltpu.VMEM((TOK, cols), BF) for cols in (B_COLS, CI, D)),
            dma(4),
            dma(8),
        ],
        name="first_backward",
    )
    gn_own, gn_sends, (gbin0, ship_b0, gcat0) = got[0], got[1:4], got[4:]
    arrived_gn = across(gn_sends)
    if fast:
        other_b0 = swap_core(after(ship_b0, near1[1], far1[0]))
    else:
        other_b0 = None
    gi0 = grads_in(left_in0, ship_b0, other_b0, gcat0, "grads0_in")
    gx0, _, sums0 = norm_backward(after(gn_own, gi0), arrived_gn, x0, g0, gain0, "norm_backward0")

    def small_grads(sums, gbin):
        onehot = (jnp.arange(4) == rank).astype(F32)
        vectors = sums.reshape(3, 2, 4, spread, share).transpose(1, 2, 3, 0, 4).reshape(2, 4, spread, 3 * share)
        b = parts_in_place(gbin).reshape(2, 1, spread, 4 * share)
        return (vectors, b) if fast else jnp.concatenate([vectors, b * onehot[None, :, None, None]], axis=-1)

    both = jax.tree.map(choose, small_grads(sums0, gbin0), small_grads(sums1, gbin1))
    if fast:
        mine, theirs = (jnp.concatenate([v[i].reshape(-1) for v in both]) for i in range(2))
        mine = mine + swap_core(theirs)
        vectors, b = mine[: 3 * D].reshape(2, 4, 2, 192), mine[3 * D :].reshape(2, 1, 2, 256)
        values = jnp.concatenate([vectors.transpose(2, 0, 1, 3).reshape(2, 2, 768), b[:, 0].transpose(1, 0, 2)], axis=-1)
        values = jnp.where(me // 8 == 0, values, values[:, ::-1])
        values = jnp.where(me % 2 == 0, values, values[::-1])
        extra = jnp.zeros((2, 2, 16, 512), BF).at[:, :, :2].set(values.reshape(2, 2, 2, 512).astype(BF))
        wo_1, wi_1 = (reduced(*v).astype(BF) for v in zip(keep1, near1, far1))
        near_in0 = flipped(gi0[1], 1)
        far_in0 = onward(gi0[0], near_in0)
        extra = after(extra, wi_1, near_in0)
    else:
        extra = None
    go0 = grads_out(g0s, left_out0, other_b0, extra, "grads0_out")

    out1 = x1.astype(F32) + total(out_own, across(after(out_sends, go0))) + bfc1
    arrived = swap_core(jnp.where(first_core, out1, gx0))
    boundary_out = jnp.where(first_core, jnp.stack([gx0, arrived]), jnp.stack([arrived, out1]))[None, :, None]
    if fast:
        near_out0 = flipped(go0[1], 1)
        far_out0 = onward(go0[0], near_out0)
        wo_0 = reduced(go0[0], near_out0, far_out0)
        wi_1 = after(wi_1, out1)
        wi_1 = [wi_1[0]] + across([wi_1[j] for j in range(1, 4)])
        wi_0 = after(reduced(gi0[0], near_in0, far_in0), wi_1)
        vector = wo_0[320:322].reshape(1024)
        ranks = vector[:768].reshape(4, 192)
        ranks = [lax.dynamic_index_in_dim(ranks, jnp.bitwise_xor(rank, j), 0, True) for j in range(4)]
        summed = sum([r.astype(F32) for r in across([r.astype(BF) for r in ranks[1:]])], ranks[0])
        vector = jnp.concatenate([summed, vector[None, 768:]], axis=1)
        wo_0, wi_0 = wo_0[:320].astype(BF), wi_0.astype(BF)
        wi_0 = [wi_0[0]] + across([wi_0[j] for j in range(1, 4)])
        wo_mine, wo_theirs = choose(wo_0, wo_1)
        pairs = [choose(a, b) for a, b in zip(wi_0, wi_1)]
        wi_other = swap_core(jnp.stack([p[1] for p in pairs]))
        g_qkv, g_out, g_in, g_fc = kernel_call(
            unpack_kernel,
            [*[p[0] for p in pairs], wi_other, wo_mine, swap_core(wo_theirs)],
            [arr((64, 3 * D), F32), arr((64, D), F32), arr((64, 4 * D), F32), arr((256, D), F32)],
            name="unpack",
        )
    else:
        vector = (both[0] + swap_core(both[1])).reshape(count, 7 * share)
        vector = lax.psum_scatter(vector, "dp", scatter_dimension=0, tiled=True)
        mine, theirs = choose(gi0[0], gi1[0])
        gi = mine.astype(F32) + swap_core(theirs).astype(F32)
        mine, theirs = choose(go0[0], go1[0])
        go = mine.astype(F32) + swap_core(theirs).astype(F32)
        g_qkv, g_out, g_in, g_fc = any_reduce(gi, go)
    g_gain, g_bias, g_bfc = (vector[:, i * share : (i + 1) * share] for i in range(3))
    g_bin = vector[:, 3 * share :]

    return (boundary_out, g_gain, g_bias, g_qkv[None], g_out[None], g_in[None], g_bin, g_fc[None], g_bfc)


def solution(mesh):
    rows = P("section", None, "dp", None, None)
    vector, matrix = P("section", "dp"), P("section", "dp", None)
    return jax.shard_map(
        body,
        mesh=mesh,
        in_specs=(rows, P(None, "dp", None), vector, vector, matrix, matrix, matrix, vector, matrix, vector),
        out_specs=(rows, vector, vector, matrix, matrix, matrix, vector, matrix, vector),
        check_vma=False,
    )
```

```python
import functools

import jax
import jax.numpy as jnp
from jax import lax
from jax.experimental import pallas as pl
from jax.experimental.pallas import tpu as pltpu
from jax.sharding import PartitionSpec as P

D = 1024
PAIR = 128
FB = 512
CI = 3 * PAIR + FB
RO = PAIR + FB
EPS = 1e-05
NEG = -1000000000.0
SCALE = 0.125
ROWS = 128
TOK = 4 * ROWS
BF = jnp.bfloat16
F32 = jnp.float32
SMALL, LARGE = 24, 56
GRANTS = {"join0": LARGE, "first_forward": LARGE, "first_backward": LARGE, "grads0_out": LARGE, "pack": LARGE, "norm_backward0": LARGE}


def mm(a, b):
    return lax.dot_general(a, b, (((1,), (0,)), ((), ())), preferred_element_type=F32)


def mm_nt(a, b):
    return lax.dot_general(a, b, (((1,), (1,)), ((), ())), preferred_element_type=F32)


def mm_tn(a, b):
    return lax.dot_general(a, b, (((0,), (0,)), ((), ())), preferred_element_type=F32)


def gelu(h):
    return 0.5 * h * (1.0 + jnp.tanh(0.7978845608 * (h + 0.044715 * h * h * h)))


def gelu_slope(h):
    th = jnp.tanh(0.7978845608 * (h + 0.044715 * h * h * h))
    inner = 0.7978845608 * (1.0 + 3 * 0.044715 * h * h)
    return 0.5 * (1.0 + th) + 0.5 * h * (1.0 - th * th) * inner


def partner(x):
    lane = lax.broadcasted_iota(jnp.int32, x.shape, 1)
    return jnp.where(lane % 2 == 0, pltpu.roll(x, PAIR - 1, 1), pltpu.roll(x, 1, 1))


def turned(x, cosine, sine):
    return x * cosine + partner(x) * sine


def by_head(x):
    lane = lax.broadcasted_iota(jnp.int32, (1, PAIR), 1)
    low = jnp.where(lane < 64, 1.0, 0.0).astype(x.dtype)
    high = jnp.where(lane < 64, 0.0, 1.0).astype(x.dtype)
    return jnp.concatenate([x * low, x * high], axis=0)


def beside(x):
    return jnp.concatenate([x[:ROWS], x[ROWS:]], axis=1)


def heads_of(x):
    return [x[ROWS * j : ROWS * (j + 1)] for j in range(4)]


def rows_of(j):
    return pl.ds(j * ROWS, ROWS)


def layer_norm_into(x_refs, gain_ref, bias_ref, normed):
    for j, x_ref in enumerate(x_refs):
        x = x_ref[0:ROWS, :].astype(F32)
        centered = x - jnp.mean(x, -1, keepdims=True)
        inv = lax.rsqrt(jnp.mean(centered * centered, -1, keepdims=True) + EPS)
        normed[rows_of(j), :] = (centered * inv * gain_ref[...] + bias_ref[...]).astype(BF)


def row_of(fast, g):
    return pl.ds(jnp.bitwise_xor(g, lax.axis_index("section")), 1) if fast else slice(g, g + 1)


def forward_in(fast, g, normed, w, bin_ref, cos_ref, sin_ref, mask_ref, qkv, probs, oa, pre):
    w_qkv, w_in = w[g]
    y = mm(normed[...], w_qkv[...])
    cosine, sine = cos_ref[...], sin_ref[...]
    qkv[g, :, 0:PAIR] = turned(y[:, 0:PAIR], cosine, sine).astype(BF)
    qkv[g, :, PAIR : 2 * PAIR] = turned(y[:, PAIR : 2 * PAIR], cosine, sine).astype(BF)
    qkv[g, :, 2 * PAIR : 3 * PAIR] = y[:, 2 * PAIR : 3 * PAIR].astype(BF)
    q, k, v = (heads_of(qkv[g, :, i * PAIR : (i + 1) * PAIR]) for i in range(3))
    s = jnp.concatenate([mm_nt(by_head(q[j]), k[j]) for j in range(4)], axis=0) * SCALE
    s = jnp.where(mask_ref[...] > 0.5, s, NEG)
    e = jnp.exp(s - jnp.max(s, -1, keepdims=True))
    p = e / jnp.sum(e, -1, keepdims=True)
    probs[g] = p
    p = p.astype(BF)
    o = [mm(beside(p[2 * ROWS * j : 2 * ROWS * (j + 1)]), by_head(v[j])) for j in range(4)]
    oa[g][:, 0:PAIR] = jnp.concatenate(o, axis=0).astype(BF)
    h = mm(normed[...], w_in[...]) + bin_ref[row_of(fast, g), :]
    pre[g] = h
    oa[g][:, PAIR:RO] = gelu(h).astype(BF)


def forward_out(oa, w_out, outs):
    for (start, w0), (_, w1) in zip(*w_out):
        for n in range(2):
            part = mm(oa[0][...], w0[:, n * 256 : (n + 1) * 256]) + mm(oa[1][...], w1[:, n * 256 : (n + 1) * 256])
            cols = pl.ds(pl.multiple_of(start + n * 256, 256), 256)
            for j in range(4):
                outs[j][0:ROWS, cols] = part[j * ROWS : (j + 1) * ROWS].astype(outs[j].dtype)


def backward_out(fast, g, gout, w_out, qkv, probs, pre, cos_ref, sin_ref, gcat, gbin_ref):
    halves = [(gout[:, pl.ds(start, 512)], w) for start, w in w_out[g]]
    go = sum(mm_nt(rows, w[0:PAIR, :]) for rows, w in halves).astype(BF)
    q, k, v = (heads_of(qkv[g, :, i * PAIR : (i + 1) * PAIR]) for i in range(3))
    cosine, sine = cos_ref[...], sin_ref[...]
    go = [by_head(rows) for rows in heads_of(go)]
    p = probs[g]
    gp = jnp.concatenate([mm_nt(go[j], v[j]) for j in range(4)], axis=0)
    gs = (p * (gp - jnp.sum(gp * p, -1, keepdims=True))).astype(BF)
    gs = [gs[2 * ROWS * j : 2 * ROWS * (j + 1)] for j in range(4)]
    p = p.astype(BF)
    gq = jnp.concatenate([mm(beside(gs[j]), by_head(k[j])) for j in range(4)], axis=0) * SCALE
    gk = jnp.concatenate([mm_tn(gs[j], by_head(q[j])) for j in range(4)], axis=0) * SCALE
    gv = jnp.concatenate([mm_tn(p[2 * ROWS * j : 2 * ROWS * (j + 1)], go[j]) for j in range(4)], axis=0)
    gcat[g][:, 0:PAIR] = turned(gq, cosine, -sine).astype(BF)
    gcat[g][:, PAIR : 2 * PAIR] = turned(gk, cosine, -sine).astype(BF)
    gcat[g][:, 2 * PAIR : 3 * PAIR] = gv.astype(BF)
    ga = sum(mm_nt(rows, w[PAIR:RO, :]) for rows, w in halves)
    gpre = (ga * gelu_slope(pre[g])).astype(BF)
    gcat[g][:, 3 * PAIR : CI] = gpre
    gbin_ref[row_of(fast, g), :] = jnp.sum(gpre.astype(F32), 0, keepdims=True)


def backward_in(gcat, w, outs):
    for n in range(4):
        cols = slice(n * 256, (n + 1) * 256)
        part = sum(
            mm_nt(gcat[g][:, 0 : 3 * PAIR], w[g][0][cols, :]) + mm_nt(gcat[g][:, 3 * PAIR : CI], w[g][1][cols, :])
            for g in range(2)
        )
        for j in range(4):
            outs[j][0:ROWS, cols] = part[j * ROWS : (j + 1) * ROWS].astype(outs[j].dtype)


A_COLS = D + 2 * RO
B_COLS = CI + 512


def views_a(ship_a):
    return ship_a.at[:, 0:D], (ship_a.at[:, D : D + RO], ship_a.at[:, D + RO : D + 2 * RO])


def views_b(ship_b):
    return ship_b.at[:, 0:CI], ship_b.at[:, CI : CI + 512]


HALF = (2 * D + 2 * RO, 512)


def weights_of(fast, refs):
    if not fast:
        wi, wo = refs
        ins = [(wi.at[g, :, 0 : 3 * PAIR], wi.at[g, :, 3 * PAIR : CI]) for g in range(2)]
        return ins, [[(0, wo.at[g, :, 0:512]), (512, wo.at[g, :, 512:1024])] for g in range(2)]
    core, halves = lax.axis_index("section"), refs
    starts = [pl.multiple_of(512 * c, 512) for c in (core, 1 - core)]
    rows = [pl.ds(pl.multiple_of(2 * D + RO * c, 128), RO) for c in (core, 1 - core)]
    ins = [(half.at[D : 2 * D, 0 : 3 * PAIR], half.at[0:D, :]) for half in halves]
    return ins, [[(start, half.at[rows[g], :]) for start, half in zip(starts, halves)] for g in range(2)]


def weight_loads(fast, refs, held, sems):
    if fast:
        core = lax.axis_index("section")
        halves = refs if len(refs) == 2 else [refs[0].at[core], refs[0].at[1 - core]]
        ins = [pltpu.make_async_copy(h.at[0 : 2 * D], v.at[0 : 2 * D], sems.at[i]) for i, (h, v) in enumerate(zip(halves, held))]
        end = 2 * D + 2 * RO
        outs = [
            pltpu.make_async_copy(h.at[2 * D : end], v.at[2 * D : end], sems.at[2 + i])
            for i, (h, v) in enumerate(zip(halves, held))
        ]
        return ins, outs
    ins = [pltpu.make_async_copy(refs[0].at[g], held[0].at[g], sems.at[g]) for g in range(2)]
    return ins, [pltpu.make_async_copy(refs[1], held[1], sems.at[2])]


def start(copies):
    for copy in copies:
        copy.start()
    return copies


def finish(copies):
    for copy in copies:
        copy.wait()


def moves(sources, targets, sems, first=0):
    return [pltpu.make_async_copy(a, b, sems.at[first + i]) for i, (a, b) in enumerate(zip(sources, targets))]


def place_of():
    return lax.axis_index("dp"), lax.axis_index("section")


def other_half(fast, gout, half_ref):
    core = lax.axis_index("section") if fast else 0
    half_ref[...] = gout[:, pl.ds(pl.multiple_of(512 * (1 - core), 512), 512)]


def join_kernel(own, far, near_own, near_far, *refs):
    pieces, joined, sems = refs[:-2], refs[-2], refs[-1]
    target = joined if len(joined.shape) == 2 else joined.at[0]
    me, _ = place_of()
    copies = []

    def copy(source, rows, cols=slice(None)):
        copies.append(pltpu.make_async_copy(source, target.at[rows, cols], sems.at[len(copies)]))
        copies[-1].start()

    for flip, piece in ((0, own), (8, far), (1, near_own), (9, near_far)):
        source = jnp.bitwise_xor(me, flip)
        g, r = source // 8, source % 2
        base = 2 * D + g * RO
        copy(piece.at[0:64], pl.ds(pl.multiple_of(base + 64 * r, 64), 64))
        copy(piece.at[64:320], pl.ds(pl.multiple_of(base + PAIR + 256 * r, 128), 256))
    blocks = [(ref, i) for ref in pieces for i in range(ref.shape[0])]
    for (ref, i), flip in zip(blocks, [f ^ (2 * j) for f in (0, 8, 1, 9) for j in range(4)]):
        start = pl.multiple_of(jnp.bitwise_xor(me, flip) * 64, 64)
        copy(ref.at[i, :, 3 * PAIR : CI], pl.ds(start, 64))
        copy(ref.at[i, :, 0 : 3 * PAIR], pl.ds(D + start, 64), slice(0, 3 * PAIR))
    for one in copies:
        one.wait()
    if len(joined.shape) == 3:
        joined[1] = joined[0]


def first_forward_kernel(fast, n_w, *refs):
    x_refs, (gain, bias, bin_ref, cos_ref, sin_ref, mask_ref), refs = refs[:4], refs[4:10], refs[10:]
    w_refs, outs, saved, refs = refs[:n_w], refs[n_w : n_w + 4], refs[n_w + 4 : n_w + 8], refs[n_w + 8 :]
    w_held, held, (w_sems, sems) = refs[:2], refs[2:6], refs[6:]
    loads_in, loads_out = weight_loads(fast, w_refs, w_held, w_sems)
    start(loads_in + loads_out)
    w_in, w_out = weights_of(fast, w_held)
    ship_a, qkv, probs, pre = held
    normed, oa = views_a(ship_a)
    layer_norm_into(x_refs, gain, bias, normed)
    puts = []
    for g in range(2):
        finish(loads_in[g : g + 1])
        forward_in(fast, g, normed, w_in, bin_ref, cos_ref, sin_ref, mask_ref, qkv, probs, oa, pre)
        puts += start(moves([h.at[g] for h in held[1:]], [h.at[g] for h in saved[1:]], sems, 1 + 3 * g))
    puts += start(moves(held[:1], saved[:1], sems))
    finish(loads_out)
    forward_out(oa, w_out, outs)
    finish(puts)


def second_layer_kernel(fast, n_w, *refs):
    x_refs, gout_refs, refs = refs[:4], refs[4:8], refs[8:]
    (gain, bias, bin_ref, cos_ref, sin_ref, mask_ref), refs = refs[:6], refs[6:]
    w_refs, refs = refs[:n_w], refs[n_w:]
    if fast:
        core = lax.axis_index("section")
        w_refs = [w_refs[0].at[core], w_refs[0].at[1 - core]]
    w_in, w_out = weights_of(fast, w_refs)
    outs, gouts, gbin_ref, refs = refs[:4], refs[4:8], refs[8], refs[9:]
    ship_a, ship_b, gcat0, qkv, probs, pre, gout = refs
    normed, oa = views_a(ship_a)
    gcat1, gout_half = views_b(ship_b)
    gcat = (gcat0, gcat1)
    layer_norm_into(x_refs, gain, bias, normed)
    for j in range(4):
        gout[rows_of(j), :] = gout_refs[j][...]
    other_half(fast, gout, gout_half)
    for g in range(2):
        forward_in(fast, g, normed, w_in, bin_ref, cos_ref, sin_ref, mask_ref, qkv, probs, oa, pre)
    for g in range(2):
        backward_out(fast, g, gout, w_out, qkv, probs, pre, cos_ref, sin_ref, gcat, gbin_ref)
    backward_in(gcat, w_in, gouts)
    forward_out(oa, w_out, outs)


def first_backward_kernel(fast, n_w, *refs):
    gout_refs, (cos_ref, sin_ref), saved, refs = refs[:4], refs[4:6], refs[6:9], refs[9:]
    w_refs, refs = refs[:n_w], refs[n_w:]
    gouts, gbin_ref, put_refs, refs = refs[:4], refs[4], refs[5:7], refs[7:]
    w_held, held, (ship_b, gcat0, gout, w_sems, sems) = refs[:2], refs[2:5], refs[5:]
    loads_in, loads_out = weight_loads(fast, w_refs, w_held, w_sems)
    loads = [moves([h.at[g] for h in saved], [h.at[g] for h in held], sems, 3 * g) for g in range(2)]
    start(loads_out + loads[0] + loads[1] + loads_in)
    w_in, w_out = weights_of(fast, w_held)
    gcat1, gout_half = views_b(ship_b)
    gcat = (gcat0, gcat1)
    for j in range(4):
        gout[rows_of(j), :] = gout_refs[j][...]
    other_half(fast, gout, gout_half)
    finish(loads_out)
    for g in range(2):
        finish(loads[g])
        backward_out(fast, g, gout, w_out, *held, cos_ref, sin_ref, gcat, gbin_ref)
    puts = start(moves([ship_b, gcat0], put_refs, sems, 6))
    finish(loads_in)
    backward_in(gcat, w_in, gouts)
    finish(puts)


def turn_kernel(ship_a, other_a, put_in, put_out, held_a, held_b, left_in, left_out, sems):
    me, core = place_of()
    g, t, r = me // 8, (me // 2) % 4, me % 2
    loads = start(moves([ship_a, other_a], [held_a, held_b], sems))
    for side, ship in enumerate((held_a, held_b)):
        tokens = slice(side * TOK, (side + 1) * TOK)
        finish(loads[side : side + 1])
        for part in range(2):
            far = jnp.bitwise_xor(g, jnp.bitwise_xor(core, part ^ side))
            flat = ship[:, D + part * RO : D + (part + 1) * RO].T
            for s in range(2):
                near = jnp.bitwise_xor(r, s)
                left_out[near, far, 0:64, tokens] = flat[64 * s : 64 * s + 64]
                left_out[near, far, 64:320, tokens] = flat[PAIR + 256 * s : PAIR + 256 * (s + 1)]
        for far in range(2):
            for j in range(4):
                pair = jnp.bitwise_xor(g, far) * 4 + jnp.bitwise_xor(t, j)
                block = ship[:, pl.ds(pl.multiple_of(pair * PAIR, PAIR), PAIR)].T
                start_row = far * 256 + 64 * j
                for s in range(2):
                    left_in[jnp.bitwise_xor(r, s), start_row : start_row + 64, tokens] = block[64 * s : 64 * s + 64]
    finish(start(moves([left_in, left_out], [put_in, put_out], sems, 2)))


def weight_grad_out_kernel(*refs):
    gout_refs, refs = refs[:4], refs[4:]
    *extras, left_ref, other_b, keep, send, left, right, right_other, sems = refs
    loads = start(
        moves([other_b.at[:, CI : CI + 512], left_ref.at[1], left_ref.at[0]], [right_other, left.at[1], left.at[0]], sems)
    )
    cols = pl.ds(pl.multiple_of(512 * lax.axis_index("section"), 512), 512)
    for j in range(4):
        right[rows_of(j), :] = gout_refs[j][:, cols]
    finish(loads[:1])
    for near, out in ((1, send), (0, keep)):
        finish(loads[2 - near : 3 - near])
        for far in range(2):
            part = mm(left[near, far, :, 0:TOK], right[...]) + mm(left[near, far, :, TOK : 2 * TOK], right_other[...])
            out[far, 0:320, :] = part.astype(BF)
            for extra in extras:
                out[far, 320:336, :] = extra[near, far]


def weight_grad_in_kernel(left_ref, gcat, other_b, keep, send, left, right, right_other, sems):
    sources = [gcat, left_ref.at[1], other_b.at[:, 0:CI], left_ref.at[0]]
    loads = start(moves(sources, [right, left.at[1], right_other, left.at[0]], sems))
    finish(loads[:3])
    for near, out in ((1, send), (0, keep)):
        if near == 0:
            finish(loads[3:])
        part = mm(left[near, :, 0:TOK], right[...]) + mm(left[near, :, TOK : 2 * TOK], right_other[...])
        part = part.astype(BF)
        for i in range(8):
            out[i // 4, i % 4] = part[64 * i : 64 * i + 64]


def whole_grad_out_kernel(*refs):
    gout_refs, (ship_a, out, gout) = refs[:4], refs[4:]
    for j in range(4):
        gout[rows_of(j), :] = gout_refs[j][...]
    for g in range(2):
        out[g] = mm_tn(ship_a[:, D + g * RO : D + (g + 1) * RO], gout[...]).astype(BF)


def whole_grad_in_kernel(ship_a, gcat0, ship_b, out):
    for g in range(2):
        right = gcat0[...] if g == 0 else ship_b[:, 0:CI]
        for m in range(4):
            rows = slice(m * 256, (m + 1) * 256)
            out[g, rows, :] = mm_tn(ship_a[:, rows], right).astype(BF)


def norm_backward_kernel(own, r1, r2, r3, x_ref, gout_ref, gain, gx_ref, low_ref, sums_ref):
    x = x_ref[0:ROWS, :].astype(F32)
    gn = own[...] + sum(r[...].astype(F32) for r in (r1, r2, r3))
    gout = gout_ref[...].astype(F32)
    centered = x - jnp.mean(x, -1, keepdims=True)
    inv = lax.rsqrt(jnp.mean(centered * centered, -1, keepdims=True) + EPS)
    unit = centered * inv
    gu = gn * gain[...]
    gx = gout + inv * (gu - jnp.mean(gu, -1, keepdims=True) - unit * jnp.mean(gu * unit, -1, keepdims=True))
    gx_ref[...] = gx
    low_ref[...] = gx.astype(BF)
    sums_ref[0:1, :] = jnp.sum(gn * unit, 0, keepdims=True)
    sums_ref[1:2, :] = jnp.sum(gn, 0, keepdims=True)
    sums_ref[2:3, :] = jnp.sum(gout, 0, keepdims=True)


def pack_kernel(w_qkv, w_out, w_in, w_fc, wi_keep, wi_send, wo_keep, wo_send):
    t, core = (lax.axis_index("dp") // 2) % 4, lax.axis_index("section")
    for ref, g in ((wi_keep, core), (wi_send, 1 - core)):
        for j in range(4):
            rank = jnp.bitwise_xor(t, j)
            for part in range(3):
                start = pl.multiple_of(part * D + g * 512 + rank * PAIR, PAIR)
                ref[j, :, part * PAIR : (part + 1) * PAIR] = w_qkv[:, pl.ds(start, PAIR)].astype(BF)
            start = pl.multiple_of(g * 2048 + rank * FB, FB)
            ref[j, :, 3 * PAIR : CI] = w_in[:, pl.ds(start, FB)].astype(BF)
    for ref, half in ((wo_keep, core), (wo_send, 1 - core)):
        cols = pl.ds(pl.multiple_of(512 * half, 512), 512)
        ref[0:64, :] = w_out[:, cols].astype(BF)
        ref[64:320, :] = w_fc[:, cols].astype(BF)


def unpack_kernel(own0, own1, own2, own3, other, wo_own, wo_other, g_qkv, g_out, g_in, g_fc):
    t, core = (lax.axis_index("dp") // 2) % 4, lax.axis_index("section")
    for side, g in ((0, core), (1, 1 - core)):
        for j in range(4):
            block = (own0, own1, own2, own3)[j][...] if side == 0 else other[j]
            block = block.astype(F32)
            rank = jnp.bitwise_xor(t, j)
            for part in range(3):
                start = pl.multiple_of(part * D + g * 512 + rank * PAIR, PAIR)
                g_qkv[:, pl.ds(start, PAIR)] = block[:, part * PAIR : (part + 1) * PAIR]
            start = pl.multiple_of(g * 2048 + rank * FB, FB)
            g_in[:, pl.ds(start, FB)] = block[:, 3 * PAIR : CI]
    for ref, half in ((wo_own, core), (wo_other, 1 - core)):
        cols = pl.ds(pl.multiple_of(512 * half, 512), 512)
        g_out[:, cols] = ref[0:64, :].astype(F32)
        g_fc[:, cols] = ref[64:320, :].astype(F32)


VM = pl.BlockSpec(memory_space=pltpu.VMEM)


HB = pl.BlockSpec(memory_space=pl.ANY)


def kernel_call(kernel, args, outs, hbm_args=0, hbm_outs=0, scratch=(), cost=2e10, name=None):
    return pl.pallas_call(
        kernel,
        out_shape=outs,
        in_specs=[VM] * (len(args) - hbm_args) + [HB] * hbm_args,
        out_specs=[VM] * (len(outs) - hbm_outs) + [HB] * hbm_outs,
        scratch_shapes=list(scratch),
        compiler_params=pltpu.CompilerParams(vmem_limit_bytes=GRANTS.get(name, SMALL) * 1024 * 1024),
        cost_estimate=pl.CostEstimate(flops=int(cost), bytes_accessed=1, transcendentals=0),
        name=name,
    )(*args)


def dma(count):
    return pltpu.SemaphoreType.DMA((count,))


def arr(shape, dtype):
    return jax.ShapeDtypeStruct(shape, dtype)


def partial_outs():
    return [arr((ROWS, D), F32)] + [arr((ROWS, D), BF)] * 3


def swap_core(value):
    return lax.ppermute(value, "section", [(0, 1), (1, 0)])


def flipped(value, flip):
    count = lax.axis_size("dp")
    return lax.ppermute(value, "dp", [(i, i ^ flip) for i in range(count)])


def after(value, *earlier):
    return lax.optimization_barrier((value, earlier))[0]


def choose(own, other):
    first_core = lax.axis_index("section") == 0
    return jnp.where(first_core, own, other), jnp.where(first_core, other, own)


def across(values):
    spread = lax.axis_size("dp") // 8
    return [flipped(v, (j + 1) * spread) for j, v in enumerate(values)]


def groups_of(spread):
    places = [[[g * 4 * spread + t * spread + r for r in range(spread)] for t in range(4)] for g in range(2)]
    t_groups = [[places[g][t][r] for t in range(4)] for g in range(2) for r in range(spread)]
    f_groups = [[places[g][t][r] for g in range(2) for r in range(spread)] for t in range(4)]
    return t_groups, f_groups


def any_gather(w_qkv, w_out, w_in, w_fc):
    share, spread = w_qkv.shape[0], lax.axis_size("dp") // 8
    t_groups, f_groups = groups_of(spread)
    qkv = w_qkv.reshape(share, 3, 2, 4, PAIR).transpose(3, 0, 2, 1, 4).reshape(4, share, 2, 3 * PAIR)
    wi = jnp.concatenate([qkv, w_in.reshape(share, 2, 4, FB).transpose(2, 0, 1, 3)], axis=-1).astype(BF)
    wi = lax.all_to_all(wi, "dp", 0, 0, axis_index_groups=t_groups, tiled=True)
    wi = lax.all_gather(wi, "dp", axis_index_groups=f_groups)
    wi = wi.reshape(2, spread, 4, share, 2, CI).transpose(4, 0, 2, 1, 3, 5).reshape(2, D, CI)
    wo = lax.all_gather(w_out.astype(BF), "dp", axis_index_groups=f_groups).reshape(2, PAIR, D)
    wf = lax.all_gather(w_fc.astype(BF), "dp", axis_index_groups=f_groups).reshape(2, FB, D)
    wo = jnp.concatenate([wo, wf], axis=1)
    return choose(wi, swap_core(wi)), choose(wo, swap_core(wo))


def any_reduce(gi, go):
    count = lax.axis_size("dp")
    spread, share = count // 8, D // count
    t_groups, f_groups = groups_of(spread)

    def scattered(value):
        return lax.psum_scatter(value, "dp", scatter_dimension=0, axis_index_groups=f_groups)

    gi = gi.reshape(2, 2, 4, spread, share, CI).transpose(1, 3, 2, 4, 0, 5).reshape(2 * spread, 4, share, 2, CI)
    gi = lax.all_to_all(scattered(gi), "dp", 0, 0, axis_index_groups=t_groups, tiled=True)
    g_qkv = gi[..., : 3 * PAIR].reshape(4, share, 2, 3, PAIR).transpose(1, 3, 2, 0, 4).reshape(share, 3 * D)
    g_in = gi[..., 3 * PAIR :].transpose(1, 2, 0, 3).reshape(share, 4 * D)
    g_out = scattered(go[:, :PAIR].reshape(2 * spread, share, D))
    g_fc = scattered(go[:, PAIR:].reshape(2 * spread, 4 * share, D))
    return g_qkv, g_out, g_in, g_fc


def body(boundary, segments, ln_gain, ln_bias, w_qkv, w_out, w_in, b_in, w_fc, b_fc):
    core, me = lax.axis_index("section"), lax.axis_index("dp")
    count = lax.axis_size("dp")
    fast = count == 16
    spread = count // 8
    rank = (me // spread) % 4
    share = D // count
    width_small = 7 * share
    first_core = core == 0

    if fast:
        small = jnp.concatenate([ln_gain, ln_bias, b_fc, b_in], axis=-1).astype(BF)
        small = jnp.concatenate([small, flipped(small, 8)])
        small = jnp.concatenate([small, flipped(small, 1)])
        small = jnp.stack(choose(small, swap_core(small)), axis=1).reshape(8, width_small)

    if fast:
        wi_keep, wi_send, wo_keep, wo_send = kernel_call(
            pack_kernel,
            [w_qkv[0], w_out[0], w_in[0], w_fc[0]],
            [arr((4, 64, CI), BF), arr((4, 64, CI), BF), arr((320, 512), BF), arr((320, 512), BF)],
            name="pack",
        )
        wi_recv, wo_recv = swap_core(wi_send), swap_core(wo_send)
        wi_first = [choose(wi_keep[j], wi_recv[j]) for j in range(4)]
        wo_first = choose(wo_keep, wo_recv)
        boundary, segments = after((boundary, segments), wi_keep)
    else:
        wi_both, wo_both = any_gather(w_qkv[0], w_out[0], w_in[0], w_fc[0])

    swapped = swap_core(lax.dynamic_index_in_dim(boundary[0], 1 - core, 0, False)[0])
    kept = lax.dynamic_index_in_dim(boundary[0], core, 0, False)[0]
    x0, g1 = choose(kept, swapped)
    if not fast:
        small = jnp.concatenate([ln_gain, ln_bias, b_fc, b_in], axis=-1).astype(BF)
        small = jnp.concatenate(choose(small, swap_core(small)))
    seg = lax.dynamic_index_in_dim(segments, core, 0, False)[0].astype(BF)
    extra = jnp.zeros((16, D), BF).at[0, :ROWS].set(seg)
    if fast:

        def join(wi_pieces, wo_pieces, name):
            pieces, sems = [*wo_pieces, *wi_pieces], [pltpu.SemaphoreType.DMA((40,))]
            if name == "join0":
                own = kernel_call(join_kernel, pieces, [arr(HALF, BF)], 8, 0, sems, 1, name)[0]
                return own
            both = kernel_call(join_kernel, pieces, [arr((2, *HALF), BF)], 8, 0, sems, 1, name)[0]
            return lax.all_to_all(both, "section", 0, 0, tiled=True)

        mine = [after(jnp.stack(w), wo_first) for w in wi_first]
        arrived = across(mine[1:])
        wi_own, wi_own1 = (jnp.stack([w[l] for w in [mine[0], *arrived]]) for l in range(2))
        wo_own, wo_own1 = wo_first
        wo_far, wo_near = flipped(wo_own, 8), flipped(wo_own, 1)
        wi_far, wi_near = flipped(after(wi_own, wo_far), 8), flipped(wi_own, 1)
        wo_near_far = flipped(wo_far, 1)
        extra = extra.at[1:9, :width_small].set(small)
        pack = jnp.concatenate([x0, extra])
        packs = [pack] + across(after([pack] * 3, arrived))
        g1s = [g1] + across(after([g1] * 3, packs))
        wo_far1, wi_far1 = flipped(after(wo_own1, wi_far), 8), flipped(after(wi_own1, wi_far), 8)

        held = jnp.stack([p[129:137, :width_small] for p in packs])
        held = held.reshape(16, 2 * width_small)
        index = jnp.arange(16)
        flip_of = jnp.bitwise_xor(index, me)
        at = (flip_of // 2) % 4 * 4 + (flip_of % 2) * 2 + flip_of // 8
        onehot = (at[:, None] == index[None, :]).astype(BF)
        everyone = mm(onehot, held).reshape(16, 2, width_small)
    else:
        w0, w1 = ([wi_both[l], wo_both[l]] for l in range(2))
        pack = jnp.concatenate([x0, extra])
        packs, g1s = [pack] + across([pack] * 3), [g1] + across([g1] * 3)
        everyone = lax.all_gather(small, "dp").astype(F32)

    def small_of(layer):
        one = everyone[:, layer]
        vectors = [one[:, i * share : (i + 1) * share].reshape(1, D) for i in range(3)]
        b = one[:, 3 * share :].reshape(2, 4, FB)
        return *vectors, lax.dynamic_index_in_dim(b, rank, 1, False)

    gain0, bias0, bfc0, bin0 = small_of(0)
    gain1, bias1, bfc1, bin1 = small_of(1)

    segs = jnp.stack([p[ROWS, :ROWS] for p in packs])
    row = lax.broadcasted_iota(jnp.int32, (ROWS, ROWS), 0)
    col = lax.broadcasted_iota(jnp.int32, (ROWS, ROWS), 1)
    mask = ((segs[:, :, None] == segs[:, None, :]) & (col <= row)).astype(F32)
    positions = jnp.sum(mask, -1).reshape(TOK, 1) - 1.0
    mask = jnp.stack([mask, mask], axis=1).reshape(8 * ROWS, ROWS)
    lane = jnp.arange(PAIR) % 64
    freq = jnp.where(lane < 32, 10000.0 ** (-(lane // 2 * 2).astype(F32) / 32), 0.0)
    angle = positions * freq
    cosine = jnp.cos(angle)
    sine = jnp.sin(angle) * jnp.where(lane % 2 == 0, -1.0, 1.0)

    if fast:
        tables = (gain0, bias0, bin0, cosine, sine, mask, gain1, bias1, bin1, bfc0, bfc1)
        wi_near_far = flipped(after(wi_far, wo_near_far, wi_near, wo_near), 1)
        wi_got = [wi_own, wi_far, wi_near, wi_near_far]
        w0 = join(after(wi_got, tables), [wo_own, wo_far, wo_near, wo_near_far], "join0")
        w0 = [w0, swap_core(after(w0, wo_far1, g1s))]
        wo_near1, wi_near1 = flipped(after(wo_own1, wi_near_far), 1), flipped(after(wi_own1, wi_near_far), 1)

    held_weights = [pltpu.VMEM(HALF, BF)] * 2 if fast else [pltpu.VMEM((2, D, CI), BF), pltpu.VMEM((2, RO, D), BF)]

    saved = [
        arr((TOK, A_COLS), BF),
        arr((2, TOK, 3 * PAIR), BF),
        arr((2, 8 * ROWS, ROWS), F32),
        arr((2, TOK, FB), F32),
    ]
    got = kernel_call(
        functools.partial(first_forward_kernel, fast, len(w0)),
        [*packs, gain0, bias0, bin0, cosine, sine, mask, *w0],
        partial_outs() + saved,
        hbm_args=2,
        hbm_outs=4,
        scratch=[*held_weights, *(pltpu.VMEM(a.shape, a.dtype) for a in saved), dma(4), dma(7)],
        cost=1,
        name="first_forward",
    )
    own, sends, (ship_a0, qkv0, probs0, pre0) = got[0], got[1:4], got[4:]

    def total(own, arrived):
        return sum([r.astype(F32) for r in arrived], own)

    arrived = across(sends)
    sums = total(own, arrived)
    if fast:
        wo_near_far1 = flipped(after(wo_far1, own, wo_near1), 1)
        wi_near_far1 = flipped(after(wi_far1, own, wi_near1), 1)
        w1 = join([wi_own1, wi_far1, wi_near1, wi_near_far1], [wo_own1, wo_far1, wo_near1, wo_near_far1], "join1")
        w1 = [w1]
    x1 = (x0.astype(F32) + sums + bfc0).astype(BF)
    x1s = [x1] + across([x1] * 3)

    back_outs = [arr((TOK, B_COLS), BF), arr((TOK, CI), BF)]
    got = kernel_call(
        functools.partial(second_layer_kernel, fast, len(w1)),
        [*x1s, *g1s, gain1, bias1, bin1, cosine, sine, mask, *w1],
        [*partial_outs(), *partial_outs(), arr((2, FB), F32), arr((TOK, A_COLS), BF), *back_outs],
        scratch=[*(pltpu.VMEM(a.shape, a.dtype) for a in saved[1:]), pltpu.VMEM((TOK, D), BF)],
        name="second_layer",
    )
    out_own, out_sends, gn_own, gn_sends = got[0], got[1:4], got[4], got[5:8]
    gbin1, ship_a1, ship_b1, gcat1 = got[8:]

    def norm_backward(own, arrived, x, gout, gain, name):
        return kernel_call(
            norm_backward_kernel,
            [own, *arrived, x, gout, gain],
            [arr((ROWS, D), F32), arr((ROWS, D), BF), arr((3, D), F32)],
            name=name,
        )

    def turned_ships(ship_a, other_a, name):
        outs = [arr((2, 512, 2 * TOK), BF), arr((2, 2, 320, 2 * TOK), BF)]
        if not fast:
            return ship_a, ship_a
        scratch = [pltpu.VMEM((TOK, A_COLS), BF)] * 2 + [pltpu.VMEM(a.shape, BF) for a in outs] + [dma(4)]
        return kernel_call(turn_kernel, [ship_a, other_a], outs, 2, 2, scratch, name=name)

    def grads_out(gouts, left, other_b, extra, name):
        if fast:
            extras = [] if extra is None else [extra]
            return kernel_call(
                weight_grad_out_kernel,
                [*gouts, *extras, left, other_b],
                [arr((2, 320 + 16 * len(extras), 512), BF)] * 2,
                hbm_args=2,
                scratch=[pltpu.VMEM(left.shape, BF), pltpu.VMEM((TOK, 512), BF), pltpu.VMEM((TOK, 512), BF), dma(3)],
                name=name,
            )
        scratch = [pltpu.VMEM((TOK, D), BF)]
        return kernel_call(whole_grad_out_kernel, [*gouts, left], [arr((2, RO, D), BF)], scratch=scratch, name=name)

    def grads_in(left, ship_b, other_b, gcat, name):
        if fast:
            scratch = [pltpu.VMEM(left.shape, BF), pltpu.VMEM((TOK, CI), BF), pltpu.VMEM((TOK, CI), BF), dma(4)]
            outs = [arr((2, 4, 64, CI), BF)] * 2
            return kernel_call(weight_grad_in_kernel, [left, gcat, other_b], outs, 3, 0, scratch, name=name)
        return kernel_call(whole_grad_in_kernel, [left, gcat, ship_b], [arr((2, D, CI), BF)], name=name)

    def onward(keep, near):
        return flipped((keep[1].astype(F32) + near[1].astype(F32)).astype(BF), 8)

    def reduced(keep, near, far):
        return keep[0].astype(F32) + near[0].astype(F32) + far.astype(F32)

    arrived_gn = across(gn_sends)
    other_a1, other_b1 = (swap_core(ship_a1), swap_core(ship_b1)) if fast else (None, None)
    other_a0 = swap_core(ship_a0) if fast else None
    left_in1, left_out1 = turned_ships(after(ship_a1, other_a0), other_a1, "turn1")
    go1 = grads_out(g1s, left_out1, other_b1, None, "grads1_out")
    _, g0, sums1 = norm_backward(after(gn_own, go1), arrived_gn, x1, g1, gain1, "norm_backward1")
    g0s = [g0] + across([g0] * 3)
    gi1 = grads_in(after(left_in1, g0), ship_b1, other_b1, gcat1, "grads1_in")
    left_in0, left_out0 = turned_ships(after(ship_a0, g0), other_a0, "turn0")
    if fast:
        keep1, send1 = zip(go1, gi1)
        near1 = [flipped(v, 1) for v in send1]
        far1 = [onward(k, v) for k, v in zip(keep1, near1)]
        g0s[0] = after(g0, near1[0], gi1, left_in0)

    got = kernel_call(
        functools.partial(first_backward_kernel, fast, len(w0)),
        [*g0s, cosine, sine, qkv0, probs0, pre0, *w0],
        [*partial_outs(), arr((2, FB), F32), *back_outs],
        hbm_args=5,
        hbm_outs=2,
        scratch=[
            *held_weights,
            *(pltpu.VMEM(a.shape, a.dtype) for a in saved[1:]),
            *(pltpu.VMEM((TOK, cols), BF) for cols in (B_COLS, CI, D)),
            dma(4),
            dma(8),
        ],
        name="first_backward",
    )
    gn_own, gn_sends, (gbin0, ship_b0, gcat0) = got[0], got[1:4], got[4:]
    arrived_gn = across(gn_sends)
    if fast:
        other_b0 = swap_core(after(ship_b0, near1[1], far1[0]))
    else:
        other_b0 = None
    gi0 = grads_in(left_in0, ship_b0, other_b0, gcat0, "grads0_in")
    gx0, _, sums0 = norm_backward(after(gn_own, gi0), arrived_gn, x0, g0, gain0, "norm_backward0")

    def small_grads(sums, gbin):
        onehot = (jnp.arange(4) == rank).astype(F32)
        vectors = sums.reshape(3, 2, 4, spread, share).transpose(1, 2, 3, 0, 4).reshape(2, 4, spread, 3 * share)
        b = gbin.reshape(2, 1, spread, 4 * share)
        return (vectors, b) if fast else jnp.concatenate([vectors, b * onehot[None, :, None, None]], axis=-1)

    both = jax.tree.map(choose, small_grads(sums0, gbin0), small_grads(sums1, gbin1))
    if fast:
        mine, theirs = (jnp.concatenate([v[i].reshape(-1) for v in both]) for i in range(2))
        mine = mine + swap_core(theirs)
        vectors, b = mine[: 3 * D].reshape(2, 4, 2, 192), mine[3 * D :].reshape(2, 1, 2, 256)
        values = jnp.concatenate([vectors.transpose(2, 0, 1, 3).reshape(2, 2, 768), b[:, 0].transpose(1, 0, 2)], axis=-1)
        values = jnp.where(me // 8 == 0, values, values[:, ::-1])
        values = jnp.where(me % 2 == 0, values, values[::-1])
        extra = jnp.zeros((2, 2, 16, 512), BF).at[:, :, :2].set(values.reshape(2, 2, 2, 512).astype(BF))
        wo_1, wi_1 = (reduced(*v).astype(BF) for v in zip(keep1, near1, far1))
        near_in0 = flipped(gi0[1], 1)
        far_in0 = onward(gi0[0], near_in0)
        extra = after(extra, wi_1, near_in0)
    else:
        extra = None
    go0 = grads_out(g0s, left_out0, other_b0, extra, "grads0_out")

    out1 = x1.astype(F32) + total(out_own, across(after(out_sends, near_in0) if fast else out_sends)) + bfc1
    arrived = swap_core(jnp.where(first_core, out1, gx0))
    boundary_out = jnp.where(first_core, jnp.stack([gx0, arrived]), jnp.stack([arrived, out1]))[None, :, None]
    if fast:
        near_out0 = flipped(go0[1], 1)
        far_out0 = onward(go0[0], near_out0)
        wo_0 = reduced(go0[0], near_out0, far_out0)
        shares = [reduced(gi0[0], near_in0, far_in0), wi_1]
        vector = wo_0[320:322].reshape(1024)
        ranks = vector[:768].reshape(4, 192)
        ranks = [lax.dynamic_index_in_dim(ranks, jnp.bitwise_xor(rank, j), 0, True) for j in range(4)]
        summed = sum([r.astype(F32) for r in across([r.astype(BF) for r in ranks[1:]])], ranks[0])
        vector = jnp.concatenate([summed, vector[None, 768:]], axis=1)
        wo_0 = wo_0[:320].astype(BF)
        shares = [jnp.concatenate([shares[0][j].astype(BF), shares[1][j]]) for j in range(4)]
        arrived = [shares[0]] + across(after(shares[1:], out1, near_out0))
        wo_mine, wo_theirs = choose(wo_0, wo_1)
        pairs = [choose(w[:64], w[64:]) for w in arrived]
        wi_other = swap_core(jnp.stack([p[1] for p in pairs]))
        g_qkv, g_out, g_in, g_fc = kernel_call(
            unpack_kernel,
            [*[p[0] for p in pairs], wi_other, wo_mine, swap_core(wo_theirs)],
            [arr((64, 3 * D), F32), arr((64, D), F32), arr((64, 4 * D), F32), arr((256, D), F32)],
            name="unpack",
        )
    else:
        vector = (both[0] + swap_core(both[1])).reshape(count, 7 * share)
        vector = lax.psum_scatter(vector, "dp", scatter_dimension=0, tiled=True)
        mine, theirs = choose(gi0[0], gi1[0])
        gi = mine.astype(F32) + swap_core(theirs).astype(F32)
        mine, theirs = choose(go0[0], go1[0])
        go = mine.astype(F32) + swap_core(theirs).astype(F32)
        g_qkv, g_out, g_in, g_fc = any_reduce(gi, go)
    g_gain, g_bias, g_bfc = (vector[:, i * share : (i + 1) * share] for i in range(3))
    g_bin = vector[:, 3 * share :]

    return (boundary_out, g_gain, g_bias, g_qkv[None], g_out[None], g_in[None], g_bin, g_fc[None], g_bfc)


def solution(mesh):
    rows = P("section", None, "dp", None, None)
    vector, matrix = P("section", "dp"), P("section", "dp", None)
    return jax.shard_map(
        body,
        mesh=mesh,
        in_specs=(rows, P(None, "dp", None), vector, vector, matrix, matrix, matrix, vector, matrix, vector),
        out_specs=(rows, vector, vector, matrix, matrix, matrix, vector, matrix, vector),
        check_vma=False,
    )
```

```python
import functools

import jax
import jax.numpy as jnp
from jax import lax
from jax.experimental import pallas as pl
from jax.experimental.pallas import tpu as pltpu
from jax.sharding import PartitionSpec as P

D = 1024
PAIR = 128
FB = 512
CI = 3 * PAIR + FB
RO = PAIR + FB
EPS = 1e-05
NEG = -1000000000.0
SCALE = 0.125
ROWS = 128
TOK = 4 * ROWS
BF = jnp.bfloat16
F32 = jnp.float32
SMALL, LARGE = 24, 56
GRANTS = {"join0": LARGE, "first_forward": LARGE, "first_backward": LARGE, "grads0_out": LARGE, "pack": LARGE, "norm_backward0": LARGE}


def mm(a, b):
    return lax.dot_general(a, b, (((1,), (0,)), ((), ())), preferred_element_type=F32)


def mm_nt(a, b):
    return lax.dot_general(a, b, (((1,), (1,)), ((), ())), preferred_element_type=F32)


def mm_tn(a, b):
    return lax.dot_general(a, b, (((0,), (0,)), ((), ())), preferred_element_type=F32)


def gelu(h):
    return 0.5 * h * (1.0 + jnp.tanh(0.7978845608 * (h + 0.044715 * h * h * h)))


def gelu_slope(h):
    th = jnp.tanh(0.7978845608 * (h + 0.044715 * h * h * h))
    inner = 0.7978845608 * (1.0 + 3 * 0.044715 * h * h)
    return 0.5 * (1.0 + th) + 0.5 * h * (1.0 - th * th) * inner


def partner(x):
    lane = lax.broadcasted_iota(jnp.int32, x.shape, 1)
    return jnp.where(lane % 2 == 0, pltpu.roll(x, PAIR - 1, 1), pltpu.roll(x, 1, 1))


def turned(x, cosine, sine):
    return x * cosine + partner(x) * sine


def by_head(x):
    lane = lax.broadcasted_iota(jnp.int32, (1, PAIR), 1)
    low = jnp.where(lane < 64, 1.0, 0.0).astype(x.dtype)
    high = jnp.where(lane < 64, 0.0, 1.0).astype(x.dtype)
    return jnp.concatenate([x * low, x * high], axis=0)


def beside(x):
    return jnp.concatenate([x[:ROWS], x[ROWS:]], axis=1)


def heads_of(x):
    return [x[ROWS * j : ROWS * (j + 1)] for j in range(4)]


def rows_of(j):
    return pl.ds(j * ROWS, ROWS)


def layer_norm_into(x_refs, gain_ref, bias_ref, normed):
    for j, x_ref in enumerate(x_refs):
        x = x_ref[0:ROWS, :].astype(F32)
        centered = x - jnp.mean(x, -1, keepdims=True)
        inv = lax.rsqrt(jnp.mean(centered * centered, -1, keepdims=True) + EPS)
        normed[rows_of(j), :] = (centered * inv * gain_ref[...] + bias_ref[...]).astype(BF)


def row_of(fast, g):
    return pl.ds(jnp.bitwise_xor(g, lax.axis_index("section")), 1) if fast else slice(g, g + 1)


def forward_in(fast, g, normed, w, bin_ref, cos_ref, sin_ref, mask_ref, qkv, probs, oa, pre):
    w_qkv, w_in = w[g]
    y = mm(normed[...], w_qkv[...])
    cosine, sine = cos_ref[...], sin_ref[...]
    qkv[g, :, 0:PAIR] = turned(y[:, 0:PAIR], cosine, sine).astype(BF)
    qkv[g, :, PAIR : 2 * PAIR] = turned(y[:, PAIR : 2 * PAIR], cosine, sine).astype(BF)
    qkv[g, :, 2 * PAIR : 3 * PAIR] = y[:, 2 * PAIR : 3 * PAIR].astype(BF)
    q, k, v = (heads_of(qkv[g, :, i * PAIR : (i + 1) * PAIR]) for i in range(3))
    for j in range(4):
        rows = pl.ds(2 * ROWS * j, 2 * ROWS)
        s = mm_nt(by_head(q[j]), k[j]) * SCALE
        s = jnp.where(mask_ref[rows, :] > 0.5, s, NEG)
        e = jnp.exp(s - jnp.max(s, -1, keepdims=True))
        p = e / jnp.sum(e, -1, keepdims=True)
        probs[g, rows, :] = p
        oa[g][rows_of(j), 0:PAIR] = mm(beside(p.astype(BF)), by_head(v[j])).astype(BF)
    h = mm(normed[...], w_in[...]) + bin_ref[row_of(fast, g), :]
    pre[g] = h
    oa[g][:, PAIR:RO] = gelu(h).astype(BF)


def forward_out(oa, w_out, outs):
    for (start, w0), (_, w1) in zip(*w_out):
        for n in range(2):
            part = mm(oa[0][...], w0[:, n * 256 : (n + 1) * 256]) + mm(oa[1][...], w1[:, n * 256 : (n + 1) * 256])
            cols = pl.ds(pl.multiple_of(start + n * 256, 256), 256)
            for j in range(4):
                outs[j][0:ROWS, cols] = part[j * ROWS : (j + 1) * ROWS].astype(outs[j].dtype)


def backward_out(fast, g, gout, w_out, qkv, probs, pre, cos_ref, sin_ref, gcat, gbin_ref):
    halves = [(gout[:, pl.ds(start, 512)], w) for start, w in w_out[g]]
    go = sum(mm_nt(rows, w[0:PAIR, :]) for rows, w in halves).astype(BF)
    q, k, v = (heads_of(qkv[g, :, i * PAIR : (i + 1) * PAIR]) for i in range(3))
    cosine, sine = cos_ref[...], sin_ref[...]
    go = [by_head(rows) for rows in heads_of(go)]
    p = probs[g]
    gp = jnp.concatenate([mm_nt(go[j], v[j]) for j in range(4)], axis=0)
    gs = (p * (gp - jnp.sum(gp * p, -1, keepdims=True))).astype(BF)
    gs = [gs[2 * ROWS * j : 2 * ROWS * (j + 1)] for j in range(4)]
    p = p.astype(BF)
    gq = jnp.concatenate([mm(beside(gs[j]), by_head(k[j])) for j in range(4)], axis=0) * SCALE
    gk = jnp.concatenate([mm_tn(gs[j], by_head(q[j])) for j in range(4)], axis=0) * SCALE
    gv = jnp.concatenate([mm_tn(p[2 * ROWS * j : 2 * ROWS * (j + 1)], go[j]) for j in range(4)], axis=0)
    gcat[g][:, 0:PAIR] = turned(gq, cosine, -sine).astype(BF)
    gcat[g][:, PAIR : 2 * PAIR] = turned(gk, cosine, -sine).astype(BF)
    gcat[g][:, 2 * PAIR : 3 * PAIR] = gv.astype(BF)
    ga = sum(mm_nt(rows, w[PAIR:RO, :]) for rows, w in halves)
    gpre = (ga * gelu_slope(pre[g])).astype(BF)
    gcat[g][:, 3 * PAIR : CI] = gpre
    gbin_ref[row_of(fast, g), :] = jnp.sum(gpre.astype(F32), 0, keepdims=True)


def backward_in(gcat, w, outs):
    for n in range(4):
        cols = slice(n * 256, (n + 1) * 256)
        part = sum(
            mm_nt(gcat[g][:, 0 : 3 * PAIR], w[g][0][cols, :]) + mm_nt(gcat[g][:, 3 * PAIR : CI], w[g][1][cols, :])
            for g in range(2)
        )
        for j in range(4):
            outs[j][0:ROWS, cols] = part[j * ROWS : (j + 1) * ROWS].astype(outs[j].dtype)


A_COLS = D + 2 * RO
B_COLS = CI + 512


def views_a(ship_a):
    return ship_a.at[:, 0:D], (ship_a.at[:, D : D + RO], ship_a.at[:, D + RO : D + 2 * RO])


def views_b(ship_b):
    return ship_b.at[:, 0:CI], ship_b.at[:, CI : CI + 512]


HALF = (2 * D + 2 * RO, 512)


def weights_of(fast, refs):
    if not fast:
        wi, wo = refs
        ins = [(wi.at[g, :, 0 : 3 * PAIR], wi.at[g, :, 3 * PAIR : CI]) for g in range(2)]
        return ins, [[(0, wo.at[g, :, 0:512]), (512, wo.at[g, :, 512:1024])] for g in range(2)]
    core, halves = lax.axis_index("section"), refs
    starts = [pl.multiple_of(512 * c, 512) for c in (core, 1 - core)]
    rows = [pl.ds(pl.multiple_of(2 * D + RO * c, 128), RO) for c in (core, 1 - core)]
    ins = [(half.at[D : 2 * D, 0 : 3 * PAIR], half.at[0:D, :]) for half in halves]
    return ins, [[(start, half.at[rows[g], :]) for start, half in zip(starts, halves)] for g in range(2)]


def weight_loads(fast, refs, held, sems):
    if fast:
        core = lax.axis_index("section")
        halves = refs if len(refs) == 2 else [refs[0].at[core], refs[0].at[1 - core]]
        ins = [pltpu.make_async_copy(h.at[0 : 2 * D], v.at[0 : 2 * D], sems.at[i]) for i, (h, v) in enumerate(zip(halves, held))]
        end = 2 * D + 2 * RO
        outs = [
            pltpu.make_async_copy(h.at[2 * D : end], v.at[2 * D : end], sems.at[2 + i])
            for i, (h, v) in enumerate(zip(halves, held))
        ]
        return ins, outs
    ins = [pltpu.make_async_copy(refs[0].at[g], held[0].at[g], sems.at[g]) for g in range(2)]
    return ins, [pltpu.make_async_copy(refs[1], held[1], sems.at[2])]


def start(copies):
    for copy in copies:
        copy.start()
    return copies


def finish(copies):
    for copy in copies:
        copy.wait()


def moves(sources, targets, sems, first=0):
    return [pltpu.make_async_copy(a, b, sems.at[first + i]) for i, (a, b) in enumerate(zip(sources, targets))]


def place_of():
    return lax.axis_index("dp"), lax.axis_index("section")


def other_half(fast, gout, half_ref):
    core = lax.axis_index("section") if fast else 0
    half_ref[...] = gout[:, pl.ds(pl.multiple_of(512 * (1 - core), 512), 512)]


def join_kernel(own, far, near_own, near_far, *refs):
    pieces, joined, sems = refs[:-2], refs[-2], refs[-1]
    target = joined if len(joined.shape) == 2 else joined.at[0]
    me, _ = place_of()
    copies = []

    def copy(source, rows, cols=slice(None)):
        copies.append(pltpu.make_async_copy(source, target.at[rows, cols], sems.at[len(copies)]))
        copies[-1].start()

    for flip, piece in ((0, own), (8, far), (1, near_own), (9, near_far)):
        source = jnp.bitwise_xor(me, flip)
        g, r = source // 8, source % 2
        base = 2 * D + g * RO
        copy(piece.at[0:64], pl.ds(pl.multiple_of(base + 64 * r, 64), 64))
        copy(piece.at[64:320], pl.ds(pl.multiple_of(base + PAIR + 256 * r, 128), 256))
    blocks = [(ref, i) for ref in pieces for i in range(ref.shape[0])]
    for (ref, i), flip in zip(blocks, [f ^ (2 * j) for f in (0, 8, 1, 9) for j in range(4)]):
        start = pl.multiple_of(jnp.bitwise_xor(me, flip) * 64, 64)
        copy(ref.at[i, :, 3 * PAIR : CI], pl.ds(start, 64))
        copy(ref.at[i, :, 0 : 3 * PAIR], pl.ds(D + start, 64), slice(0, 3 * PAIR))
    for one in copies:
        one.wait()
    if len(joined.shape) == 3:
        joined[1] = joined[0]


def first_forward_kernel(fast, n_w, *refs):
    x_refs, (gain, bias, bin_ref, cos_ref, sin_ref, mask_ref), refs = refs[:4], refs[4:10], refs[10:]
    w_refs, outs, saved, refs = refs[:n_w], refs[n_w : n_w + 4], refs[n_w + 4 : n_w + 8], refs[n_w + 8 :]
    w_held, held, (w_sems, sems) = refs[:2], refs[2:6], refs[6:]
    loads_in, loads_out = weight_loads(fast, w_refs, w_held, w_sems)
    start(loads_in + loads_out)
    w_in, w_out = weights_of(fast, w_held)
    ship_a, qkv, probs, pre = held
    normed, oa = views_a(ship_a)
    layer_norm_into(x_refs, gain, bias, normed)
    puts = []
    for g in range(2):
        finish(loads_in[g : g + 1])
        forward_in(fast, g, normed, w_in, bin_ref, cos_ref, sin_ref, mask_ref, qkv, probs, oa, pre)
        puts += start(moves([h.at[g] for h in held[1:]], [h.at[g] for h in saved[1:]], sems, 1 + 3 * g))
    puts += start(moves(held[:1], saved[:1], sems))
    finish(loads_out)
    forward_out(oa, w_out, outs)
    finish(puts)


def second_layer_kernel(fast, n_w, *refs):
    x_refs, gout_refs, refs = refs[:4], refs[4:8], refs[8:]
    (gain, bias, bin_ref, cos_ref, sin_ref, mask_ref), refs = refs[:6], refs[6:]
    w_refs, refs = refs[:n_w], refs[n_w:]
    if fast:
        core = lax.axis_index("section")
        w_refs = [w_refs[0].at[core], w_refs[0].at[1 - core]]
    w_in, w_out = weights_of(fast, w_refs)
    outs, gouts, gbin_ref, refs = refs[:4], refs[4:8], refs[8], refs[9:]
    ship_a, ship_b, gcat0, qkv, probs, pre, gout = refs
    normed, oa = views_a(ship_a)
    gcat1, gout_half = views_b(ship_b)
    gcat = (gcat0, gcat1)
    layer_norm_into(x_refs, gain, bias, normed)
    for j in range(4):
        gout[rows_of(j), :] = gout_refs[j][...]
    other_half(fast, gout, gout_half)
    for g in range(2):
        forward_in(fast, g, normed, w_in, bin_ref, cos_ref, sin_ref, mask_ref, qkv, probs, oa, pre)
    for g in range(2):
        backward_out(fast, g, gout, w_out, qkv, probs, pre, cos_ref, sin_ref, gcat, gbin_ref)
    backward_in(gcat, w_in, gouts)
    forward_out(oa, w_out, outs)


def first_backward_kernel(fast, n_w, *refs):
    gout_refs, (cos_ref, sin_ref), saved, refs = refs[:4], refs[4:6], refs[6:9], refs[9:]
    w_refs, refs = refs[:n_w], refs[n_w:]
    gouts, gbin_ref, put_refs, refs = refs[:4], refs[4], refs[5:7], refs[7:]
    w_held, held, (ship_b, gcat0, gout, w_sems, sems) = refs[:2], refs[2:5], refs[5:]
    loads_in, loads_out = weight_loads(fast, w_refs, w_held, w_sems)
    loads = [moves([h.at[g] for h in saved], [h.at[g] for h in held], sems, 3 * g) for g in range(2)]
    start(loads_out + loads[0] + loads[1] + loads_in)
    w_in, w_out = weights_of(fast, w_held)
    gcat1, gout_half = views_b(ship_b)
    gcat = (gcat0, gcat1)
    for j in range(4):
        gout[rows_of(j), :] = gout_refs[j][...]
    other_half(fast, gout, gout_half)
    finish(loads_out)
    for g in range(2):
        finish(loads[g])
        backward_out(fast, g, gout, w_out, *held, cos_ref, sin_ref, gcat, gbin_ref)
    puts = start(moves([ship_b, gcat0], put_refs, sems, 6))
    finish(loads_in)
    backward_in(gcat, w_in, gouts)
    finish(puts)


def turn_kernel(ship_a, other_a, put_in, put_out, held_a, held_b, left_in, left_out, sems):
    me, core = place_of()
    g, t, r = me // 8, (me // 2) % 4, me % 2
    loads = start(moves([ship_a, other_a], [held_a, held_b], sems))
    for side, ship in enumerate((held_a, held_b)):
        tokens = slice(side * TOK, (side + 1) * TOK)
        finish(loads[side : side + 1])
        for part in range(2):
            far = jnp.bitwise_xor(g, jnp.bitwise_xor(core, part ^ side))
            flat = ship[:, D + part * RO : D + (part + 1) * RO].T
            for s in range(2):
                near = jnp.bitwise_xor(r, s)
                left_out[near, far, 0:64, tokens] = flat[64 * s : 64 * s + 64]
                left_out[near, far, 64:320, tokens] = flat[PAIR + 256 * s : PAIR + 256 * (s + 1)]
        for far in range(2):
            for j in range(4):
                pair = jnp.bitwise_xor(g, far) * 4 + jnp.bitwise_xor(t, j)
                block = ship[:, pl.ds(pl.multiple_of(pair * PAIR, PAIR), PAIR)].T
                start_row = far * 256 + 64 * j
                for s in range(2):
                    left_in[jnp.bitwise_xor(r, s), start_row : start_row + 64, tokens] = block[64 * s : 64 * s + 64]
    finish(start(moves([left_in, left_out], [put_in, put_out], sems, 2)))


def weight_grad_out_kernel(*refs):
    gout_refs, refs = refs[:4], refs[4:]
    *extras, left_ref, other_b, keep, send, left, right, right_other, sems = refs
    loads = start(
        moves([other_b.at[:, CI : CI + 512], left_ref.at[1], left_ref.at[0]], [right_other, left.at[1], left.at[0]], sems)
    )
    cols = pl.ds(pl.multiple_of(512 * lax.axis_index("section"), 512), 512)
    for j in range(4):
        right[rows_of(j), :] = gout_refs[j][:, cols]
    finish(loads[:1])
    for near, out in ((1, send), (0, keep)):
        finish(loads[2 - near : 3 - near])
        for far in range(2):
            part = mm(left[near, far, :, 0:TOK], right[...]) + mm(left[near, far, :, TOK : 2 * TOK], right_other[...])
            out[far, 0:320, :] = part.astype(BF)
            for extra in extras:
                out[far, 320:336, :] = extra[near, far]


def weight_grad_in_kernel(left_ref, gcat, other_b, keep, send, left, right, right_other, sems):
    sources = [gcat, left_ref.at[1], other_b.at[:, 0:CI], left_ref.at[0]]
    loads = start(moves(sources, [right, left.at[1], right_other, left.at[0]], sems))
    finish(loads[:3])
    for near, out in ((1, send), (0, keep)):
        if near == 0:
            finish(loads[3:])
        part = mm(left[near, :, 0:TOK], right[...]) + mm(left[near, :, TOK : 2 * TOK], right_other[...])
        part = part.astype(BF)
        for i in range(8):
            out[i // 4, i % 4] = part[64 * i : 64 * i + 64]


def whole_grad_out_kernel(*refs):
    gout_refs, (ship_a, out, gout) = refs[:4], refs[4:]
    for j in range(4):
        gout[rows_of(j), :] = gout_refs[j][...]
    for g in range(2):
        out[g] = mm_tn(ship_a[:, D + g * RO : D + (g + 1) * RO], gout[...]).astype(BF)


def whole_grad_in_kernel(ship_a, gcat0, ship_b, out):
    for g in range(2):
        right = gcat0[...] if g == 0 else ship_b[:, 0:CI]
        for m in range(4):
            rows = slice(m * 256, (m + 1) * 256)
            out[g, rows, :] = mm_tn(ship_a[:, rows], right).astype(BF)


def norm_backward_kernel(own, r1, r2, r3, x_ref, gout_ref, gain, gx_ref, low_ref, sums_ref):
    x = x_ref[0:ROWS, :].astype(F32)
    gn = own[...] + sum(r[...].astype(F32) for r in (r1, r2, r3))
    gout = gout_ref[...].astype(F32)
    centered = x - jnp.mean(x, -1, keepdims=True)
    inv = lax.rsqrt(jnp.mean(centered * centered, -1, keepdims=True) + EPS)
    unit = centered * inv
    gu = gn * gain[...]
    gx = gout + inv * (gu - jnp.mean(gu, -1, keepdims=True) - unit * jnp.mean(gu * unit, -1, keepdims=True))
    gx_ref[...] = gx
    low_ref[...] = gx.astype(BF)
    sums_ref[0:1, :] = jnp.sum(gn * unit, 0, keepdims=True)
    sums_ref[1:2, :] = jnp.sum(gn, 0, keepdims=True)
    sums_ref[2:3, :] = jnp.sum(gout, 0, keepdims=True)


def pack_kernel(w_qkv, w_out, w_in, w_fc, wi_keep, wi_send, wo_keep, wo_send):
    t, core = (lax.axis_index("dp") // 2) % 4, lax.axis_index("section")
    for ref, g in ((wi_keep, core), (wi_send, 1 - core)):
        for j in range(4):
            rank = jnp.bitwise_xor(t, j)
            for part in range(3):
                start = pl.multiple_of(part * D + g * 512 + rank * PAIR, PAIR)
                ref[j, :, part * PAIR : (part + 1) * PAIR] = w_qkv[:, pl.ds(start, PAIR)].astype(BF)
            start = pl.multiple_of(g * 2048 + rank * FB, FB)
            ref[j, :, 3 * PAIR : CI] = w_in[:, pl.ds(start, FB)].astype(BF)
    for ref, half in ((wo_keep, core), (wo_send, 1 - core)):
        cols = pl.ds(pl.multiple_of(512 * half, 512), 512)
        ref[0:64, :] = w_out[:, cols].astype(BF)
        ref[64:320, :] = w_fc[:, cols].astype(BF)


def unpack_kernel(own0, own1, own2, own3, other, wo_own, wo_other, g_qkv, g_out, g_in, g_fc):
    t, core = (lax.axis_index("dp") // 2) % 4, lax.axis_index("section")
    for side, g in ((0, core), (1, 1 - core)):
        for j in range(4):
            block = (own0, own1, own2, own3)[j][...] if side == 0 else other[j]
            block = block.astype(F32)
            rank = jnp.bitwise_xor(t, j)
            for part in range(3):
                start = pl.multiple_of(part * D + g * 512 + rank * PAIR, PAIR)
                g_qkv[:, pl.ds(start, PAIR)] = block[:, part * PAIR : (part + 1) * PAIR]
            start = pl.multiple_of(g * 2048 + rank * FB, FB)
            g_in[:, pl.ds(start, FB)] = block[:, 3 * PAIR : CI]
    for ref, half in ((wo_own, core), (wo_other, 1 - core)):
        cols = pl.ds(pl.multiple_of(512 * half, 512), 512)
        g_out[:, cols] = ref[0:64, :].astype(F32)
        g_fc[:, cols] = ref[64:320, :].astype(F32)


VM = pl.BlockSpec(memory_space=pltpu.VMEM)


HB = pl.BlockSpec(memory_space=pl.ANY)


def kernel_call(kernel, args, outs, hbm_args=0, hbm_outs=0, scratch=(), cost=2e10, name=None):
    return pl.pallas_call(
        kernel,
        out_shape=outs,
        in_specs=[VM] * (len(args) - hbm_args) + [HB] * hbm_args,
        out_specs=[VM] * (len(outs) - hbm_outs) + [HB] * hbm_outs,
        scratch_shapes=list(scratch),
        compiler_params=pltpu.CompilerParams(vmem_limit_bytes=GRANTS.get(name, SMALL) * 1024 * 1024),
        cost_estimate=pl.CostEstimate(flops=int(cost), bytes_accessed=1, transcendentals=0),
        name=name,
    )(*args)


def dma(count):
    return pltpu.SemaphoreType.DMA((count,))


def arr(shape, dtype):
    return jax.ShapeDtypeStruct(shape, dtype)


def partial_outs():
    return [arr((ROWS, D), F32)] + [arr((ROWS, D), BF)] * 3


def swap_core(value):
    return lax.ppermute(value, "section", [(0, 1), (1, 0)])


def flipped(value, flip):
    count = lax.axis_size("dp")
    return lax.ppermute(value, "dp", [(i, i ^ flip) for i in range(count)])


def after(value, *earlier):
    return lax.optimization_barrier((value, earlier))[0]


def choose(own, other):
    first_core = lax.axis_index("section") == 0
    return jnp.where(first_core, own, other), jnp.where(first_core, other, own)


def across(values):
    spread = lax.axis_size("dp") // 8
    return [flipped(v, (j + 1) * spread) for j, v in enumerate(values)]


def groups_of(spread):
    places = [[[g * 4 * spread + t * spread + r for r in range(spread)] for t in range(4)] for g in range(2)]
    t_groups = [[places[g][t][r] for t in range(4)] for g in range(2) for r in range(spread)]
    f_groups = [[places[g][t][r] for g in range(2) for r in range(spread)] for t in range(4)]
    return t_groups, f_groups


def any_gather(w_qkv, w_out, w_in, w_fc):
    share, spread = w_qkv.shape[0], lax.axis_size("dp") // 8
    t_groups, f_groups = groups_of(spread)
    qkv = w_qkv.reshape(share, 3, 2, 4, PAIR).transpose(3, 0, 2, 1, 4).reshape(4, share, 2, 3 * PAIR)
    wi = jnp.concatenate([qkv, w_in.reshape(share, 2, 4, FB).transpose(2, 0, 1, 3)], axis=-1).astype(BF)
    wi = lax.all_to_all(wi, "dp", 0, 0, axis_index_groups=t_groups, tiled=True)
    wi = lax.all_gather(wi, "dp", axis_index_groups=f_groups)
    wi = wi.reshape(2, spread, 4, share, 2, CI).transpose(4, 0, 2, 1, 3, 5).reshape(2, D, CI)
    wo = lax.all_gather(w_out.astype(BF), "dp", axis_index_groups=f_groups).reshape(2, PAIR, D)
    wf = lax.all_gather(w_fc.astype(BF), "dp", axis_index_groups=f_groups).reshape(2, FB, D)
    wo = jnp.concatenate([wo, wf], axis=1)
    return choose(wi, swap_core(wi)), choose(wo, swap_core(wo))


def any_reduce(gi, go):
    count = lax.axis_size("dp")
    spread, share = count // 8, D // count
    t_groups, f_groups = groups_of(spread)

    def scattered(value):
        return lax.psum_scatter(value, "dp", scatter_dimension=0, axis_index_groups=f_groups)

    gi = gi.reshape(2, 2, 4, spread, share, CI).transpose(1, 3, 2, 4, 0, 5).reshape(2 * spread, 4, share, 2, CI)
    gi = lax.all_to_all(scattered(gi), "dp", 0, 0, axis_index_groups=t_groups, tiled=True)
    g_qkv = gi[..., : 3 * PAIR].reshape(4, share, 2, 3, PAIR).transpose(1, 3, 2, 0, 4).reshape(share, 3 * D)
    g_in = gi[..., 3 * PAIR :].transpose(1, 2, 0, 3).reshape(share, 4 * D)
    g_out = scattered(go[:, :PAIR].reshape(2 * spread, share, D))
    g_fc = scattered(go[:, PAIR:].reshape(2 * spread, 4 * share, D))
    return g_qkv, g_out, g_in, g_fc


def body(boundary, segments, ln_gain, ln_bias, w_qkv, w_out, w_in, b_in, w_fc, b_fc):
    core, me = lax.axis_index("section"), lax.axis_index("dp")
    count = lax.axis_size("dp")
    fast = count == 16
    spread = count // 8
    rank = (me // spread) % 4
    share = D // count
    width_small = 7 * share
    first_core = core == 0

    if fast:
        small = jnp.concatenate([ln_gain, ln_bias, b_fc, b_in], axis=-1).astype(BF)

    if fast:
        wi_keep, wi_send, wo_keep, wo_send = kernel_call(
            pack_kernel,
            [w_qkv[0], w_out[0], w_in[0], w_fc[0]],
            [arr((4, 64, CI), BF), arr((4, 64, CI), BF), arr((320, 512), BF), arr((320, 512), BF)],
            name="pack",
        )
        wi_recv, wo_recv = swap_core(wi_send), swap_core(wo_send)
        wi_first = [choose(wi_keep[j], wi_recv[j]) for j in range(4)]
        wo_first = choose(wo_keep, wo_recv)
        boundary, segments = after((boundary, segments), wi_keep)
    else:
        wi_both, wo_both = any_gather(w_qkv[0], w_out[0], w_in[0], w_fc[0])

    swapped = swap_core(lax.dynamic_index_in_dim(boundary[0], 1 - core, 0, False)[0])
    kept = lax.dynamic_index_in_dim(boundary[0], core, 0, False)[0]
    x0, g1 = choose(kept, swapped)
    if not fast:
        small = jnp.concatenate([ln_gain, ln_bias, b_fc, b_in], axis=-1).astype(BF)
        small = jnp.concatenate(choose(small, swap_core(small)))
    seg = lax.dynamic_index_in_dim(segments, core, 0, False)[0].astype(BF)
    extra = jnp.zeros((16, D), BF).at[0, :ROWS].set(seg)
    if fast:

        def join(wi_pieces, wo_pieces, name):
            pieces, sems = [*wo_pieces, *wi_pieces], [pltpu.SemaphoreType.DMA((40,))]
            if name == "join0":
                own = kernel_call(join_kernel, pieces, [arr(HALF, BF)], 8, 0, sems, 1, name)[0]
                return own
            both = kernel_call(join_kernel, pieces, [arr((2, *HALF), BF)], 8, 0, sems, 1, name)[0]
            return lax.all_to_all(both, "section", 0, 0, tiled=True)

        mine = [after(jnp.stack(w), wo_first) for w in wi_first]
        arrived = across(mine[1:])
        wi_own, wi_own1 = (jnp.stack([w[l] for w in [mine[0], *arrived]]) for l in range(2))
        wo_own, wo_own1 = wo_first
        wo_far, wo_near = flipped(wo_own, 8), flipped(wo_own, 1)
        wi_far, wi_near = flipped(after(wi_own, wo_far), 8), flipped(wi_own, 1)
        wo_near_far = flipped(wo_far, 1)
        small = after(small, wo_near)
        small = jnp.concatenate([small, flipped(small, 1)])
        small = jnp.concatenate([small, flipped(small, 8)])
        small = jnp.stack(choose(small, swap_core(small)), axis=1).reshape(8, width_small)
        extra = extra.at[1:9, :width_small].set(small)
        pack = jnp.concatenate([x0, extra])
        packs = [pack] + across(after([pack] * 3, arrived))
        g1s = [g1] + across(after([g1] * 3, packs))
        wo_far1, wi_far1 = flipped(after(wo_own1, wi_far), 8), flipped(after(wi_own1, wi_far), 8)

        held = jnp.stack([p[129:137, :width_small] for p in packs])
        held = held.reshape(16, 2 * width_small)
        index = jnp.arange(16)
        flip_of = jnp.bitwise_xor(index, me)
        at = (flip_of // 2) % 4 * 4 + (flip_of // 8) * 2 + flip_of % 2
        onehot = (at[:, None] == index[None, :]).astype(BF)
        everyone = mm(onehot, held).reshape(16, 2, width_small)
    else:
        w0, w1 = ([wi_both[l], wo_both[l]] for l in range(2))
        pack = jnp.concatenate([x0, extra])
        packs, g1s = [pack] + across([pack] * 3), [g1] + across([g1] * 3)
        everyone = lax.all_gather(small, "dp").astype(F32)

    def small_of(layer):
        one = everyone[:, layer]
        vectors = [one[:, i * share : (i + 1) * share].reshape(1, D) for i in range(3)]
        b = one[:, 3 * share :].reshape(2, 4, FB)
        return *vectors, lax.dynamic_index_in_dim(b, rank, 1, False)

    gain0, bias0, bfc0, bin0 = small_of(0)
    gain1, bias1, bfc1, bin1 = small_of(1)

    segs = jnp.stack([p[ROWS, :ROWS] for p in packs])
    row = lax.broadcasted_iota(jnp.int32, (ROWS, ROWS), 0)
    col = lax.broadcasted_iota(jnp.int32, (ROWS, ROWS), 1)
    mask = ((segs[:, :, None] == segs[:, None, :]) & (col <= row)).astype(F32)
    positions = jnp.sum(mask, -1).reshape(TOK, 1) - 1.0
    mask = jnp.stack([mask, mask], axis=1).reshape(8 * ROWS, ROWS)
    lane = jnp.arange(PAIR) % 64
    freq = jnp.where(lane < 32, 10000.0 ** (-(lane // 2 * 2).astype(F32) / 32), 0.0)
    angle = positions * freq
    cosine = jnp.cos(angle)
    sine = jnp.sin(angle) * jnp.where(lane % 2 == 0, -1.0, 1.0)

    if fast:
        tables = (gain0, bias0, bin0, cosine, sine, mask, gain1, bias1, bin1, bfc0, bfc1)
        wi_near_far = flipped(after(wi_far, wo_near_far, wi_near, wo_near), 1)
        wi_got = [wi_own, wi_far, wi_near, wi_near_far]
        w0 = join(after(wi_got, tables), [wo_own, wo_far, wo_near, wo_near_far], "join0")
        w0 = [w0, swap_core(after(w0, wo_far1, g1s))]
        wo_near1, wi_near1 = flipped(after(wo_own1, wi_near_far), 1), flipped(after(wi_own1, wi_near_far), 1)

    held_weights = [pltpu.VMEM(HALF, BF)] * 2 if fast else [pltpu.VMEM((2, D, CI), BF), pltpu.VMEM((2, RO, D), BF)]

    saved = [
        arr((TOK, A_COLS), BF),
        arr((2, TOK, 3 * PAIR), BF),
        arr((2, 8 * ROWS, ROWS), F32),
        arr((2, TOK, FB), F32),
    ]
    got = kernel_call(
        functools.partial(first_forward_kernel, fast, len(w0)),
        [*packs, gain0, bias0, bin0, cosine, sine, mask, *w0],
        partial_outs() + saved,
        hbm_args=2,
        hbm_outs=4,
        scratch=[*held_weights, *(pltpu.VMEM(a.shape, a.dtype) for a in saved), dma(4), dma(7)],
        cost=1,
        name="first_forward",
    )
    own, sends, (ship_a0, qkv0, probs0, pre0) = got[0], got[1:4], got[4:]

    def total(own, arrived):
        return sum([r.astype(F32) for r in arrived], own)

    arrived = across(sends)
    sums = total(own, arrived)
    if fast:
        wo_near_far1 = flipped(after(wo_far1, own, wo_near1), 1)
        wi_near_far1 = flipped(after(wi_far1, own, wi_near1), 1)
        w1 = join([wi_own1, wi_far1, wi_near1, wi_near_far1], [wo_own1, wo_far1, wo_near1, wo_near_far1], "join1")
        w1 = [w1]
    x1 = (x0.astype(F32) + sums + bfc0).astype(BF)
    x1s = [x1] + across([x1] * 3)

    back_outs = [arr((TOK, B_COLS), BF), arr((TOK, CI), BF)]
    got = kernel_call(
        functools.partial(second_layer_kernel, fast, len(w1)),
        [*x1s, *g1s, gain1, bias1, bin1, cosine, sine, mask, *w1],
        [*partial_outs(), *partial_outs(), arr((2, FB), F32), arr((TOK, A_COLS), BF), *back_outs],
        scratch=[*(pltpu.VMEM(a.shape, a.dtype) for a in saved[1:]), pltpu.VMEM((TOK, D), BF)],
        name="second_layer",
    )
    out_own, out_sends, gn_own, gn_sends = got[0], got[1:4], got[4], got[5:8]
    gbin1, ship_a1, ship_b1, gcat1 = got[8:]

    def norm_backward(own, arrived, x, gout, gain, name):
        return kernel_call(
            norm_backward_kernel,
            [own, *arrived, x, gout, gain],
            [arr((ROWS, D), F32), arr((ROWS, D), BF), arr((3, D), F32)],
            name=name,
        )

    def turned_ships(ship_a, other_a, name):
        outs = [arr((2, 512, 2 * TOK), BF), arr((2, 2, 320, 2 * TOK), BF)]
        if not fast:
            return ship_a, ship_a
        scratch = [pltpu.VMEM((TOK, A_COLS), BF)] * 2 + [pltpu.VMEM(a.shape, BF) for a in outs] + [dma(4)]
        return kernel_call(turn_kernel, [ship_a, other_a], outs, 2, 2, scratch, name=name)

    def grads_out(gouts, left, other_b, extra, name):
        if fast:
            extras = [] if extra is None else [extra]
            return kernel_call(
                weight_grad_out_kernel,
                [*gouts, *extras, left, other_b],
                [arr((2, 320 + 16 * len(extras), 512), BF)] * 2,
                hbm_args=2,
                scratch=[pltpu.VMEM(left.shape, BF), pltpu.VMEM((TOK, 512), BF), pltpu.VMEM((TOK, 512), BF), dma(3)],
                name=name,
            )
        scratch = [pltpu.VMEM((TOK, D), BF)]
        return kernel_call(whole_grad_out_kernel, [*gouts, left], [arr((2, RO, D), BF)], scratch=scratch, name=name)

    def grads_in(left, ship_b, other_b, gcat, name):
        if fast:
            scratch = [pltpu.VMEM(left.shape, BF), pltpu.VMEM((TOK, CI), BF), pltpu.VMEM((TOK, CI), BF), dma(4)]
            outs = [arr((2, 4, 64, CI), BF)] * 2
            return kernel_call(weight_grad_in_kernel, [left, gcat, other_b], outs, 3, 0, scratch, name=name)
        return kernel_call(whole_grad_in_kernel, [left, gcat, ship_b], [arr((2, D, CI), BF)], name=name)

    def onward(keep, near):
        return flipped((keep[1].astype(F32) + near[1].astype(F32)).astype(BF), 8)

    def reduced(keep, near, far):
        return keep[0].astype(F32) + near[0].astype(F32) + far.astype(F32)

    arrived_gn = across(gn_sends)
    other_a1, other_b1 = (swap_core(ship_a1), swap_core(ship_b1)) if fast else (None, None)
    other_a0 = swap_core(ship_a0) if fast else None
    left_in1, left_out1 = turned_ships(after(ship_a1, other_a0), other_a1, "turn1")
    go1 = grads_out(g1s, left_out1, other_b1, None, "grads1_out")
    _, g0, sums1 = norm_backward(after(gn_own, go1), arrived_gn, x1, g1, gain1, "norm_backward1")
    g0s = [g0] + across([g0] * 3)
    gi1 = grads_in(after(left_in1, g0), ship_b1, other_b1, gcat1, "grads1_in")
    left_in0, left_out0 = turned_ships(after(ship_a0, g0), other_a0, "turn0")
    if fast:
        keep1, send1 = zip(go1, gi1)
        near1 = [flipped(v, 1) for v in send1]
        far1 = [onward(k, v) for k, v in zip(keep1, near1)]
        g0s[0] = after(g0, near1[0], gi1, left_in0)

    got = kernel_call(
        functools.partial(first_backward_kernel, fast, len(w0)),
        [*g0s, cosine, sine, qkv0, probs0, pre0, *w0],
        [*partial_outs(), arr((2, FB), F32), *back_outs],
        hbm_args=5,
        hbm_outs=2,
        scratch=[
            *held_weights,
            *(pltpu.VMEM(a.shape, a.dtype) for a in saved[1:]),
            *(pltpu.VMEM((TOK, cols), BF) for cols in (B_COLS, CI, D)),
            dma(4),
            dma(8),
        ],
        name="first_backward",
    )
    gn_own, gn_sends, (gbin0, ship_b0, gcat0) = got[0], got[1:4], got[4:]
    arrived_gn = across(gn_sends)
    if fast:
        other_b0 = swap_core(after(ship_b0, near1[1], far1[0]))
    else:
        other_b0 = None
    gi0 = grads_in(left_in0, ship_b0, other_b0, gcat0, "grads0_in")
    gx0, _, sums0 = norm_backward(after(gn_own, gi0), arrived_gn, x0, g0, gain0, "norm_backward0")

    def small_grads(sums, gbin):
        onehot = (jnp.arange(4) == rank).astype(F32)
        vectors = sums.reshape(3, 2, 4, spread, share).transpose(1, 2, 3, 0, 4).reshape(2, 4, spread, 3 * share)
        b = gbin.reshape(2, 1, spread, 4 * share)
        return (vectors, b) if fast else jnp.concatenate([vectors, b * onehot[None, :, None, None]], axis=-1)

    both = jax.tree.map(choose, small_grads(sums0, gbin0), small_grads(sums1, gbin1))
    if fast:
        mine, theirs = (jnp.concatenate([v[i].reshape(-1) for v in both]) for i in range(2))
        mine = mine + swap_core(theirs)
        vectors, b = mine[: 3 * D].reshape(2, 4, 2, 192), mine[3 * D :].reshape(2, 1, 2, 256)
        values = jnp.concatenate([vectors.transpose(2, 0, 1, 3).reshape(2, 2, 768), b[:, 0].transpose(1, 0, 2)], axis=-1)
        values = jnp.where(me // 8 == 0, values, values[:, ::-1])
        values = jnp.where(me % 2 == 0, values, values[::-1])
        extra = jnp.zeros((2, 2, 16, 512), BF).at[:, :, :2].set(values.reshape(2, 2, 2, 512).astype(BF))
        wo_1, wi_1 = (reduced(*v).astype(BF) for v in zip(keep1, near1, far1))
        near_in0 = flipped(gi0[1], 1)
        far_in0 = onward(gi0[0], near_in0)
        extra = after(extra, wi_1, near_in0)
    else:
        extra = None
    go0 = grads_out(g0s, left_out0, other_b0, extra, "grads0_out")

    out1 = x1.astype(F32) + total(out_own, across(after(out_sends, near_in0) if fast else out_sends)) + bfc1
    arrived = swap_core(jnp.where(first_core, out1, gx0))
    boundary_out = jnp.where(first_core, jnp.stack([gx0, arrived]), jnp.stack([arrived, out1]))[None, :, None]
    if fast:
        near_out0 = flipped(go0[1], 1)
        far_out0 = onward(go0[0], near_out0)
        wo_0 = reduced(go0[0], near_out0, far_out0)
        shares = [reduced(gi0[0], near_in0, far_in0), wi_1]
        vector = wo_0[320:322].reshape(1024)
        ranks = vector[:768].reshape(4, 192)
        ranks = [lax.dynamic_index_in_dim(ranks, jnp.bitwise_xor(rank, j), 0, True) for j in range(4)]
        summed = sum([r.astype(F32) for r in across([r.astype(BF) for r in ranks[1:]])], ranks[0])
        vector = jnp.concatenate([summed, vector[None, 768:]], axis=1)
        wo_0 = wo_0[:320].astype(BF)
        shares = [jnp.concatenate([shares[0][j].astype(BF), shares[1][j]]) for j in range(4)]
        arrived = [shares[0]] + across(after(shares[1:], out1, near_out0))
        wo_mine, wo_theirs = choose(wo_0, wo_1)
        pairs = [choose(w[:64], w[64:]) for w in arrived]
        wi_other = swap_core(jnp.stack([p[1] for p in pairs]))
        g_qkv, g_out, g_in, g_fc = kernel_call(
            unpack_kernel,
            [*[p[0] for p in pairs], wi_other, wo_mine, swap_core(wo_theirs)],
            [arr((64, 3 * D), F32), arr((64, D), F32), arr((64, 4 * D), F32), arr((256, D), F32)],
            name="unpack",
        )
    else:
        vector = (both[0] + swap_core(both[1])).reshape(count, 7 * share)
        vector = lax.psum_scatter(vector, "dp", scatter_dimension=0, tiled=True)
        mine, theirs = choose(gi0[0], gi1[0])
        gi = mine.astype(F32) + swap_core(theirs).astype(F32)
        mine, theirs = choose(go0[0], go1[0])
        go = mine.astype(F32) + swap_core(theirs).astype(F32)
        g_qkv, g_out, g_in, g_fc = any_reduce(gi, go)
    g_gain, g_bias, g_bfc = (vector[:, i * share : (i + 1) * share] for i in range(3))
    g_bin = vector[:, 3 * share :]

    return (boundary_out, g_gain, g_bias, g_qkv[None], g_out[None], g_in[None], g_bin, g_fc[None], g_bfc)


def solution(mesh):
    rows = P("section", None, "dp", None, None)
    vector, matrix = P("section", "dp"), P("section", "dp", None)
    return jax.shard_map(
        body,
        mesh=mesh,
        in_specs=(rows, P(None, "dp", None), vector, vector, matrix, matrix, matrix, vector, matrix, vector),
        out_specs=(rows, vector, vector, matrix, matrix, matrix, vector, matrix, vector),
        check_vma=False,
    )
```

```python
import functools

import jax
import jax.numpy as jnp
from jax import lax
from jax.experimental import pallas as pl
from jax.experimental.pallas import tpu as pltpu
from jax.sharding import PartitionSpec as P

D = 1024
PAIR = 128
FB = 512
CI = 3 * PAIR + FB
RO = PAIR + FB
EPS = 1e-05
NEG = -1000000000.0
SCALE = 0.125
ROWS = 128
TOK = 4 * ROWS
BF = jnp.bfloat16
F32 = jnp.float32
SMALL, LARGE = 24, 56
GRANTS = {"turn0": LARGE, "grads0_in": LARGE, "join0": LARGE, "first_forward": LARGE, "first_backward": LARGE, "grads0_out": LARGE, "pack": LARGE, "norm_backward0": LARGE}


def mm(a, b):
    return lax.dot_general(a, b, (((1,), (0,)), ((), ())), preferred_element_type=F32)


def mm_nt(a, b):
    return lax.dot_general(a, b, (((1,), (1,)), ((), ())), preferred_element_type=F32)


def mm_tn(a, b):
    return lax.dot_general(a, b, (((0,), (0,)), ((), ())), preferred_element_type=F32)


def gelu(h):
    return 0.5 * h * (1.0 + jnp.tanh(0.7978845608 * (h + 0.044715 * h * h * h)))


def gelu_slope(h):
    th = jnp.tanh(0.7978845608 * (h + 0.044715 * h * h * h))
    inner = 0.7978845608 * (1.0 + 3 * 0.044715 * h * h)
    return 0.5 * (1.0 + th) + 0.5 * h * (1.0 - th * th) * inner


def partner(x):
    lane = lax.broadcasted_iota(jnp.int32, x.shape, 1)
    return jnp.where(lane % 2 == 0, pltpu.roll(x, PAIR - 1, 1), pltpu.roll(x, 1, 1))


def turned(x, cosine, sine):
    return x * cosine + partner(x) * sine


def by_head(x):
    lane = lax.broadcasted_iota(jnp.int32, (1, PAIR), 1)
    low = jnp.where(lane < 64, 1.0, 0.0).astype(x.dtype)
    high = jnp.where(lane < 64, 0.0, 1.0).astype(x.dtype)
    return jnp.concatenate([x * low, x * high], axis=0)


def beside(x):
    return jnp.concatenate([x[:ROWS], x[ROWS:]], axis=1)


def heads_of(x):
    return [x[ROWS * j : ROWS * (j + 1)] for j in range(4)]


def rows_of(j):
    return pl.ds(j * ROWS, ROWS)


def layer_norm_into(x_refs, gain_ref, bias_ref, normed):
    for j, x_ref in enumerate(x_refs):
        x = x_ref[0:ROWS, :].astype(F32)
        centered = x - jnp.mean(x, -1, keepdims=True)
        inv = lax.rsqrt(jnp.mean(centered * centered, -1, keepdims=True) + EPS)
        normed[rows_of(j), :] = (centered * inv * gain_ref[...] + bias_ref[...]).astype(BF)


def row_of(fast, g):
    return pl.ds(jnp.bitwise_xor(g, lax.axis_index("section")), 1) if fast else slice(g, g + 1)


def forward_in(fast, g, normed, w, bin_ref, cos_ref, sin_ref, mask_ref, qkv, probs, oa, pre):
    w_qkv, w_in = w[g]
    y = mm(normed[...], w_qkv[...])
    cosine, sine = cos_ref[...], sin_ref[...]
    qkv[g, :, 0:PAIR] = turned(y[:, 0:PAIR], cosine, sine).astype(BF)
    qkv[g, :, PAIR : 2 * PAIR] = turned(y[:, PAIR : 2 * PAIR], cosine, sine).astype(BF)
    qkv[g, :, 2 * PAIR : 3 * PAIR] = y[:, 2 * PAIR : 3 * PAIR].astype(BF)
    q, k, v = (heads_of(qkv[g, :, i * PAIR : (i + 1) * PAIR]) for i in range(3))
    for j in range(4):
        rows = pl.ds(2 * ROWS * j, 2 * ROWS)
        s = mm_nt(by_head(q[j]), k[j]) * SCALE
        s = jnp.where(mask_ref[rows, :] > 0.5, s, NEG)
        e = jnp.exp(s - jnp.max(s, -1, keepdims=True))
        p = e / jnp.sum(e, -1, keepdims=True)
        probs[g, rows, :] = p
        oa[g][rows_of(j), 0:PAIR] = mm(beside(p.astype(BF)), by_head(v[j])).astype(BF)
    h = mm(normed[...], w_in[...]) + bin_ref[row_of(fast, g), :]
    pre[g] = h
    oa[g][:, PAIR:RO] = gelu(h).astype(BF)


def forward_out(oa, w_out, outs):
    for (start, w0), (_, w1) in zip(*w_out):
        for n in range(2):
            part = mm(oa[0][...], w0[:, n * 256 : (n + 1) * 256]) + mm(oa[1][...], w1[:, n * 256 : (n + 1) * 256])
            cols = pl.ds(pl.multiple_of(start + n * 256, 256), 256)
            for j in range(4):
                outs[j][0:ROWS, cols] = part[j * ROWS : (j + 1) * ROWS].astype(outs[j].dtype)


def backward_out(fast, g, gout, w_out, qkv, probs, pre, cos_ref, sin_ref, gcat, gbin_ref):
    halves = [(gout[:, pl.ds(start, 512)], w) for start, w in w_out[g]]
    go = sum(mm_nt(rows, w[0:PAIR, :]) for rows, w in halves).astype(BF)
    q, k, v = (heads_of(qkv[g, :, i * PAIR : (i + 1) * PAIR]) for i in range(3))
    cosine, sine = cos_ref[...], sin_ref[...]
    go = [by_head(rows) for rows in heads_of(go)]
    p = probs[g]
    gp = jnp.concatenate([mm_nt(go[j], v[j]) for j in range(4)], axis=0)
    gs = (p * (gp - jnp.sum(gp * p, -1, keepdims=True))).astype(BF)
    gs = [gs[2 * ROWS * j : 2 * ROWS * (j + 1)] for j in range(4)]
    p = p.astype(BF)
    gq = jnp.concatenate([mm(beside(gs[j]), by_head(k[j])) for j in range(4)], axis=0) * SCALE
    gk = jnp.concatenate([mm_tn(gs[j], by_head(q[j])) for j in range(4)], axis=0) * SCALE
    gv = jnp.concatenate([mm_tn(p[2 * ROWS * j : 2 * ROWS * (j + 1)], go[j]) for j in range(4)], axis=0)
    gcat[g][:, 0:PAIR] = turned(gq, cosine, -sine).astype(BF)
    gcat[g][:, PAIR : 2 * PAIR] = turned(gk, cosine, -sine).astype(BF)
    gcat[g][:, 2 * PAIR : 3 * PAIR] = gv.astype(BF)
    ga = sum(mm_nt(rows, w[PAIR:RO, :]) for rows, w in halves)
    gpre = (ga * gelu_slope(pre[g])).astype(BF)
    gcat[g][:, 3 * PAIR : CI] = gpre
    gbin_ref[row_of(fast, g), :] = jnp.sum(gpre.astype(F32), 0, keepdims=True)


def backward_in(gcat, w, outs):
    for n in range(4):
        cols = slice(n * 256, (n + 1) * 256)
        part = sum(
            mm_nt(gcat[g][:, 0 : 3 * PAIR], w[g][0][cols, :]) + mm_nt(gcat[g][:, 3 * PAIR : CI], w[g][1][cols, :])
            for g in range(2)
        )
        for j in range(4):
            outs[j][0:ROWS, cols] = part[j * ROWS : (j + 1) * ROWS].astype(outs[j].dtype)


A_COLS = D + 2 * RO
B_COLS = CI + 512


def views_a(ship_a):
    return ship_a.at[:, 0:D], (ship_a.at[:, D : D + RO], ship_a.at[:, D + RO : D + 2 * RO])


def views_b(ship_b):
    return ship_b.at[:, 0:CI], ship_b.at[:, CI : CI + 512]


HALF = (2 * D + 2 * RO, 512)


def weights_of(fast, refs):
    if not fast:
        wi, wo = refs
        ins = [(wi.at[g, :, 0 : 3 * PAIR], wi.at[g, :, 3 * PAIR : CI]) for g in range(2)]
        return ins, [[(0, wo.at[g, :, 0:512]), (512, wo.at[g, :, 512:1024])] for g in range(2)]
    core, halves = lax.axis_index("section"), refs
    starts = [pl.multiple_of(512 * c, 512) for c in (core, 1 - core)]
    rows = [pl.ds(pl.multiple_of(2 * D + RO * c, 128), RO) for c in (core, 1 - core)]
    ins = [(half.at[D : 2 * D, 0 : 3 * PAIR], half.at[0:D, :]) for half in halves]
    return ins, [[(start, half.at[rows[g], :]) for start, half in zip(starts, halves)] for g in range(2)]


def weight_loads(fast, refs, held, sems):
    if fast:
        core = lax.axis_index("section")
        halves = refs if len(refs) == 2 else [refs[0].at[core], refs[0].at[1 - core]]
        ins = [pltpu.make_async_copy(h.at[0 : 2 * D], v.at[0 : 2 * D], sems.at[i]) for i, (h, v) in enumerate(zip(halves, held))]
        end = 2 * D + 2 * RO
        outs = [
            pltpu.make_async_copy(h.at[2 * D : end], v.at[2 * D : end], sems.at[2 + i])
            for i, (h, v) in enumerate(zip(halves, held))
        ]
        return ins, outs
    ins = [pltpu.make_async_copy(refs[0].at[g], held[0].at[g], sems.at[g]) for g in range(2)]
    return ins, [pltpu.make_async_copy(refs[1], held[1], sems.at[2])]


def start(copies):
    for copy in copies:
        copy.start()
    return copies


def finish(copies):
    for copy in copies:
        copy.wait()


def moves(sources, targets, sems, first=0):
    return [pltpu.make_async_copy(a, b, sems.at[first + i]) for i, (a, b) in enumerate(zip(sources, targets))]


def place_of():
    return lax.axis_index("dp"), lax.axis_index("section")


def other_half(fast, gout, half_ref):
    core = lax.axis_index("section") if fast else 0
    half_ref[...] = gout[:, pl.ds(pl.multiple_of(512 * (1 - core), 512), 512)]


def join_kernel(own, far, near_own, near_far, *refs):
    pieces, joined, sems = refs[:-2], refs[-2], refs[-1]
    target = joined if len(joined.shape) == 2 else joined.at[0]
    me, _ = place_of()
    copies = []

    def copy(source, rows, cols=slice(None)):
        copies.append(pltpu.make_async_copy(source, target.at[rows, cols], sems.at[len(copies)]))
        copies[-1].start()

    for flip, piece in ((0, own), (8, far), (1, near_own), (9, near_far)):
        source = jnp.bitwise_xor(me, flip)
        g, r = source // 8, source % 2
        base = 2 * D + g * RO
        copy(piece.at[0:64], pl.ds(pl.multiple_of(base + 64 * r, 64), 64))
        copy(piece.at[64:320], pl.ds(pl.multiple_of(base + PAIR + 256 * r, 128), 256))
    blocks = [(ref, i) for ref in pieces for i in range(ref.shape[0])]
    for (ref, i), flip in zip(blocks, [f ^ (2 * j) for f in (0, 8, 1, 9) for j in range(4)]):
        start = pl.multiple_of(jnp.bitwise_xor(me, flip) * 64, 64)
        copy(ref.at[i, :, 3 * PAIR : CI], pl.ds(start, 64))
        copy(ref.at[i, :, 0 : 3 * PAIR], pl.ds(D + start, 64), slice(0, 3 * PAIR))
    for one in copies:
        one.wait()
    if len(joined.shape) == 3:
        joined[1] = joined[0]


def first_forward_kernel(fast, n_w, *refs):
    x_refs, (gain, bias, bin_ref, cos_ref, sin_ref, mask_ref), refs = refs[:4], refs[4:10], refs[10:]
    w_refs, outs, saved, refs = refs[:n_w], refs[n_w : n_w + 4], refs[n_w + 4 : n_w + 8], refs[n_w + 8 :]
    w_held, held, (w_sems, sems) = refs[:2], refs[2:6], refs[6:]
    loads_in, loads_out = weight_loads(fast, w_refs, w_held, w_sems)
    start(loads_in + loads_out)
    w_in, w_out = weights_of(fast, w_held)
    ship_a, qkv, probs, pre = held
    normed, oa = views_a(ship_a)
    layer_norm_into(x_refs, gain, bias, normed)
    puts = []
    for g in range(2):
        finish(loads_in[g : g + 1])
        forward_in(fast, g, normed, w_in, bin_ref, cos_ref, sin_ref, mask_ref, qkv, probs, oa, pre)
        puts += start(moves([h.at[g] for h in held[1:]], [h.at[g] for h in saved[1:]], sems, 1 + 3 * g))
    puts += start(moves(held[:1], saved[:1], sems))
    finish(loads_out)
    forward_out(oa, w_out, outs)
    finish(puts)


def second_layer_kernel(fast, n_w, *refs):
    x_refs, gout_refs, refs = refs[:4], refs[4:8], refs[8:]
    (gain, bias, bin_ref, cos_ref, sin_ref, mask_ref), refs = refs[:6], refs[6:]
    w_refs, refs = refs[:n_w], refs[n_w:]
    if fast:
        core = lax.axis_index("section")
        w_refs = [w_refs[0].at[core], w_refs[0].at[1 - core]]
    w_in, w_out = weights_of(fast, w_refs)
    outs, gouts, gbin_ref, refs = refs[:4], refs[4:8], refs[8], refs[9:]
    ship_a, ship_b, gcat0, qkv, probs, pre, gout = refs
    normed, oa = views_a(ship_a)
    gcat1, gout_half = views_b(ship_b)
    gcat = (gcat0, gcat1)
    layer_norm_into(x_refs, gain, bias, normed)
    for j in range(4):
        gout[rows_of(j), :] = gout_refs[j][...]
    other_half(fast, gout, gout_half)
    for g in range(2):
        forward_in(fast, g, normed, w_in, bin_ref, cos_ref, sin_ref, mask_ref, qkv, probs, oa, pre)
    for g in range(2):
        backward_out(fast, g, gout, w_out, qkv, probs, pre, cos_ref, sin_ref, gcat, gbin_ref)
    backward_in(gcat, w_in, gouts)
    forward_out(oa, w_out, outs)


def first_backward_kernel(fast, n_w, *refs):
    gout_refs, (cos_ref, sin_ref), saved, refs = refs[:4], refs[4:6], refs[6:9], refs[9:]
    w_refs, refs = refs[:n_w], refs[n_w:]
    gouts, gbin_ref, put_refs, refs = refs[:4], refs[4], refs[5:7], refs[7:]
    w_held, held, (ship_b, gcat0, gout, w_sems, sems) = refs[:2], refs[2:5], refs[5:]
    loads_in, loads_out = weight_loads(fast, w_refs, w_held, w_sems)
    loads = [moves([h.at[g] for h in saved], [h.at[g] for h in held], sems, 3 * g) for g in range(2)]
    start(loads_out + loads[0] + loads[1] + loads_in)
    w_in, w_out = weights_of(fast, w_held)
    gcat1, gout_half = views_b(ship_b)
    gcat = (gcat0, gcat1)
    for j in range(4):
        gout[rows_of(j), :] = gout_refs[j][...]
    other_half(fast, gout, gout_half)
    finish(loads_out)
    for g in range(2):
        finish(loads[g])
        backward_out(fast, g, gout, w_out, *held, cos_ref, sin_ref, gcat, gbin_ref)
    puts = start(moves([ship_b, gcat0], put_refs, sems, 6))
    finish(loads_in)
    backward_in(gcat, w_in, gouts)
    finish(puts)


def turn_kernel(ship_a, other_a, put_in, put_out, held_a, held_b, left_in, left_out, sems):
    me, core = place_of()
    g, t, r = me // 8, (me // 2) % 4, me % 2
    loads = start(moves([ship_a, other_a], [held_a, held_b], sems))
    for side, ship in enumerate((held_a, held_b)):
        tokens = slice(side * TOK, (side + 1) * TOK)
        finish(loads[side : side + 1])
        for part in range(2):
            far = jnp.bitwise_xor(g, jnp.bitwise_xor(core, part ^ side))
            flat = ship[:, D + part * RO : D + (part + 1) * RO].T
            for s in range(2):
                near = jnp.bitwise_xor(r, s)
                left_out[near, far, 0:64, tokens] = flat[64 * s : 64 * s + 64]
                left_out[near, far, 64:320, tokens] = flat[PAIR + 256 * s : PAIR + 256 * (s + 1)]
        for far in range(2):
            for j in range(4):
                pair = jnp.bitwise_xor(g, far) * 4 + jnp.bitwise_xor(t, j)
                block = ship[:, pl.ds(pl.multiple_of(pair * PAIR, PAIR), PAIR)].T
                start_row = far * 256 + 64 * j
                for s in range(2):
                    left_in[jnp.bitwise_xor(r, s), start_row : start_row + 64, tokens] = block[64 * s : 64 * s + 64]
    finish(start(moves([left_in, left_out], [put_in, put_out], sems, 2)))


def weight_grad_out_kernel(*refs):
    gout_refs, refs = refs[:4], refs[4:]
    *extras, left_ref, other_b, keep, send, left, right, right_other, sems = refs
    loads = start(
        moves([other_b.at[:, CI : CI + 512], left_ref.at[1], left_ref.at[0]], [right_other, left.at[1], left.at[0]], sems)
    )
    cols = pl.ds(pl.multiple_of(512 * lax.axis_index("section"), 512), 512)
    for j in range(4):
        right[rows_of(j), :] = gout_refs[j][:, cols]
    finish(loads[:1])
    for near, out in ((1, send), (0, keep)):
        finish(loads[2 - near : 3 - near])
        for far in range(2):
            part = mm(left[near, far, :, 0:TOK], right[...]) + mm(left[near, far, :, TOK : 2 * TOK], right_other[...])
            out[far, 0:320, :] = part.astype(BF)
            for extra in extras:
                out[far, 320:336, :] = extra[near, far]


def weight_grad_in_kernel(left_ref, gcat, other_b, keep, send, left, right, right_other, sems):
    sources = [gcat, left_ref.at[1], other_b.at[:, 0:CI], left_ref.at[0]]
    loads = start(moves(sources, [right, left.at[1], right_other, left.at[0]], sems))
    finish(loads[:3])
    for near, out in ((1, send), (0, keep)):
        if near == 0:
            finish(loads[3:])
        part = mm(left[near, :, 0:TOK], right[...]) + mm(left[near, :, TOK : 2 * TOK], right_other[...])
        part = part.astype(BF)
        for i in range(8):
            out[i // 4, i % 4] = part[64 * i : 64 * i + 64]


def whole_grad_out_kernel(*refs):
    gout_refs, (ship_a, out, gout) = refs[:4], refs[4:]
    for j in range(4):
        gout[rows_of(j), :] = gout_refs[j][...]
    for g in range(2):
        out[g] = mm_tn(ship_a[:, D + g * RO : D + (g + 1) * RO], gout[...]).astype(BF)


def whole_grad_in_kernel(ship_a, gcat0, ship_b, out):
    for g in range(2):
        right = gcat0[...] if g == 0 else ship_b[:, 0:CI]
        for m in range(4):
            rows = slice(m * 256, (m + 1) * 256)
            out[g, rows, :] = mm_tn(ship_a[:, rows], right).astype(BF)


def norm_backward_kernel(own, r1, r2, r3, x_ref, gout_ref, gain, gx_ref, low_ref, sums_ref):
    x = x_ref[0:ROWS, :].astype(F32)
    gn = own[...] + sum(r[...].astype(F32) for r in (r1, r2, r3))
    gout = gout_ref[...].astype(F32)
    centered = x - jnp.mean(x, -1, keepdims=True)
    inv = lax.rsqrt(jnp.mean(centered * centered, -1, keepdims=True) + EPS)
    unit = centered * inv
    gu = gn * gain[...]
    gx = gout + inv * (gu - jnp.mean(gu, -1, keepdims=True) - unit * jnp.mean(gu * unit, -1, keepdims=True))
    gx_ref[...] = gx
    low_ref[...] = gx.astype(BF)
    sums_ref[0:1, :] = jnp.sum(gn * unit, 0, keepdims=True)
    sums_ref[1:2, :] = jnp.sum(gn, 0, keepdims=True)
    sums_ref[2:3, :] = jnp.sum(gout, 0, keepdims=True)


def pack_kernel(w_qkv, w_out, w_in, w_fc, wi_keep, wi_send, wo_keep, wo_send):
    t, core = (lax.axis_index("dp") // 2) % 4, lax.axis_index("section")
    for ref, g in ((wi_keep, core), (wi_send, 1 - core)):
        for j in range(4):
            rank = jnp.bitwise_xor(t, j)
            for part in range(3):
                start = pl.multiple_of(part * D + g * 512 + rank * PAIR, PAIR)
                ref[j, :, part * PAIR : (part + 1) * PAIR] = w_qkv[:, pl.ds(start, PAIR)].astype(BF)
            start = pl.multiple_of(g * 2048 + rank * FB, FB)
            ref[j, :, 3 * PAIR : CI] = w_in[:, pl.ds(start, FB)].astype(BF)
    for ref, half in ((wo_keep, core), (wo_send, 1 - core)):
        cols = pl.ds(pl.multiple_of(512 * half, 512), 512)
        ref[0:64, :] = w_out[:, cols].astype(BF)
        ref[64:320, :] = w_fc[:, cols].astype(BF)


def unpack_kernel(own0, own1, own2, own3, other, wo_own, wo_other, g_qkv, g_out, g_in, g_fc):
    t, core = (lax.axis_index("dp") // 2) % 4, lax.axis_index("section")
    for side, g in ((0, core), (1, 1 - core)):
        for j in range(4):
            block = (own0, own1, own2, own3)[j][...] if side == 0 else other[j]
            block = block.astype(F32)
            rank = jnp.bitwise_xor(t, j)
            for part in range(3):
                start = pl.multiple_of(part * D + g * 512 + rank * PAIR, PAIR)
                g_qkv[:, pl.ds(start, PAIR)] = block[:, part * PAIR : (part + 1) * PAIR]
            start = pl.multiple_of(g * 2048 + rank * FB, FB)
            g_in[:, pl.ds(start, FB)] = block[:, 3 * PAIR : CI]
    for ref, half in ((wo_own, core), (wo_other, 1 - core)):
        cols = pl.ds(pl.multiple_of(512 * half, 512), 512)
        g_out[:, cols] = ref[0:64, :].astype(F32)
        g_fc[:, cols] = ref[64:320, :].astype(F32)


VM = pl.BlockSpec(memory_space=pltpu.VMEM)


HB = pl.BlockSpec(memory_space=pl.ANY)


def kernel_call(kernel, args, outs, hbm_args=0, hbm_outs=0, scratch=(), cost=2e10, name=None):
    return pl.pallas_call(
        kernel,
        out_shape=outs,
        in_specs=[VM] * (len(args) - hbm_args) + [HB] * hbm_args,
        out_specs=[VM] * (len(outs) - hbm_outs) + [HB] * hbm_outs,
        scratch_shapes=list(scratch),
        compiler_params=pltpu.CompilerParams(vmem_limit_bytes=GRANTS.get(name, SMALL) * 1024 * 1024),
        cost_estimate=pl.CostEstimate(flops=int(cost), bytes_accessed=1, transcendentals=0),
        name=name,
    )(*args)


def dma(count):
    return pltpu.SemaphoreType.DMA((count,))


def arr(shape, dtype):
    return jax.ShapeDtypeStruct(shape, dtype)


def partial_outs():
    return [arr((ROWS, D), F32)] + [arr((ROWS, D), BF)] * 3


def swap_core(value):
    return lax.ppermute(value, "section", [(0, 1), (1, 0)])


def flipped(value, flip):
    count = lax.axis_size("dp")
    return lax.ppermute(value, "dp", [(i, i ^ flip) for i in range(count)])


def after(value, *earlier):
    return lax.optimization_barrier((value, earlier))[0]


def choose(own, other):
    first_core = lax.axis_index("section") == 0
    return jnp.where(first_core, own, other), jnp.where(first_core, other, own)


def across(values):
    spread = lax.axis_size("dp") // 8
    return [flipped(v, (j + 1) * spread) for j, v in enumerate(values)]


def groups_of(spread):
    places = [[[g * 4 * spread + t * spread + r for r in range(spread)] for t in range(4)] for g in range(2)]
    t_groups = [[places[g][t][r] for t in range(4)] for g in range(2) for r in range(spread)]
    f_groups = [[places[g][t][r] for g in range(2) for r in range(spread)] for t in range(4)]
    return t_groups, f_groups


def any_gather(w_qkv, w_out, w_in, w_fc):
    share, spread = w_qkv.shape[0], lax.axis_size("dp") // 8
    t_groups, f_groups = groups_of(spread)
    qkv = w_qkv.reshape(share, 3, 2, 4, PAIR).transpose(3, 0, 2, 1, 4).reshape(4, share, 2, 3 * PAIR)
    wi = jnp.concatenate([qkv, w_in.reshape(share, 2, 4, FB).transpose(2, 0, 1, 3)], axis=-1).astype(BF)
    wi = lax.all_to_all(wi, "dp", 0, 0, axis_index_groups=t_groups, tiled=True)
    wi = lax.all_gather(wi, "dp", axis_index_groups=f_groups)
    wi = wi.reshape(2, spread, 4, share, 2, CI).transpose(4, 0, 2, 1, 3, 5).reshape(2, D, CI)
    wo = lax.all_gather(w_out.astype(BF), "dp", axis_index_groups=f_groups).reshape(2, PAIR, D)
    wf = lax.all_gather(w_fc.astype(BF), "dp", axis_index_groups=f_groups).reshape(2, FB, D)
    wo = jnp.concatenate([wo, wf], axis=1)
    return choose(wi, swap_core(wi)), choose(wo, swap_core(wo))


def any_reduce(gi, go):
    count = lax.axis_size("dp")
    spread, share = count // 8, D // count
    t_groups, f_groups = groups_of(spread)

    def scattered(value):
        return lax.psum_scatter(value, "dp", scatter_dimension=0, axis_index_groups=f_groups)

    gi = gi.reshape(2, 2, 4, spread, share, CI).transpose(1, 3, 2, 4, 0, 5).reshape(2 * spread, 4, share, 2, CI)
    gi = lax.all_to_all(scattered(gi), "dp", 0, 0, axis_index_groups=t_groups, tiled=True)
    g_qkv = gi[..., : 3 * PAIR].reshape(4, share, 2, 3, PAIR).transpose(1, 3, 2, 0, 4).reshape(share, 3 * D)
    g_in = gi[..., 3 * PAIR :].transpose(1, 2, 0, 3).reshape(share, 4 * D)
    g_out = scattered(go[:, :PAIR].reshape(2 * spread, share, D))
    g_fc = scattered(go[:, PAIR:].reshape(2 * spread, 4 * share, D))
    return g_qkv, g_out, g_in, g_fc


def body(boundary, segments, ln_gain, ln_bias, w_qkv, w_out, w_in, b_in, w_fc, b_fc):
    core, me = lax.axis_index("section"), lax.axis_index("dp")
    count = lax.axis_size("dp")
    fast = count == 16
    spread = count // 8
    rank = (me // spread) % 4
    share = D // count
    width_small = 7 * share
    first_core = core == 0

    if fast:
        small = jnp.concatenate([ln_gain, ln_bias, b_fc, b_in], axis=-1).astype(BF)

    if fast:
        wi_keep, wi_send, wo_keep, wo_send = kernel_call(
            pack_kernel,
            [w_qkv[0], w_out[0], w_in[0], w_fc[0]],
            [arr((4, 64, CI), BF), arr((4, 64, CI), BF), arr((320, 512), BF), arr((320, 512), BF)],
            name="pack",
        )
        wi_recv, wo_recv = swap_core(wi_send), swap_core(wo_send)
        wi_first = [choose(wi_keep[j], wi_recv[j]) for j in range(4)]
        wo_first = choose(wo_keep, wo_recv)
        boundary, segments = after((boundary, segments), wi_keep)
    else:
        wi_both, wo_both = any_gather(w_qkv[0], w_out[0], w_in[0], w_fc[0])

    swapped = swap_core(lax.dynamic_index_in_dim(boundary[0], 1 - core, 0, False)[0])
    kept = lax.dynamic_index_in_dim(boundary[0], core, 0, False)[0]
    x0, g1 = choose(kept, swapped)
    if not fast:
        small = jnp.concatenate([ln_gain, ln_bias, b_fc, b_in], axis=-1).astype(BF)
        small = jnp.concatenate(choose(small, swap_core(small)))
    seg = lax.dynamic_index_in_dim(segments, core, 0, False)[0].astype(BF)
    extra = jnp.zeros((16, D), BF).at[0, :ROWS].set(seg)
    if fast:

        def join(wi_pieces, wo_pieces, name):
            pieces, sems = [*wo_pieces, *wi_pieces], [pltpu.SemaphoreType.DMA((40,))]
            if name == "join0":
                own = kernel_call(join_kernel, pieces, [arr(HALF, BF)], 8, 0, sems, 1, name)[0]
                return own
            both = kernel_call(join_kernel, pieces, [arr((2, *HALF), BF)], 8, 0, sems, 1, name)[0]
            return lax.all_to_all(both, "section", 0, 0, tiled=True)

        mine = [after(jnp.stack(w), wo_first) for w in wi_first]
        arrived = across(mine[1:])
        wi_own, wi_own1 = (jnp.stack([w[l] for w in [mine[0], *arrived]]) for l in range(2))
        wo_own, wo_own1 = wo_first
        wo_far, wo_near = flipped(wo_own, 8), flipped(wo_own, 1)
        wi_far, wi_near = flipped(after(wi_own, wo_far), 8), flipped(wi_own, 1)
        wo_near_far = flipped(wo_far, 1)
        small = after(small, wo_near)
        small = jnp.concatenate([small, flipped(small, 1)])
        small = jnp.concatenate([small, flipped(small, 8)])
        small = jnp.stack(choose(small, swap_core(small)), axis=1).reshape(8, width_small)
        extra = extra.at[1:9, :width_small].set(small)
        pack = jnp.concatenate([x0, extra])
        packs = [pack] + across(after([pack] * 3, arrived))
        g1s = [g1] + across(after([g1] * 3, packs))
        wo_far1, wi_far1 = flipped(after(wo_own1, wi_far), 8), flipped(after(wi_own1, wi_far), 8)

        held = jnp.stack([p[129:137, :width_small] for p in packs])
        held = held.reshape(16, 2 * width_small)
        index = jnp.arange(16)
        flip_of = jnp.bitwise_xor(index, me)
        at = (flip_of // 2) % 4 * 4 + (flip_of // 8) * 2 + flip_of % 2
        onehot = (at[:, None] == index[None, :]).astype(BF)
        everyone = mm(onehot, held).reshape(16, 2, width_small)
    else:
        w0, w1 = ([wi_both[l], wo_both[l]] for l in range(2))
        pack = jnp.concatenate([x0, extra])
        packs, g1s = [pack] + across([pack] * 3), [g1] + across([g1] * 3)
        everyone = lax.all_gather(small, "dp").astype(F32)

    def small_of(layer):
        one = everyone[:, layer]
        vectors = [one[:, i * share : (i + 1) * share].reshape(1, D) for i in range(3)]
        b = one[:, 3 * share :].reshape(2, 4, FB)
        return *vectors, lax.dynamic_index_in_dim(b, rank, 1, False)

    gain0, bias0, bfc0, bin0 = small_of(0)
    gain1, bias1, bfc1, bin1 = small_of(1)

    segs = jnp.stack([p[ROWS, :ROWS] for p in packs])
    row = lax.broadcasted_iota(jnp.int32, (ROWS, ROWS), 0)
    col = lax.broadcasted_iota(jnp.int32, (ROWS, ROWS), 1)
    mask = ((segs[:, :, None] == segs[:, None, :]) & (col <= row)).astype(F32)
    positions = jnp.sum(mask, -1).reshape(TOK, 1) - 1.0
    mask = jnp.stack([mask, mask], axis=1).reshape(8 * ROWS, ROWS)
    lane = jnp.arange(PAIR) % 64
    freq = jnp.where(lane < 32, 10000.0 ** (-(lane // 2 * 2).astype(F32) / 32), 0.0)
    angle = positions * freq
    cosine = jnp.cos(angle)
    sine = jnp.sin(angle) * jnp.where(lane % 2 == 0, -1.0, 1.0)

    if fast:
        tables = (gain0, bias0, bin0, cosine, sine, mask, gain1, bias1, bin1, bfc0, bfc1)
        wi_near_far = flipped(after(wi_far, wo_near_far, wi_near, wo_near), 1)
        wi_got = [wi_own, wi_far, wi_near, wi_near_far]
        w0 = join(after(wi_got, tables), [wo_own, wo_far, wo_near, wo_near_far], "join0")
        w0 = [w0, swap_core(after(w0, wo_far1, g1s))]
        wo_near1, wi_near1 = flipped(after(wo_own1, wi_near_far), 1), flipped(after(wi_own1, wi_near_far), 1)

    held_weights = [pltpu.VMEM(HALF, BF)] * 2 if fast else [pltpu.VMEM((2, D, CI), BF), pltpu.VMEM((2, RO, D), BF)]

    saved = [
        arr((TOK, A_COLS), BF),
        arr((2, TOK, 3 * PAIR), BF),
        arr((2, 8 * ROWS, ROWS), F32),
        arr((2, TOK, FB), F32),
    ]
    got = kernel_call(
        functools.partial(first_forward_kernel, fast, len(w0)),
        [*packs, gain0, bias0, bin0, cosine, sine, mask, *w0],
        partial_outs() + saved,
        hbm_args=2,
        hbm_outs=4,
        scratch=[*held_weights, *(pltpu.VMEM(a.shape, a.dtype) for a in saved), dma(4), dma(7)],
        cost=1,
        name="first_forward",
    )
    own, sends, (ship_a0, qkv0, probs0, pre0) = got[0], got[1:4], got[4:]

    def total(own, arrived):
        return sum([r.astype(F32) for r in arrived], own)

    arrived = across(sends)
    sums = total(own, arrived)
    if fast:
        wo_near_far1 = flipped(after(wo_far1, own, wo_near1), 1)
        wi_near_far1 = flipped(after(wi_far1, own, wi_near1), 1)
        w1 = join([wi_own1, wi_far1, wi_near1, wi_near_far1], [wo_own1, wo_far1, wo_near1, wo_near_far1], "join1")
        w1 = [w1]
    x1 = (x0.astype(F32) + sums + bfc0).astype(BF)
    x1s = [x1] + across([x1] * 3)

    back_outs = [arr((TOK, B_COLS), BF), arr((TOK, CI), BF)]
    got = kernel_call(
        functools.partial(second_layer_kernel, fast, len(w1)),
        [*x1s, *g1s, gain1, bias1, bin1, cosine, sine, mask, *w1],
        [*partial_outs(), *partial_outs(), arr((2, FB), F32), arr((TOK, A_COLS), BF), *back_outs],
        scratch=[*(pltpu.VMEM(a.shape, a.dtype) for a in saved[1:]), pltpu.VMEM((TOK, D), BF)],
        name="second_layer",
    )
    out_own, out_sends, gn_own, gn_sends = got[0], got[1:4], got[4], got[5:8]
    gbin1, ship_a1, ship_b1, gcat1 = got[8:]

    def norm_backward(own, arrived, x, gout, gain, name):
        return kernel_call(
            norm_backward_kernel,
            [own, *arrived, x, gout, gain],
            [arr((ROWS, D), F32), arr((ROWS, D), BF), arr((3, D), F32)],
            name=name,
        )

    def turned_ships(ship_a, other_a, name):
        outs = [arr((2, 512, 2 * TOK), BF), arr((2, 2, 320, 2 * TOK), BF)]
        if not fast:
            return ship_a, ship_a
        scratch = [pltpu.VMEM((TOK, A_COLS), BF)] * 2 + [pltpu.VMEM(a.shape, BF) for a in outs] + [dma(4)]
        return kernel_call(turn_kernel, [ship_a, other_a], outs, 2, 2, scratch, name=name)

    def grads_out(gouts, left, other_b, extra, name):
        if fast:
            extras = [] if extra is None else [extra]
            return kernel_call(
                weight_grad_out_kernel,
                [*gouts, *extras, left, other_b],
                [arr((2, 320 + 16 * len(extras), 512), BF)] * 2,
                hbm_args=2,
                scratch=[pltpu.VMEM(left.shape, BF), pltpu.VMEM((TOK, 512), BF), pltpu.VMEM((TOK, 512), BF), dma(3)],
                name=name,
            )
        scratch = [pltpu.VMEM((TOK, D), BF)]
        return kernel_call(whole_grad_out_kernel, [*gouts, left], [arr((2, RO, D), BF)], scratch=scratch, name=name)

    def grads_in(left, ship_b, other_b, gcat, name):
        if fast:
            scratch = [pltpu.VMEM(left.shape, BF), pltpu.VMEM((TOK, CI), BF), pltpu.VMEM((TOK, CI), BF), dma(4)]
            outs = [arr((2, 4, 64, CI), BF)] * 2
            return kernel_call(weight_grad_in_kernel, [left, gcat, other_b], outs, 3, 0, scratch, name=name)
        return kernel_call(whole_grad_in_kernel, [left, gcat, ship_b], [arr((2, D, CI), BF)], name=name)

    def onward(keep, near):
        return flipped((keep[1].astype(F32) + near[1].astype(F32)).astype(BF), 8)

    def reduced(keep, near, far):
        return keep[0].astype(F32) + near[0].astype(F32) + far.astype(F32)

    arrived_gn = across(gn_sends)
    other_a1, other_b1 = (swap_core(ship_a1), swap_core(ship_b1)) if fast else (None, None)
    other_a0 = swap_core(ship_a0) if fast else None
    left_in1, left_out1 = turned_ships(after(ship_a1, other_a0), other_a1, "turn1")
    go1 = grads_out(g1s, left_out1, other_b1, None, "grads1_out")
    _, g0, sums1 = norm_backward(after(gn_own, go1), arrived_gn, x1, g1, gain1, "norm_backward1")
    g0s = [g0] + across([g0] * 3)
    gi1 = grads_in(after(left_in1, g0), ship_b1, other_b1, gcat1, "grads1_in")
    left_in0, left_out0 = turned_ships(after(ship_a0, g0), other_a0, "turn0")
    if fast:
        keep1, send1 = zip(go1, gi1)
        near1 = [flipped(v, 1) for v in send1]
        far1 = [onward(k, v) for k, v in zip(keep1, near1)]
        g0s[0] = after(g0, near1[0], gi1, left_in0)

    got = kernel_call(
        functools.partial(first_backward_kernel, fast, len(w0)),
        [*g0s, cosine, sine, qkv0, probs0, pre0, *w0],
        [*partial_outs(), arr((2, FB), F32), *back_outs],
        hbm_args=5,
        hbm_outs=2,
        scratch=[
            *held_weights,
            *(pltpu.VMEM(a.shape, a.dtype) for a in saved[1:]),
            *(pltpu.VMEM((TOK, cols), BF) for cols in (B_COLS, CI, D)),
            dma(4),
            dma(8),
        ],
        name="first_backward",
    )
    gn_own, gn_sends, (gbin0, ship_b0, gcat0) = got[0], got[1:4], got[4:]
    arrived_gn = across(gn_sends)
    if fast:
        other_b0 = swap_core(after(ship_b0, near1[1], far1[0]))
    else:
        other_b0 = None
    gi0 = grads_in(left_in0, ship_b0, other_b0, gcat0, "grads0_in")
    gx0, _, sums0 = norm_backward(after(gn_own, gi0), arrived_gn, x0, g0, gain0, "norm_backward0")

    def small_grads(sums, gbin):
        onehot = (jnp.arange(4) == rank).astype(F32)
        vectors = sums.reshape(3, 2, 4, spread, share).transpose(1, 2, 3, 0, 4).reshape(2, 4, spread, 3 * share)
        b = gbin.reshape(2, 1, spread, 4 * share)
        return (vectors, b) if fast else jnp.concatenate([vectors, b * onehot[None, :, None, None]], axis=-1)

    both = jax.tree.map(choose, small_grads(sums0, gbin0), small_grads(sums1, gbin1))
    if fast:
        mine, theirs = (jnp.concatenate([v[i].reshape(-1) for v in both]) for i in range(2))
        mine = mine + swap_core(theirs)
        vectors, b = mine[: 3 * D].reshape(2, 4, 2, 192), mine[3 * D :].reshape(2, 1, 2, 256)
        values = jnp.concatenate([vectors.transpose(2, 0, 1, 3).reshape(2, 2, 768), b[:, 0].transpose(1, 0, 2)], axis=-1)
        values = jnp.where(me // 8 == 0, values, values[:, ::-1])
        values = jnp.where(me % 2 == 0, values, values[::-1])
        extra = jnp.zeros((2, 2, 16, 512), BF).at[:, :, :2].set(values.reshape(2, 2, 2, 512).astype(BF))
        wo_1, wi_1 = (reduced(*v).astype(BF) for v in zip(keep1, near1, far1))
        near_in0 = flipped(gi0[1], 1)
        far_in0 = onward(gi0[0], near_in0)
        extra = after(extra, wi_1, near_in0)
    else:
        extra = None
    go0 = grads_out(g0s, left_out0, other_b0, extra, "grads0_out")

    out1 = x1.astype(F32) + total(out_own, across(after(out_sends, near_in0) if fast else out_sends)) + bfc1
    arrived = swap_core(jnp.where(first_core, out1, gx0))
    boundary_out = jnp.where(first_core, jnp.stack([gx0, arrived]), jnp.stack([arrived, out1]))[None, :, None]
    if fast:
        near_out0 = flipped(go0[1], 1)
        far_out0 = onward(go0[0], near_out0)
        wo_0 = reduced(go0[0], near_out0, far_out0)
        shares = [reduced(gi0[0], near_in0, far_in0), wi_1]
        vector = wo_0[320:322].reshape(1024)
        ranks = vector[:768].reshape(4, 192)
        ranks = [lax.dynamic_index_in_dim(ranks, jnp.bitwise_xor(rank, j), 0, True) for j in range(4)]
        summed = sum([r.astype(F32) for r in across([r.astype(BF) for r in ranks[1:]])], ranks[0])
        vector = jnp.concatenate([summed, vector[None, 768:]], axis=1)
        wo_0 = wo_0[:320].astype(BF)
        shares = [jnp.concatenate([shares[0][j].astype(BF), shares[1][j]]) for j in range(4)]
        arrived = [shares[0]] + across(after(shares[1:], out1, near_out0))
        wo_mine, wo_theirs = choose(wo_0, wo_1)
        pairs = [choose(w[:64], w[64:]) for w in arrived]
        wi_other = swap_core(jnp.stack([p[1] for p in pairs]))
        g_qkv, g_out, g_in, g_fc = kernel_call(
            unpack_kernel,
            [*[p[0] for p in pairs], wi_other, wo_mine, swap_core(wo_theirs)],
            [arr((64, 3 * D), F32), arr((64, D), F32), arr((64, 4 * D), F32), arr((256, D), F32)],
            name="unpack",
        )
    else:
        vector = (both[0] + swap_core(both[1])).reshape(count, 7 * share)
        vector = lax.psum_scatter(vector, "dp", scatter_dimension=0, tiled=True)
        mine, theirs = choose(gi0[0], gi1[0])
        gi = mine.astype(F32) + swap_core(theirs).astype(F32)
        mine, theirs = choose(go0[0], go1[0])
        go = mine.astype(F32) + swap_core(theirs).astype(F32)
        g_qkv, g_out, g_in, g_fc = any_reduce(gi, go)
    g_gain, g_bias, g_bfc = (vector[:, i * share : (i + 1) * share] for i in range(3))
    g_bin = vector[:, 3 * share :]

    return (boundary_out, g_gain, g_bias, g_qkv[None], g_out[None], g_in[None], g_bin, g_fc[None], g_bfc)


def solution(mesh):
    rows = P("section", None, "dp", None, None)
    vector, matrix = P("section", "dp"), P("section", "dp", None)
    return jax.shard_map(
        body,
        mesh=mesh,
        in_specs=(rows, P(None, "dp", None), vector, vector, matrix, matrix, matrix, vector, matrix, vector),
        out_specs=(rows, vector, vector, matrix, matrix, matrix, vector, matrix, vector),
        check_vma=False,
    )
```

```python
import functools

import jax
import jax.numpy as jnp
from jax import lax
from jax.experimental import pallas as pl
from jax.experimental.pallas import tpu as pltpu
from jax.sharding import PartitionSpec as P

D = 1024
PAIR = 128
FB = 512
CI = 3 * PAIR + FB
RO = PAIR + FB
EPS = 1e-05
NEG = -1000000000.0
SCALE = 0.125
ROWS = 128
TOK = 4 * ROWS
BF = jnp.bfloat16
F32 = jnp.float32
SMALL, LARGE = 24, 56
GRANTS = {"turn0": LARGE, "grads0_in": LARGE, "join0": LARGE, "first_forward": LARGE, "first_backward": LARGE, "grads0_out": LARGE, "pack": LARGE, "norm_backward0": LARGE}


def mm(a, b):
    return lax.dot_general(a, b, (((1,), (0,)), ((), ())), preferred_element_type=F32)


def mm_nt(a, b):
    return lax.dot_general(a, b, (((1,), (1,)), ((), ())), preferred_element_type=F32)


def mm_tn(a, b):
    return lax.dot_general(a, b, (((0,), (0,)), ((), ())), preferred_element_type=F32)


def gelu(h):
    return 0.5 * h * (1.0 + jnp.tanh(0.7978845608 * (h + 0.044715 * h * h * h)))


def gelu_slope(h):
    th = jnp.tanh(0.7978845608 * (h + 0.044715 * h * h * h))
    inner = 0.7978845608 * (1.0 + 3 * 0.044715 * h * h)
    return 0.5 * (1.0 + th) + 0.5 * h * (1.0 - th * th) * inner


def partner(x):
    lane = lax.broadcasted_iota(jnp.int32, x.shape, 1)
    return jnp.where(lane % 2 == 0, pltpu.roll(x, PAIR - 1, 1), pltpu.roll(x, 1, 1))


def turned(x, cosine, sine):
    return x * cosine + partner(x) * sine


def by_head(x):
    lane = lax.broadcasted_iota(jnp.int32, (1, PAIR), 1)
    low = jnp.where(lane < 64, 1.0, 0.0).astype(x.dtype)
    high = jnp.where(lane < 64, 0.0, 1.0).astype(x.dtype)
    return jnp.concatenate([x * low, x * high], axis=0)


def beside(x):
    return jnp.concatenate([x[:ROWS], x[ROWS:]], axis=1)


def heads_of(x):
    return [x[ROWS * j : ROWS * (j + 1)] for j in range(4)]


def rows_of(j):
    return pl.ds(j * ROWS, ROWS)


def layer_norm_into(x_refs, gain_ref, bias_ref, normed):
    for j, x_ref in enumerate(x_refs):
        x = x_ref[0:ROWS, :].astype(F32)
        centered = x - jnp.mean(x, -1, keepdims=True)
        inv = lax.rsqrt(jnp.mean(centered * centered, -1, keepdims=True) + EPS)
        normed[rows_of(j), :] = (centered * inv * gain_ref[...] + bias_ref[...]).astype(BF)


def row_of(fast, g):
    return pl.ds(jnp.bitwise_xor(g, lax.axis_index("section")), 1) if fast else slice(g, g + 1)


def forward_in(fast, g, normed, w, bin_ref, cos_ref, sin_ref, mask_ref, qkv, probs, oa, pre):
    w_qkv, w_in = w[g]
    y = mm(normed[...], w_qkv[...])
    cosine, sine = cos_ref[...], sin_ref[...]
    qkv[g, :, 0:PAIR] = turned(y[:, 0:PAIR], cosine, sine).astype(BF)
    qkv[g, :, PAIR : 2 * PAIR] = turned(y[:, PAIR : 2 * PAIR], cosine, sine).astype(BF)
    qkv[g, :, 2 * PAIR : 3 * PAIR] = y[:, 2 * PAIR : 3 * PAIR].astype(BF)
    q, k, v = (heads_of(qkv[g, :, i * PAIR : (i + 1) * PAIR]) for i in range(3))
    for j in range(4):
        rows = pl.ds(2 * ROWS * j, 2 * ROWS)
        s = mm_nt(by_head(q[j]), k[j]) * SCALE
        s = jnp.where(mask_ref[rows, :] > 0.5, s, NEG)
        e = jnp.exp(s - jnp.max(s, -1, keepdims=True))
        p = e * (1.0 / jnp.sum(e, -1, keepdims=True))
        probs[g, rows, :] = p
        oa[g][rows_of(j), 0:PAIR] = mm(beside(p.astype(BF)), by_head(v[j])).astype(BF)
    h = mm(normed[...], w_in[...]) + bin_ref[row_of(fast, g), :]
    pre[g] = h
    oa[g][:, PAIR:RO] = gelu(h).astype(BF)


def forward_out(oa, w_out, outs):
    for (start, w0), (_, w1) in zip(*w_out):
        for n in range(2):
            part = mm(oa[0][...], w0[:, n * 256 : (n + 1) * 256]) + mm(oa[1][...], w1[:, n * 256 : (n + 1) * 256])
            cols = pl.ds(pl.multiple_of(start + n * 256, 256), 256)
            for j in range(4):
                outs[j][0:ROWS, cols] = part[j * ROWS : (j + 1) * ROWS].astype(outs[j].dtype)


def backward_out(fast, g, gout, w_out, qkv, probs, pre, cos_ref, sin_ref, gcat, gbin_ref):
    halves = [(gout[:, pl.ds(start, 512)], w) for start, w in w_out[g]]
    go = sum(mm_nt(rows, w[0:PAIR, :]) for rows, w in halves).astype(BF)
    q, k, v = (heads_of(qkv[g, :, i * PAIR : (i + 1) * PAIR]) for i in range(3))
    cosine, sine = cos_ref[...], sin_ref[...]
    go = [by_head(rows) for rows in heads_of(go)]
    p = probs[g]
    gp = jnp.concatenate([mm_nt(go[j], v[j]) for j in range(4)], axis=0)
    gs = (p * (gp - jnp.sum(gp * p, -1, keepdims=True))).astype(BF)
    gs = [gs[2 * ROWS * j : 2 * ROWS * (j + 1)] for j in range(4)]
    p = p.astype(BF)
    gq = jnp.concatenate([mm(beside(gs[j]), by_head(k[j])) for j in range(4)], axis=0) * SCALE
    gk = jnp.concatenate([mm_tn(gs[j], by_head(q[j])) for j in range(4)], axis=0) * SCALE
    gv = jnp.concatenate([mm_tn(p[2 * ROWS * j : 2 * ROWS * (j + 1)], go[j]) for j in range(4)], axis=0)
    gcat[g][:, 0:PAIR] = turned(gq, cosine, -sine).astype(BF)
    gcat[g][:, PAIR : 2 * PAIR] = turned(gk, cosine, -sine).astype(BF)
    gcat[g][:, 2 * PAIR : 3 * PAIR] = gv.astype(BF)
    ga = sum(mm_nt(rows, w[PAIR:RO, :]) for rows, w in halves)
    gpre = (ga * gelu_slope(pre[g])).astype(BF)
    gcat[g][:, 3 * PAIR : CI] = gpre
    gbin_ref[row_of(fast, g), :] = jnp.sum(gpre.astype(F32), 0, keepdims=True)


def backward_in(gcat, w, outs):
    for n in range(4):
        cols = slice(n * 256, (n + 1) * 256)
        part = sum(
            mm_nt(gcat[g][:, 0 : 3 * PAIR], w[g][0][cols, :]) + mm_nt(gcat[g][:, 3 * PAIR : CI], w[g][1][cols, :])
            for g in range(2)
        )
        for j in range(4):
            outs[j][0:ROWS, cols] = part[j * ROWS : (j + 1) * ROWS].astype(outs[j].dtype)


A_COLS = D + 2 * RO
B_COLS = CI + 512


def views_a(ship_a):
    return ship_a.at[:, 0:D], (ship_a.at[:, D : D + RO], ship_a.at[:, D + RO : D + 2 * RO])


def views_b(ship_b):
    return ship_b.at[:, 0:CI], ship_b.at[:, CI : CI + 512]


HALF = (2 * D + 2 * RO, 512)


def weights_of(fast, refs):
    if not fast:
        wi, wo = refs
        ins = [(wi.at[g, :, 0 : 3 * PAIR], wi.at[g, :, 3 * PAIR : CI]) for g in range(2)]
        return ins, [[(0, wo.at[g, :, 0:512]), (512, wo.at[g, :, 512:1024])] for g in range(2)]
    core, halves = lax.axis_index("section"), refs
    starts = [pl.multiple_of(512 * c, 512) for c in (core, 1 - core)]
    rows = [pl.ds(pl.multiple_of(2 * D + RO * c, 128), RO) for c in (core, 1 - core)]
    ins = [(half.at[D : 2 * D, 0 : 3 * PAIR], half.at[0:D, :]) for half in halves]
    return ins, [[(start, half.at[rows[g], :]) for start, half in zip(starts, halves)] for g in range(2)]


def weight_loads(fast, refs, held, sems):
    if fast:
        core = lax.axis_index("section")
        halves = refs if len(refs) == 2 else [refs[0].at[core], refs[0].at[1 - core]]
        ins = [pltpu.make_async_copy(h.at[0 : 2 * D], v.at[0 : 2 * D], sems.at[i]) for i, (h, v) in enumerate(zip(halves, held))]
        end = 2 * D + 2 * RO
        outs = [
            pltpu.make_async_copy(h.at[2 * D : end], v.at[2 * D : end], sems.at[2 + i])
            for i, (h, v) in enumerate(zip(halves, held))
        ]
        return ins, outs
    ins = [pltpu.make_async_copy(refs[0].at[g], held[0].at[g], sems.at[g]) for g in range(2)]
    return ins, [pltpu.make_async_copy(refs[1], held[1], sems.at[2])]


def start(copies):
    for copy in copies:
        copy.start()
    return copies


def finish(copies):
    for copy in copies:
        copy.wait()


def moves(sources, targets, sems, first=0):
    return [pltpu.make_async_copy(a, b, sems.at[first + i]) for i, (a, b) in enumerate(zip(sources, targets))]


def place_of():
    return lax.axis_index("dp"), lax.axis_index("section")


def other_half(fast, gout, half_ref):
    core = lax.axis_index("section") if fast else 0
    half_ref[...] = gout[:, pl.ds(pl.multiple_of(512 * (1 - core), 512), 512)]


def join_kernel(own, far, near_own, near_far, *refs):
    pieces, joined, sems = refs[:-2], refs[-2], refs[-1]
    target = joined if len(joined.shape) == 2 else joined.at[0]
    me, _ = place_of()
    copies = []

    def copy(source, rows, cols=slice(None)):
        copies.append(pltpu.make_async_copy(source, target.at[rows, cols], sems.at[len(copies)]))
        copies[-1].start()

    for flip, piece in ((0, own), (8, far), (1, near_own), (9, near_far)):
        source = jnp.bitwise_xor(me, flip)
        g, r = source // 8, source % 2
        base = 2 * D + g * RO
        copy(piece.at[0:64], pl.ds(pl.multiple_of(base + 64 * r, 64), 64))
        copy(piece.at[64:320], pl.ds(pl.multiple_of(base + PAIR + 256 * r, 128), 256))
    blocks = [(ref, i) for ref in pieces for i in range(ref.shape[0])]
    for (ref, i), flip in zip(blocks, [f ^ (2 * j) for f in (0, 8, 1, 9) for j in range(4)]):
        start = pl.multiple_of(jnp.bitwise_xor(me, flip) * 64, 64)
        copy(ref.at[i, :, 3 * PAIR : CI], pl.ds(start, 64))
        copy(ref.at[i, :, 0 : 3 * PAIR], pl.ds(D + start, 64), slice(0, 3 * PAIR))
    for one in copies:
        one.wait()
    if len(joined.shape) == 3:
        joined[1] = joined[0]


def first_forward_kernel(fast, n_w, *refs):
    x_refs, (gain, bias, bin_ref, cos_ref, sin_ref, mask_ref), refs = refs[:4], refs[4:10], refs[10:]
    w_refs, outs, saved, refs = refs[:n_w], refs[n_w : n_w + 4], refs[n_w + 4 : n_w + 8], refs[n_w + 8 :]
    w_held, held, (w_sems, sems) = refs[:2], refs[2:6], refs[6:]
    loads_in, loads_out = weight_loads(fast, w_refs, w_held, w_sems)
    start(loads_in + loads_out)
    w_in, w_out = weights_of(fast, w_held)
    ship_a, qkv, probs, pre = held
    normed, oa = views_a(ship_a)
    layer_norm_into(x_refs, gain, bias, normed)
    puts = []
    for g in range(2):
        finish(loads_in[g : g + 1])
        forward_in(fast, g, normed, w_in, bin_ref, cos_ref, sin_ref, mask_ref, qkv, probs, oa, pre)
        puts += start(moves([h.at[g] for h in held[1:]], [h.at[g] for h in saved[1:]], sems, 1 + 3 * g))
    puts += start(moves(held[:1], saved[:1], sems))
    finish(loads_out)
    forward_out(oa, w_out, outs)
    finish(puts)


def second_layer_kernel(fast, n_w, *refs):
    x_refs, gout_refs, refs = refs[:4], refs[4:8], refs[8:]
    (gain, bias, bin_ref, cos_ref, sin_ref, mask_ref), refs = refs[:6], refs[6:]
    w_refs, refs = refs[:n_w], refs[n_w:]
    if fast:
        core = lax.axis_index("section")
        w_refs = [w_refs[0].at[core], w_refs[0].at[1 - core]]
    w_in, w_out = weights_of(fast, w_refs)
    outs, gouts, gbin_ref, refs = refs[:4], refs[4:8], refs[8], refs[9:]
    ship_a, ship_b, gcat0, qkv, probs, pre, gout = refs
    normed, oa = views_a(ship_a)
    gcat1, gout_half = views_b(ship_b)
    gcat = (gcat0, gcat1)
    layer_norm_into(x_refs, gain, bias, normed)
    for j in range(4):
        gout[rows_of(j), :] = gout_refs[j][...]
    other_half(fast, gout, gout_half)
    for g in range(2):
        forward_in(fast, g, normed, w_in, bin_ref, cos_ref, sin_ref, mask_ref, qkv, probs, oa, pre)
    for g in range(2):
        backward_out(fast, g, gout, w_out, qkv, probs, pre, cos_ref, sin_ref, gcat, gbin_ref)
    backward_in(gcat, w_in, gouts)
    forward_out(oa, w_out, outs)


def first_backward_kernel(fast, n_w, *refs):
    gout_refs, (cos_ref, sin_ref), saved, refs = refs[:4], refs[4:6], refs[6:9], refs[9:]
    w_refs, refs = refs[:n_w], refs[n_w:]
    gouts, gbin_ref, put_refs, refs = refs[:4], refs[4], refs[5:7], refs[7:]
    w_held, held, (ship_b, gcat0, gout, w_sems, sems) = refs[:2], refs[2:5], refs[5:]
    loads_in, loads_out = weight_loads(fast, w_refs, w_held, w_sems)
    loads = [moves([h.at[g] for h in saved], [h.at[g] for h in held], sems, 3 * g) for g in range(2)]
    start(loads_out + loads[0] + loads[1] + loads_in)
    w_in, w_out = weights_of(fast, w_held)
    gcat1, gout_half = views_b(ship_b)
    gcat = (gcat0, gcat1)
    for j in range(4):
        gout[rows_of(j), :] = gout_refs[j][...]
    other_half(fast, gout, gout_half)
    finish(loads_out)
    for g in range(2):
        finish(loads[g])
        backward_out(fast, g, gout, w_out, *held, cos_ref, sin_ref, gcat, gbin_ref)
    puts = start(moves([ship_b, gcat0], put_refs, sems, 6))
    finish(loads_in)
    backward_in(gcat, w_in, gouts)
    finish(puts)


def turn_kernel(ship_a, other_a, put_in, put_out, held_a, held_b, left_in, left_out, sems):
    me, core = place_of()
    g, t, r = me // 8, (me // 2) % 4, me % 2
    loads = start(moves([ship_a, other_a], [held_a, held_b], sems))
    for side, ship in enumerate((held_a, held_b)):
        tokens = slice(side * TOK, (side + 1) * TOK)
        finish(loads[side : side + 1])
        for part in range(2):
            far = jnp.bitwise_xor(g, jnp.bitwise_xor(core, part ^ side))
            flat = ship[:, D + part * RO : D + (part + 1) * RO].T
            for s in range(2):
                near = jnp.bitwise_xor(r, s)
                left_out[near, far, 0:64, tokens] = flat[64 * s : 64 * s + 64]
                left_out[near, far, 64:320, tokens] = flat[PAIR + 256 * s : PAIR + 256 * (s + 1)]
        for far in range(2):
            for j in range(4):
                pair = jnp.bitwise_xor(g, far) * 4 + jnp.bitwise_xor(t, j)
                block = ship[:, pl.ds(pl.multiple_of(pair * PAIR, PAIR), PAIR)].T
                start_row = far * 256 + 64 * j
                for s in range(2):
                    left_in[jnp.bitwise_xor(r, s), start_row : start_row + 64, tokens] = block[64 * s : 64 * s + 64]
    finish(start(moves([left_in, left_out], [put_in, put_out], sems, 2)))


def weight_grad_out_kernel(*refs):
    gout_refs, refs = refs[:4], refs[4:]
    *extras, left_ref, other_b, keep, send, left, right, right_other, sems = refs
    loads = start(
        moves([other_b.at[:, CI : CI + 512], left_ref.at[1], left_ref.at[0]], [right_other, left.at[1], left.at[0]], sems)
    )
    cols = pl.ds(pl.multiple_of(512 * lax.axis_index("section"), 512), 512)
    for j in range(4):
        right[rows_of(j), :] = gout_refs[j][:, cols]
    finish(loads[:1])
    for near, out in ((1, send), (0, keep)):
        finish(loads[2 - near : 3 - near])
        for far in range(2):
            part = mm(left[near, far, :, 0:TOK], right[...]) + mm(left[near, far, :, TOK : 2 * TOK], right_other[...])
            out[far, 0:320, :] = part.astype(BF)
            for extra in extras:
                out[far, 320:336, :] = extra[near, far]


def weight_grad_in_kernel(left_ref, gcat, other_b, keep, send, left, right, right_other, sems):
    sources = [gcat, left_ref.at[1], other_b.at[:, 0:CI], left_ref.at[0]]
    loads = start(moves(sources, [right, left.at[1], right_other, left.at[0]], sems))
    finish(loads[:3])
    for near, out in ((1, send), (0, keep)):
        if near == 0:
            finish(loads[3:])
        part = mm(left[near, :, 0:TOK], right[...]) + mm(left[near, :, TOK : 2 * TOK], right_other[...])
        part = part.astype(BF)
        for i in range(8):
            out[i // 4, i % 4] = part[64 * i : 64 * i + 64]


def whole_grad_out_kernel(*refs):
    gout_refs, (ship_a, out, gout) = refs[:4], refs[4:]
    for j in range(4):
        gout[rows_of(j), :] = gout_refs[j][...]
    for g in range(2):
        out[g] = mm_tn(ship_a[:, D + g * RO : D + (g + 1) * RO], gout[...]).astype(BF)


def whole_grad_in_kernel(ship_a, gcat0, ship_b, out):
    for g in range(2):
        right = gcat0[...] if g == 0 else ship_b[:, 0:CI]
        for m in range(4):
            rows = slice(m * 256, (m + 1) * 256)
            out[g, rows, :] = mm_tn(ship_a[:, rows], right).astype(BF)


def norm_backward_kernel(own, r1, r2, r3, x_ref, gout_ref, gain, gx_ref, low_ref, sums_ref):
    x = x_ref[0:ROWS, :].astype(F32)
    gn = own[...] + sum(r[...].astype(F32) for r in (r1, r2, r3))
    gout = gout_ref[...].astype(F32)
    centered = x - jnp.mean(x, -1, keepdims=True)
    inv = lax.rsqrt(jnp.mean(centered * centered, -1, keepdims=True) + EPS)
    unit = centered * inv
    gu = gn * gain[...]
    gx = gout + inv * (gu - jnp.mean(gu, -1, keepdims=True) - unit * jnp.mean(gu * unit, -1, keepdims=True))
    gx_ref[...] = gx
    low_ref[...] = gx.astype(BF)
    sums_ref[0:1, :] = jnp.sum(gn * unit, 0, keepdims=True)
    sums_ref[1:2, :] = jnp.sum(gn, 0, keepdims=True)
    sums_ref[2:3, :] = jnp.sum(gout, 0, keepdims=True)


def pack_kernel(w_qkv, w_out, w_in, w_fc, wi_keep, wi_send, wo_keep, wo_send):
    t, core = (lax.axis_index("dp") // 2) % 4, lax.axis_index("section")
    for ref, g in ((wi_keep, core), (wi_send, 1 - core)):
        for j in range(4):
            rank = jnp.bitwise_xor(t, j)
            for part in range(3):
                start = pl.multiple_of(part * D + g * 512 + rank * PAIR, PAIR)
                ref[j, :, part * PAIR : (part + 1) * PAIR] = w_qkv[:, pl.ds(start, PAIR)].astype(BF)
            start = pl.multiple_of(g * 2048 + rank * FB, FB)
            ref[j, :, 3 * PAIR : CI] = w_in[:, pl.ds(start, FB)].astype(BF)
    for ref, half in ((wo_keep, core), (wo_send, 1 - core)):
        cols = pl.ds(pl.multiple_of(512 * half, 512), 512)
        ref[0:64, :] = w_out[:, cols].astype(BF)
        ref[64:320, :] = w_fc[:, cols].astype(BF)


def unpack_kernel(own0, own1, own2, own3, other, wo_own, wo_other, g_qkv, g_out, g_in, g_fc):
    t, core = (lax.axis_index("dp") // 2) % 4, lax.axis_index("section")
    for side, g in ((0, core), (1, 1 - core)):
        for j in range(4):
            block = (own0, own1, own2, own3)[j][...] if side == 0 else other[j]
            block = block.astype(F32)
            rank = jnp.bitwise_xor(t, j)
            for part in range(3):
                start = pl.multiple_of(part * D + g * 512 + rank * PAIR, PAIR)
                g_qkv[:, pl.ds(start, PAIR)] = block[:, part * PAIR : (part + 1) * PAIR]
            start = pl.multiple_of(g * 2048 + rank * FB, FB)
            g_in[:, pl.ds(start, FB)] = block[:, 3 * PAIR : CI]
    for ref, half in ((wo_own, core), (wo_other, 1 - core)):
        cols = pl.ds(pl.multiple_of(512 * half, 512), 512)
        g_out[:, cols] = ref[0:64, :].astype(F32)
        g_fc[:, cols] = ref[64:320, :].astype(F32)


VM = pl.BlockSpec(memory_space=pltpu.VMEM)


HB = pl.BlockSpec(memory_space=pl.ANY)


def kernel_call(kernel, args, outs, hbm_args=0, hbm_outs=0, scratch=(), cost=2e10, name=None):
    return pl.pallas_call(
        kernel,
        out_shape=outs,
        in_specs=[VM] * (len(args) - hbm_args) + [HB] * hbm_args,
        out_specs=[VM] * (len(outs) - hbm_outs) + [HB] * hbm_outs,
        scratch_shapes=list(scratch),
        compiler_params=pltpu.CompilerParams(vmem_limit_bytes=GRANTS.get(name, SMALL) * 1024 * 1024),
        cost_estimate=pl.CostEstimate(flops=int(cost), bytes_accessed=1, transcendentals=0),
        name=name,
    )(*args)


def dma(count):
    return pltpu.SemaphoreType.DMA((count,))


def arr(shape, dtype):
    return jax.ShapeDtypeStruct(shape, dtype)


def partial_outs():
    return [arr((ROWS, D), F32)] + [arr((ROWS, D), BF)] * 3


def swap_core(value):
    return lax.ppermute(value, "section", [(0, 1), (1, 0)])


def flipped(value, flip):
    count = lax.axis_size("dp")
    return lax.ppermute(value, "dp", [(i, i ^ flip) for i in range(count)])


def after(value, *earlier):
    return lax.optimization_barrier((value, earlier))[0]


def choose(own, other):
    first_core = lax.axis_index("section") == 0
    return jnp.where(first_core, own, other), jnp.where(first_core, other, own)


def across(values):
    spread = lax.axis_size("dp") // 8
    return [flipped(v, (j + 1) * spread) for j, v in enumerate(values)]


def groups_of(spread):
    places = [[[g * 4 * spread + t * spread + r for r in range(spread)] for t in range(4)] for g in range(2)]
    t_groups = [[places[g][t][r] for t in range(4)] for g in range(2) for r in range(spread)]
    f_groups = [[places[g][t][r] for g in range(2) for r in range(spread)] for t in range(4)]
    return t_groups, f_groups


def any_gather(w_qkv, w_out, w_in, w_fc):
    share, spread = w_qkv.shape[0], lax.axis_size("dp") // 8
    t_groups, f_groups = groups_of(spread)
    qkv = w_qkv.reshape(share, 3, 2, 4, PAIR).transpose(3, 0, 2, 1, 4).reshape(4, share, 2, 3 * PAIR)
    wi = jnp.concatenate([qkv, w_in.reshape(share, 2, 4, FB).transpose(2, 0, 1, 3)], axis=-1).astype(BF)
    wi = lax.all_to_all(wi, "dp", 0, 0, axis_index_groups=t_groups, tiled=True)
    wi = lax.all_gather(wi, "dp", axis_index_groups=f_groups)
    wi = wi.reshape(2, spread, 4, share, 2, CI).transpose(4, 0, 2, 1, 3, 5).reshape(2, D, CI)
    wo = lax.all_gather(w_out.astype(BF), "dp", axis_index_groups=f_groups).reshape(2, PAIR, D)
    wf = lax.all_gather(w_fc.astype(BF), "dp", axis_index_groups=f_groups).reshape(2, FB, D)
    wo = jnp.concatenate([wo, wf], axis=1)
    return choose(wi, swap_core(wi)), choose(wo, swap_core(wo))


def any_reduce(gi, go):
    count = lax.axis_size("dp")
    spread, share = count // 8, D // count
    t_groups, f_groups = groups_of(spread)

    def scattered(value):
        return lax.psum_scatter(value, "dp", scatter_dimension=0, axis_index_groups=f_groups)

    gi = gi.reshape(2, 2, 4, spread, share, CI).transpose(1, 3, 2, 4, 0, 5).reshape(2 * spread, 4, share, 2, CI)
    gi = lax.all_to_all(scattered(gi), "dp", 0, 0, axis_index_groups=t_groups, tiled=True)
    g_qkv = gi[..., : 3 * PAIR].reshape(4, share, 2, 3, PAIR).transpose(1, 3, 2, 0, 4).reshape(share, 3 * D)
    g_in = gi[..., 3 * PAIR :].transpose(1, 2, 0, 3).reshape(share, 4 * D)
    g_out = scattered(go[:, :PAIR].reshape(2 * spread, share, D))
    g_fc = scattered(go[:, PAIR:].reshape(2 * spread, 4 * share, D))
    return g_qkv, g_out, g_in, g_fc


def body(boundary, segments, ln_gain, ln_bias, w_qkv, w_out, w_in, b_in, w_fc, b_fc):
    core, me = lax.axis_index("section"), lax.axis_index("dp")
    count = lax.axis_size("dp")
    fast = count == 16
    spread = count // 8
    rank = (me // spread) % 4
    share = D // count
    width_small = 7 * share
    first_core = core == 0

    if fast:
        small = jnp.concatenate([ln_gain, ln_bias, b_fc, b_in], axis=-1).astype(BF)

    if fast:
        wi_keep, wi_send, wo_keep, wo_send = kernel_call(
            pack_kernel,
            [w_qkv[0], w_out[0], w_in[0], w_fc[0]],
            [arr((4, 64, CI), BF), arr((4, 64, CI), BF), arr((320, 512), BF), arr((320, 512), BF)],
            name="pack",
        )
        wi_recv, wo_recv = swap_core(wi_send), swap_core(wo_send)
        wi_first = [choose(wi_keep[j], wi_recv[j]) for j in range(4)]
        wo_first = choose(wo_keep, wo_recv)
        boundary, segments = after((boundary, segments), wi_keep)
    else:
        wi_both, wo_both = any_gather(w_qkv[0], w_out[0], w_in[0], w_fc[0])

    swapped = swap_core(lax.dynamic_index_in_dim(boundary[0], 1 - core, 0, False)[0])
    kept = lax.dynamic_index_in_dim(boundary[0], core, 0, False)[0]
    x0, g1 = choose(kept, swapped)
    if not fast:
        small = jnp.concatenate([ln_gain, ln_bias, b_fc, b_in], axis=-1).astype(BF)
        small = jnp.concatenate(choose(small, swap_core(small)))
    seg = lax.dynamic_index_in_dim(segments, core, 0, False)[0].astype(BF)
    extra = jnp.zeros((16, D), BF).at[0, :ROWS].set(seg)
    if fast:

        def join(wi_pieces, wo_pieces, name):
            pieces, sems = [*wo_pieces, *wi_pieces], [pltpu.SemaphoreType.DMA((40,))]
            if name == "join0":
                own = kernel_call(join_kernel, pieces, [arr(HALF, BF)], 8, 0, sems, 1, name)[0]
                return own
            both = kernel_call(join_kernel, pieces, [arr((2, *HALF), BF)], 8, 0, sems, 1, name)[0]
            return lax.all_to_all(both, "section", 0, 0, tiled=True)

        mine = [after(jnp.stack(w), wo_first) for w in wi_first]
        arrived = across(mine[1:])
        wi_own, wi_own1 = (jnp.stack([w[l] for w in [mine[0], *arrived]]) for l in range(2))
        wo_own, wo_own1 = wo_first
        wo_far, wo_near = flipped(wo_own, 8), flipped(wo_own, 1)
        wi_far, wi_near = flipped(after(wi_own, wo_far), 8), flipped(wi_own, 1)
        wo_near_far = flipped(wo_far, 1)
        small = after(small, wo_near)
        small = jnp.concatenate([small, flipped(small, 1)])
        small = jnp.concatenate([small, flipped(small, 8)])
        small = jnp.stack(choose(small, swap_core(small)), axis=1).reshape(8, width_small)
        extra = extra.at[1:9, :width_small].set(small)
        pack = jnp.concatenate([x0, extra])
        packs = [pack] + across(after([pack] * 3, arrived))
        g1s = [g1] + across(after([g1] * 3, packs))
        wo_far1, wi_far1 = flipped(after(wo_own1, wi_far), 8), flipped(after(wi_own1, wi_far), 8)

        held = jnp.stack([p[129:137, :width_small] for p in packs])
        held = held.reshape(16, 2 * width_small)
        index = jnp.arange(16)
        flip_of = jnp.bitwise_xor(index, me)
        at = (flip_of // 2) % 4 * 4 + (flip_of // 8) * 2 + flip_of % 2
        onehot = (at[:, None] == index[None, :]).astype(BF)
        everyone = mm(onehot, held).reshape(16, 2, width_small)
    else:
        w0, w1 = ([wi_both[l], wo_both[l]] for l in range(2))
        pack = jnp.concatenate([x0, extra])
        packs, g1s = [pack] + across([pack] * 3), [g1] + across([g1] * 3)
        everyone = lax.all_gather(small, "dp").astype(F32)

    def small_of(layer):
        one = everyone[:, layer]
        vectors = [one[:, i * share : (i + 1) * share].reshape(1, D) for i in range(3)]
        b = one[:, 3 * share :].reshape(2, 4, FB)
        return *vectors, lax.dynamic_index_in_dim(b, rank, 1, False)

    gain0, bias0, bfc0, bin0 = small_of(0)
    gain1, bias1, bfc1, bin1 = small_of(1)

    segs = jnp.stack([p[ROWS, :ROWS] for p in packs])
    row = lax.broadcasted_iota(jnp.int32, (ROWS, ROWS), 0)
    col = lax.broadcasted_iota(jnp.int32, (ROWS, ROWS), 1)
    mask = ((segs[:, :, None] == segs[:, None, :]) & (col <= row)).astype(F32)
    positions = jnp.sum(mask, -1).reshape(TOK, 1) - 1.0
    mask = jnp.stack([mask, mask], axis=1).reshape(8 * ROWS, ROWS)
    lane = jnp.arange(PAIR) % 64
    freq = jnp.where(lane < 32, 10000.0 ** (-(lane // 2 * 2).astype(F32) / 32), 0.0)
    angle = positions * freq
    cosine = jnp.cos(angle)
    sine = jnp.sin(angle) * jnp.where(lane % 2 == 0, -1.0, 1.0)

    if fast:
        tables = (gain0, bias0, bin0, cosine, sine, mask, gain1, bias1, bin1, bfc0, bfc1)
        wi_near_far = flipped(after(wi_far, wo_near_far, wi_near, wo_near), 1)
        wi_got = [wi_own, wi_far, wi_near, wi_near_far]
        w0 = join(after(wi_got, tables), [wo_own, wo_far, wo_near, wo_near_far], "join0")
        w0 = [w0, swap_core(after(w0, wo_far1, g1s))]
        wo_near1, wi_near1 = flipped(after(wo_own1, wi_near_far), 1), flipped(after(wi_own1, wi_near_far), 1)

    held_weights = [pltpu.VMEM(HALF, BF)] * 2 if fast else [pltpu.VMEM((2, D, CI), BF), pltpu.VMEM((2, RO, D), BF)]

    saved = [
        arr((TOK, A_COLS), BF),
        arr((2, TOK, 3 * PAIR), BF),
        arr((2, 8 * ROWS, ROWS), F32),
        arr((2, TOK, FB), F32),
    ]
    got = kernel_call(
        functools.partial(first_forward_kernel, fast, len(w0)),
        [*packs, gain0, bias0, bin0, cosine, sine, mask, *w0],
        partial_outs() + saved,
        hbm_args=2,
        hbm_outs=4,
        scratch=[*held_weights, *(pltpu.VMEM(a.shape, a.dtype) for a in saved), dma(4), dma(7)],
        cost=1,
        name="first_forward",
    )
    own, sends, (ship_a0, qkv0, probs0, pre0) = got[0], got[1:4], got[4:]

    def total(own, arrived):
        return sum([r.astype(F32) for r in arrived], own)

    arrived = across(sends)
    sums = total(own, arrived)
    if fast:
        wo_near_far1 = flipped(after(wo_far1, own, wo_near1), 1)
        wi_near_far1 = flipped(after(wi_far1, own, wi_near1), 1)
        w1 = join([wi_own1, wi_far1, wi_near1, wi_near_far1], [wo_own1, wo_far1, wo_near1, wo_near_far1], "join1")
        w1 = [w1]
    x1 = (x0.astype(F32) + sums + bfc0).astype(BF)
    x1s = [x1] + across([x1] * 3)

    back_outs = [arr((TOK, B_COLS), BF), arr((TOK, CI), BF)]
    got = kernel_call(
        functools.partial(second_layer_kernel, fast, len(w1)),
        [*x1s, *g1s, gain1, bias1, bin1, cosine, sine, mask, *w1],
        [*partial_outs(), *partial_outs(), arr((2, FB), F32), arr((TOK, A_COLS), BF), *back_outs],
        scratch=[*(pltpu.VMEM(a.shape, a.dtype) for a in saved[1:]), pltpu.VMEM((TOK, D), BF)],
        name="second_layer",
    )
    out_own, out_sends, gn_own, gn_sends = got[0], got[1:4], got[4], got[5:8]
    gbin1, ship_a1, ship_b1, gcat1 = got[8:]

    def norm_backward(own, arrived, x, gout, gain, name):
        return kernel_call(
            norm_backward_kernel,
            [own, *arrived, x, gout, gain],
            [arr((ROWS, D), F32), arr((ROWS, D), BF), arr((3, D), F32)],
            name=name,
        )

    def turned_ships(ship_a, other_a, name):
        outs = [arr((2, 512, 2 * TOK), BF), arr((2, 2, 320, 2 * TOK), BF)]
        if not fast:
            return ship_a, ship_a
        scratch = [pltpu.VMEM((TOK, A_COLS), BF)] * 2 + [pltpu.VMEM(a.shape, BF) for a in outs] + [dma(4)]
        return kernel_call(turn_kernel, [ship_a, other_a], outs, 2, 2, scratch, name=name)

    def grads_out(gouts, left, other_b, extra, name):
        if fast:
            extras = [] if extra is None else [extra]
            return kernel_call(
                weight_grad_out_kernel,
                [*gouts, *extras, left, other_b],
                [arr((2, 320 + 16 * len(extras), 512), BF)] * 2,
                hbm_args=2,
                scratch=[pltpu.VMEM(left.shape, BF), pltpu.VMEM((TOK, 512), BF), pltpu.VMEM((TOK, 512), BF), dma(3)],
                name=name,
            )
        scratch = [pltpu.VMEM((TOK, D), BF)]
        return kernel_call(whole_grad_out_kernel, [*gouts, left], [arr((2, RO, D), BF)], scratch=scratch, name=name)

    def grads_in(left, ship_b, other_b, gcat, name):
        if fast:
            scratch = [pltpu.VMEM(left.shape, BF), pltpu.VMEM((TOK, CI), BF), pltpu.VMEM((TOK, CI), BF), dma(4)]
            outs = [arr((2, 4, 64, CI), BF)] * 2
            return kernel_call(weight_grad_in_kernel, [left, gcat, other_b], outs, 3, 0, scratch, name=name)
        return kernel_call(whole_grad_in_kernel, [left, gcat, ship_b], [arr((2, D, CI), BF)], name=name)

    def onward(keep, near):
        return flipped((keep[1].astype(F32) + near[1].astype(F32)).astype(BF), 8)

    def reduced(keep, near, far):
        return keep[0].astype(F32) + near[0].astype(F32) + far.astype(F32)

    arrived_gn = across(gn_sends)
    other_a1, other_b1 = (swap_core(ship_a1), swap_core(ship_b1)) if fast else (None, None)
    other_a0 = swap_core(ship_a0) if fast else None
    left_in1, left_out1 = turned_ships(after(ship_a1, other_a0), other_a1, "turn1")
    go1 = grads_out(g1s, left_out1, other_b1, None, "grads1_out")
    _, g0, sums1 = norm_backward(after(gn_own, go1), arrived_gn, x1, g1, gain1, "norm_backward1")
    g0s = [g0] + across([g0] * 3)
    gi1 = grads_in(after(left_in1, g0), ship_b1, other_b1, gcat1, "grads1_in")
    left_in0, left_out0 = turned_ships(after(ship_a0, g0), other_a0, "turn0")
    if fast:
        keep1, send1 = zip(go1, gi1)
        near1 = [flipped(v, 1) for v in send1]
        far1 = [onward(k, v) for k, v in zip(keep1, near1)]
        g0s[0] = after(g0, near1[0], gi1, left_in0)

    got = kernel_call(
        functools.partial(first_backward_kernel, fast, len(w0)),
        [*g0s, cosine, sine, qkv0, probs0, pre0, *w0],
        [*partial_outs(), arr((2, FB), F32), *back_outs],
        hbm_args=5,
        hbm_outs=2,
        scratch=[
            *held_weights,
            *(pltpu.VMEM(a.shape, a.dtype) for a in saved[1:]),
            *(pltpu.VMEM((TOK, cols), BF) for cols in (B_COLS, CI, D)),
            dma(4),
            dma(8),
        ],
        name="first_backward",
    )
    gn_own, gn_sends, (gbin0, ship_b0, gcat0) = got[0], got[1:4], got[4:]
    arrived_gn = across(gn_sends)
    if fast:
        other_b0 = swap_core(after(ship_b0, near1[1], far1[0]))
    else:
        other_b0 = None
    gi0 = grads_in(left_in0, ship_b0, other_b0, gcat0, "grads0_in")
    gx0, _, sums0 = norm_backward(after(gn_own, gi0), arrived_gn, x0, g0, gain0, "norm_backward0")

    def small_grads(sums, gbin):
        onehot = (jnp.arange(4) == rank).astype(F32)
        vectors = sums.reshape(3, 2, 4, spread, share).transpose(1, 2, 3, 0, 4).reshape(2, 4, spread, 3 * share)
        b = gbin.reshape(2, 1, spread, 4 * share)
        return (vectors, b) if fast else jnp.concatenate([vectors, b * onehot[None, :, None, None]], axis=-1)

    both = jax.tree.map(choose, small_grads(sums0, gbin0), small_grads(sums1, gbin1))
    if fast:
        mine, theirs = (jnp.concatenate([v[i].reshape(-1) for v in both]) for i in range(2))
        mine = mine + swap_core(theirs)
        vectors, b = mine[: 3 * D].reshape(2, 4, 2, 192), mine[3 * D :].reshape(2, 1, 2, 256)
        values = jnp.concatenate([vectors.transpose(2, 0, 1, 3).reshape(2, 2, 768), b[:, 0].transpose(1, 0, 2)], axis=-1)
        values = jnp.where(me // 8 == 0, values, values[:, ::-1])
        values = jnp.where(me % 2 == 0, values, values[::-1])
        extra = jnp.zeros((2, 2, 16, 512), BF).at[:, :, :2].set(values.reshape(2, 2, 2, 512).astype(BF))
        wo_1, wi_1 = (reduced(*v).astype(BF) for v in zip(keep1, near1, far1))
        near_in0 = flipped(gi0[1], 1)
        far_in0 = onward(gi0[0], near_in0)
        extra = after(extra, wi_1, near_in0)
    else:
        extra = None
    go0 = grads_out(g0s, left_out0, other_b0, extra, "grads0_out")

    out1 = x1.astype(F32) + total(out_own, across(after(out_sends, near_in0) if fast else out_sends)) + bfc1
    arrived = swap_core(jnp.where(first_core, out1, gx0))
    boundary_out = jnp.where(first_core, jnp.stack([gx0, arrived]), jnp.stack([arrived, out1]))[None, :, None]
    if fast:
        near_out0 = flipped(go0[1], 1)
        far_out0 = onward(go0[0], near_out0)
        wo_0 = reduced(go0[0], near_out0, far_out0)
        shares = [reduced(gi0[0], near_in0, far_in0), wi_1]
        vector = wo_0[320:322].reshape(1024)
        ranks = vector[:768].reshape(4, 192)
        ranks = [lax.dynamic_index_in_dim(ranks, jnp.bitwise_xor(rank, j), 0, True) for j in range(4)]
        summed = sum([r.astype(F32) for r in across([r.astype(BF) for r in ranks[1:]])], ranks[0])
        vector = jnp.concatenate([summed, vector[None, 768:]], axis=1)
        wo_0 = wo_0[:320].astype(BF)
        shares = [jnp.concatenate([shares[0][j].astype(BF), shares[1][j]]) for j in range(4)]
        arrived = [shares[0]] + across(after(shares[1:], out1, near_out0))
        wo_mine, wo_theirs = choose(wo_0, wo_1)
        pairs = [choose(w[:64], w[64:]) for w in arrived]
        wi_other = swap_core(jnp.stack([p[1] for p in pairs]))
        g_qkv, g_out, g_in, g_fc = kernel_call(
            unpack_kernel,
            [*[p[0] for p in pairs], wi_other, wo_mine, swap_core(wo_theirs)],
            [arr((64, 3 * D), F32), arr((64, D), F32), arr((64, 4 * D), F32), arr((256, D), F32)],
            name="unpack",
        )
    else:
        vector = (both[0] + swap_core(both[1])).reshape(count, 7 * share)
        vector = lax.psum_scatter(vector, "dp", scatter_dimension=0, tiled=True)
        mine, theirs = choose(gi0[0], gi1[0])
        gi = mine.astype(F32) + swap_core(theirs).astype(F32)
        mine, theirs = choose(go0[0], go1[0])
        go = mine.astype(F32) + swap_core(theirs).astype(F32)
        g_qkv, g_out, g_in, g_fc = any_reduce(gi, go)
    g_gain, g_bias, g_bfc = (vector[:, i * share : (i + 1) * share] for i in range(3))
    g_bin = vector[:, 3 * share :]

    return (boundary_out, g_gain, g_bias, g_qkv[None], g_out[None], g_in[None], g_bin, g_fc[None], g_bfc)


def solution(mesh):
    rows = P("section", None, "dp", None, None)
    vector, matrix = P("section", "dp"), P("section", "dp", None)
    return jax.shard_map(
        body,
        mesh=mesh,
        in_specs=(rows, P(None, "dp", None), vector, vector, matrix, matrix, matrix, vector, matrix, vector),
        out_specs=(rows, vector, vector, matrix, matrix, matrix, vector, matrix, vector),
        check_vma=False,
    )
```
